32 devices in a mesh: head: 4 (over z), sq: 8 (over y, x, core).
Axes of the slice: x: 2, y: 2, z: 4, core: 2. Of those that a mesh axis runs over, the one named last changes fastest.
Arguments:
- layer_in: bfloat16 [8192, 2048], P(('sq', 'head')), may hold values from -6 to 6
- norm1_gain: bfloat16 [2048], P('sq'), may hold values from 0.5 to 1.5
- norm1_bias: bfloat16 [2048], P('sq'), may hold values from -1.1953125 to 1.1953125
- w_query: bfloat16 [2048, 2048], P('sq', 'head'), may hold values from -0.125 to 0.125
- w_key: bfloat16 [2048, 2048], P('sq', 'head'), may hold values from -0.125 to 0.125
- w_value: bfloat16 [2048, 4096], P('sq', 'head'), may hold values from -0.125 to 0.125
- w_swish: bfloat16 [2048, 4096], P('sq', 'head'), may hold values from -0.125 to 0.125
- w_out: bfloat16 [4096, 2048], P('head', 'sq'), may hold values from -0.1875 to 0.1875
- norm2_gain: bfloat16 [2048], P('sq'), may hold values from 0.5 to 1.5
- norm2_bias: bfloat16 [2048], P('sq'), may hold values from -1.1953125 to 1.1953125
- w_gate: bfloat16 [2048, 4096], P('sq', 'head'), may hold values from -0.125 to 0.125
- w_up: bfloat16 [2048, 4096], P('sq', 'head'), may hold values from -0.125 to 0.125
- w_down: bfloat16 [4096, 2048], P('head', 'sq'), may hold values from -0.1875 to 0.1875
- cotangent: bfloat16 [8192, 2048], P(('sq', 'head')), may hold values from -6 to 6
Outputs:
- result: bfloat16 [8192, 2048], P(('sq', 'head'))
- grad_in: float32 [8192, 2048], P(('sq', 'head'))
- grad_norm1_gain: float32 [2048], P(('head', 'sq'))
- grad_norm1_bias: float32 [2048], P(('head', 'sq'))
- grad_query: float32 [2048, 2048], P('sq', 'head')
- grad_key: float32 [2048, 2048], P('sq', 'head')
- grad_value: float32 [2048, 4096], P('sq', 'head')
- grad_swish: float32 [2048, 4096], P('sq', 'head')
- grad_out: float32 [4096, 2048], P('head', 'sq')
- grad_norm2_gain: float32 [2048], P('sq')
- grad_norm2_bias: float32 [2048], P('sq')
- grad_gate: float32 [2048, 4096], P('sq', 'head')
- grad_up: float32 [2048, 4096], P('sq', 'head')
- grad_down: float32 [4096, 2048], P('head', 'sq')
The draws below stay inside these ranges and needn't reach their ends.
All inputs are finite; a program needn't handle non-finite values.
Results may differ from the reference program's by a relative error of at most 0.025.
Values may be sent and summed in bfloat16 or wider, within the bound.
No kernel may reach another device: no remote copies, remote signals or barrier semaphores. Data moves between devices by JAX's collectives and lax.ppermute only.
A program may use at most 320 MiB of HBM per device.

```python
import jax
import jax.numpy as jnp
from jax import lax

D = 2048
HEADS = 8
KD = 256
VD = 512
FF = 4096
SPAN = 1024
VALD = 4096
SEQ = 8192


def raised(drawn, rng, source, target, blocks, factor):
    owner, partner = [(jnp.arange(drawn.shape[axis_at]) // (drawn.shape[axis_at] // blocks)).reshape([-1 if axis == axis_at else 1 for axis in range(drawn.ndim)]) for axis_at in (source, target)]
    chosen = jax.random.permutation(rng, blocks)[partner]
    strong = (owner == chosen) | (owner == (partner + blocks // 2) % blocks)
    return jnp.where(strong, factor * drawn, drawn)


def level_of(key, shape, shards, low, high):
    factor_of = 1.0
    for dim, parts in shards:
        steps = jax.random.uniform(jax.random.fold_in(jax.random.fold_in(key, 6), dim), (parts,), jnp.float32, low / len(shards), high / len(shards))
        factor_of = factor_of * jnp.repeat(jnp.exp(steps), shape[dim] // parts).reshape((-1,) + (1,) * (len(shape) - 1 - dim))
    return factor_of


def gaussian(key, dims, scale, limit, cuts=(), held_as=jnp.bfloat16):
    factor_of = level_of(key, dims, cuts, -0.22, 0.18) if cuts else 1.0
    result = jax.random.normal(key, dims, jnp.float32) * scale * factor_of
    return jnp.minimum(jnp.maximum(result, -limit), limit).astype(held_as)


def bell_draw_with(stream_key, shape, width, reach, cuts, heavy, dtype=jnp.bfloat16):
    array = width * jax.random.normal(stream_key, shape, jnp.float32)
    if cuts:
        array = array * level_of(stream_key, shape, cuts, -0.22, 0.18)
    return jnp.clip(raised(array, jax.random.fold_in(stream_key, 3), *heavy), -reach, reach).astype(dtype)


def setup_inputs(seed: int = 0) -> dict:
    key_of = jax.random.split(jax.random.key(seed), 15)
    layer_in = bell_draw_with(key_of[0], (SEQ, D), 1.0, 6.0, ((0, 32),), (0, 1, 32, 2.75))
    norm1_gain = jnp.clip(1.0 + 0.1 * jax.random.normal(key_of[1], (D,), jnp.float32), 0.5, 1.5).astype(jnp.bfloat16)
    norm1_bias = gaussian(key_of[2], (D,), 0.3, 1.1953125, ((0, 8),))
    w_query = gaussian(key_of[3], (D, D), D ** -0.5, 0.125, ((0, 8), (1, 4)))
    w_key = gaussian(key_of[4], (D, D), D ** -0.5, 0.125, ((0, 8), (1, 4)))
    w_value = gaussian(key_of[5], (D, VALD), D ** -0.5, 0.125, ((0, 8), (1, 4)))
    w_swish = gaussian(key_of[6], (D, VALD), D ** -0.5, 0.125, ((0, 8), (1, 4)))
    w_out = gaussian(key_of[7], (VALD, D), (VALD // 4) ** -0.5, 0.1875, ((0, 4), (1, 8)))
    norm2_gain = jnp.clip(1.0 + 0.1 * jax.random.normal(key_of[8], (D,), jnp.float32), 0.5, 1.5).astype(jnp.bfloat16)
    norm2_bias = gaussian(key_of[9], (D,), 0.3, 1.1953125, ((0, 8),))
    w_gate = gaussian(key_of[10], (D, FF), D ** -0.5, 0.125, ((0, 8), (1, 4)))
    w_up = gaussian(key_of[11], (D, FF), D ** -0.5, 0.125, ((0, 8), (1, 4)))
    w_down = gaussian(key_of[12], (FF, D), (FF // 4) ** -0.5, 0.1875, ((0, 4), (1, 8)))
    cotangent = gaussian(key_of[13], (SEQ, D), 1.0, 6.0, ((0, 32),))
    return {"layer_in": layer_in, "norm1_gain": norm1_gain, "norm1_bias": norm1_bias, "w_query": w_query, "w_key": w_key, "w_value": w_value, "w_swish": w_swish, "w_out": w_out, "norm2_gain": norm2_gain, "norm2_bias": norm2_bias, "w_gate": w_gate, "w_up": w_up, "w_down": w_down, "cotangent": cotangent}


eps_layer = 1e-05
eps_group = 1e-06
highest = lax.Precision.HIGHEST

@jax.custom_vjp
def low(v):
    return lax.optimization_barrier(v.astype(jnp.bfloat16)).astype(jnp.float32)

@jax.custom_vjp
def low_back(v):
    return v

def low_keep(v):
    return (low(v), None)

def low_pass(kept, grad):
    return (grad,)

def back_keep(v):
    return (v, None)

def back_low(kept, grad):
    return (low(grad),)
low.defvjp(low_keep, low_pass)
low_back.defvjp(back_keep, back_low)

def matmul(left_side, right_side):
    return jnp.dot(left_side, right_side, precision=highest, preferred_element_type=jnp.float32)

def layer_norm(values, weight_gain, weight_shift):
    centered = values - lax.optimization_barrier(jnp.mean(values, axis=-1, keepdims=True))
    spread = lax.rsqrt(lax.optimization_barrier(jnp.mean(centered * centered, axis=-1, keepdims=True)) + eps_layer)
    return centered * spread * weight_gain + weight_shift

def group_norm(values):
    return values * lax.rsqrt(lax.optimization_barrier(jnp.mean(values * values, axis=-1, keepdims=True)) + eps_group)

def log_decay(first_head, head_count):
    head_ids = (first_head + jnp.arange(head_count)).astype(jnp.float32)
    return jnp.log(1.0 - jnp.exp2(-5.0 - head_ids))

def retention(queries, key_rows, value_rows):
    log_rate = log_decay(0, HEADS)
    position = jnp.arange(SPAN).astype(jnp.float32)
    spacing = position[:, None] - position[None, :]
    causal = spacing >= 0
    decay_mat = jnp.where(causal[None], jnp.exp(log_rate[:, None, None] * jnp.where(causal, spacing, 0.0)[None]), 0.0)
    query_decay = jnp.exp(log_rate[None, :] * (position[:, None] + 1.0))
    key_decay = jnp.exp(log_rate[None, :] * (SPAN - 1.0 - position[:, None]))
    span_decay = jnp.exp(log_rate * SPAN)

    def advance(carry_state, pieces):
        query_blk, key_blk, value_blk = pieces
        scores = low_back(jnp.einsum('ihd,jhd->hij', query_blk, key_blk, precision=highest))
        mixing = low(scores * decay_mat)
        inner_sum = jnp.einsum('hij,jhe->ihe', mixing, value_blk, precision=highest)
        carried = query_decay[:, :, None] * jnp.einsum('ihd,hde->ihe', query_blk, carry_state, precision=highest)
        update = jnp.einsum('jhd,jhe->hde', key_blk * key_decay[:, :, None], value_blk, precision=highest)
        return (span_decay[:, None, None] * carry_state + update, inner_sum + carried)
    blocks = SEQ // SPAN
    start_state = jnp.zeros((HEADS, KD, VD), jnp.float32)
    pieces = (queries.reshape(blocks, SPAN, HEADS, KD), key_rows.reshape(blocks, SPAN, HEADS, KD), value_rows.reshape(blocks, SPAN, HEADS, VD))
    _, outputs = lax.scan(jax.checkpoint(advance), start_state, pieces)
    return outputs.reshape(SEQ, HEADS, VD)

def forward(inputs, gain_one, shift_one, weight_query, weight_key, weight_value, weight_swish, weight_out, gain_two, shift_two, weight_gate, weight_up, weight_down):
    normed = low(layer_norm(inputs, gain_one, shift_one))
    queries = low_back(low(matmul(normed, weight_query)))
    key_rows = low_back(low(matmul(normed, weight_key) * KD ** (-0.5)))
    value_rows = low_back(low(matmul(normed, weight_value)))
    swish_pre = low_back(matmul(normed, weight_swish))
    retained = retention(queries.reshape(SEQ, HEADS, KD), key_rows.reshape(SEQ, HEADS, KD), value_rows.reshape(SEQ, HEADS, VD))
    retained = low_back(retained)
    grouped = low_back(low(group_norm(retained))).reshape(SEQ, HEADS * VD)
    gated = low(grouped * jax.nn.silu(swish_pre))
    branch = low_back(matmul(gated, weight_out))
    hidden = inputs + branch
    second = low(layer_norm(hidden, gain_two, shift_two))
    gate_pre = low_back(matmul(second, weight_gate))
    up_pre = low_back(matmul(second, weight_up))
    inner_act = low(jax.nn.gelu(gate_pre) * up_pre)
    return hidden + matmul(inner_act, weight_down)

def reference(layer_in, norm1_gain, norm1_bias, w_query, w_key, w_value, w_swish, w_out, norm2_gain, norm2_bias, w_gate, w_up, w_down, cotangent):
    primals = tuple((item.astype(jnp.float32) for item in (layer_in, norm1_gain, norm1_bias, w_query, w_key, w_value, w_swish, w_out, norm2_gain, norm2_bias, w_gate, w_up, w_down)))
    output, backward = jax.vjp(forward, *primals)
    gradient = backward(cotangent.astype(jnp.float32))
    return (output.astype(jnp.bfloat16), gradient[0], gradient[1], gradient[2], gradient[3], gradient[4], gradient[5], gradient[6], gradient[7], gradient[8], gradient[9], gradient[10], gradient[11], gradient[12])
```

```python
import jax
import jax.numpy as jnp
from jax import lax
from jax.sharding import PartitionSpec as P

KD = 256
VD = 512
CHUNK = 256


eps_layer = 1e-05
eps_group = 1e-06
low = jnp.bfloat16
wide = jnp.float32


def mask_of(slot, count):
    bits = count.bit_length() - 1
    return ((slot << 1) & (count - 1)) | (slot >> (bits - 1))


def slot_of(mask, count):
    bits = count.bit_length() - 1
    return (mask >> 1) | ((mask & 1) << (bits - 1))


def flip(value, mask):
    count = lax.axis_size("sq")
    return lax.ppermute(value, "sq", [(i, i ^ mask) for i in range(count)])


def route(swapped):
    count = lax.axis_size("sq")
    lower = list(range(count.bit_length() - 2))
    return lower[::-1] if swapped else lower


def own_order(values):
    count = lax.axis_size("sq")
    width = values.shape[-1] // count
    place = lax.axis_index("sq")
    return jnp.concatenate(
        [
            lax.dynamic_slice_in_dim(values, (place ^ mask_of(s, count)) * width, width, -1)
            for s in range(count)
        ],
        axis=-1,
    )


def true_order(values):
    count = lax.axis_size("sq")
    width = values.shape[-1] // count
    place = lax.axis_index("sq")
    return jnp.concatenate(
        [
            lax.dynamic_slice_in_dim(values, slot_of(place ^ b, count) * width, width, -1)
            for b in range(count)
        ],
        axis=-1,
    )


def gather_sq(shard, axis, swapped):
    count = lax.axis_size("sq")
    pieces = {0: shard}
    for bit in route(swapped):
        got = {s | 1 << bit: flip(p, mask_of(1 << bit, count)) for s, p in pieces.items()}
        pieces.update(got)
    near = jnp.concatenate([pieces[s] for s in range(count // 2)], axis=axis)
    far = flip(near, mask_of(count // 2, count))
    return jnp.concatenate([near, far], axis=axis)


def scatter_sq(product, axis, swapped):
    count = lax.axis_size("sq")
    got = flip(product(1).astype(low), mask_of(count // 2, count))
    total = (product(0) + got.astype(wide)).astype(low)
    width = total.shape[axis] // (count // 2)
    pieces = {
        s: lax.slice_in_dim(total, s * width, (s + 1) * width, axis=axis) for s in range(count // 2)
    }
    bits = route(swapped)[::-1]
    for step, bit in enumerate(bits):
        keep = [s for s in pieces if not s >> bit & 1]
        sent = jnp.concatenate([pieces[s | 1 << bit] for s in keep], axis=axis)
        got = flip(sent, mask_of(1 << bit, count)).astype(wide)
        parts = {}
        for k, s in enumerate(keep):
            part = pieces[s].astype(wide) + lax.slice_in_dim(
                got, k * width, (k + 1) * width, axis=axis
            )
            parts[s] = part if step == len(bits) - 1 else part.astype(low)
        pieces = parts
    return pieces[0]


def ring_step(value):
    count = lax.axis_size("head")
    return lax.ppermute(value, "head", [(i, (i + 1) % count) for i in range(count)])


def gather_head(rows):
    count = lax.axis_size("head")
    place = lax.axis_index("head")
    size = rows.shape[0]
    whole = jnp.zeros((count * size,) + rows.shape[1:], rows.dtype)
    held = rows
    for turn in range(count):
        whole = lax.dynamic_update_slice_in_dim(
            whole, held, lax.rem(place - turn + count, count) * size, 0
        )
        if turn < count - 1:
            held = ring_step(held)
    return whole


def scatter_head(product, size):
    count = lax.axis_size("head")
    place = lax.axis_index("head")
    total = product(lax.rem(place - 1 + count, count) * size)
    for turn in range(2, count + 1):
        got = ring_step(total.astype(low)).astype(wide)
        total = product(lax.rem(place - turn + count, count) * size) + got
    return total


def sum_all(values):
    for axis in ("sq", "head"):
        count = lax.axis_size(axis)
        step = 1
        while step < count:
            values = values + lax.ppermute(values, axis, [(i, i ^ step) for i in range(count)])
            step *= 2
    return values


def layer_norm(values, weight_gain, weight_shift):
    centered = values - jnp.mean(values, axis=-1, keepdims=True)
    spread = lax.rsqrt(jnp.mean(centered * centered, axis=-1, keepdims=True) + eps_layer)
    return centered * spread * weight_gain + weight_shift


def group_norm(values):
    return values * lax.rsqrt(jnp.mean(values * values, axis=-1, keepdims=True) + eps_group)


def swish_gate(normed, pre_gate):
    return normed * jax.nn.silu(pre_gate)


def gelu_gate(pre_gate, pre_up):
    return jax.nn.gelu(pre_gate) * pre_up


def log_decay(first_head, head_count):
    head_ids = (first_head + jnp.arange(head_count)).astype(jnp.float32)
    return jnp.log(1.0 - jnp.exp2(-5.0 - head_ids))


def project(left_side, right_side):
    return jnp.dot(left_side, right_side, preferred_element_type=jnp.float32)


def outer_sum(left_side, right_side):
    return lax.dot_general(
        left_side, right_side, (((0,), (0,)), ((), ())), preferred_element_type=jnp.float32
    )


def back_project(gradient, weight):
    return lax.dot_general(
        gradient, weight, (((1,), (1,)), ((), ())), preferred_element_type=jnp.float32
    )


def carried_from(state, log_rate, length, backward):
    count = lax.axis_size("sq")
    place = lax.axis_index("sq")
    sent = state.astype(low)
    slots = gather_sq(sent[None], 0, False)
    total = jnp.zeros_like(state)
    for slot in range(1, count):
        other = place ^ mask_of(slot, count)
        ahead = (other - place) if backward else (place - other)
        between = jnp.maximum(ahead - 1, 0).astype(wide) * length
        factor = jnp.where(ahead > 0, jnp.exp(log_rate * between), 0.0)
        total = total + factor[:, None, None] * slots[slot].astype(wide)
    return total


def heads_of(values, size):
    return values.reshape(values.shape[0], -1, size).transpose(1, 0, 2)


def rows_of(values):
    return values.transpose(1, 0, 2).reshape(values.shape[1], -1)


def retain_forward(queries, key_rows, value_rows, incoming, log_rate):
    heads, length, _ = queries.shape
    position = jnp.arange(length).astype(wide)
    spacing = position[:, None] - position[None, :]
    decay = jnp.where(
        spacing >= 0, jnp.exp(log_rate[:, None, None] * jnp.maximum(spacing, 0.0)[None]), 0.0
    )
    reach = jnp.exp(log_rate[:, None] * (position + 1.0))
    scores = jnp.einsum("hid,hjd->hij", queries, key_rows, preferred_element_type=wide)
    mixing = (scores * decay).astype(low)
    inner = jnp.einsum("hij,hje->hie", mixing, value_rows, preferred_element_type=wide)
    carried = jnp.einsum(
        "hid,hde->hie", queries, incoming.astype(low), preferred_element_type=wide
    )
    return inner + reach[:, :, None] * carried, mixing, decay


def shards(
    layer_in,
    norm1_gain,
    norm1_bias,
    w_query,
    w_key,
    w_value,
    w_swish,
    w_out,
    norm2_gain,
    norm2_bias,
    w_gate,
    w_up,
    w_down,
    cotangent,
):
    count_sq = lax.axis_size("sq")
    count_head = lax.axis_size("head")
    sq_index = lax.axis_index("sq")
    head_index = lax.axis_index("head")
    own_rows = layer_in.shape[0]
    length = own_rows * count_head
    key_scale = KD ** (-0.5)
    query_width = w_query.shape[1]
    value_width = w_value.shape[1]
    local_heads = query_width // KD

    x_own = own_order(layer_in)
    cot_own = own_order(cotangent)
    x_low = gather_head(x_own)
    norms = gather_sq(jnp.stack([norm1_gain, norm1_bias, norm2_gain, norm2_bias]), 1, False).astype(
        wide
    )
    gain_one, shift_one, gain_two, shift_two = norms[0], norms[1], norms[2], norms[3]
    w_kv = gather_sq(jnp.concatenate([w_key, w_value], axis=1), 0, False)
    w_qs = gather_sq(jnp.concatenate([w_query, w_swish], axis=1), 0, True)
    out_rows = gather_sq(w_out, 1, False)
    down_rows = gather_sq(w_down, 1, True)
    gate_cols = gather_sq(w_gate, 0, False)
    up_cols = gather_sq(w_up, 0, True)

    normed = layer_norm(x_low.astype(wide), gain_one, shift_one).astype(low)
    kv = project(normed, w_kv)
    key_low = heads_of((kv[:, :query_width] * key_scale).astype(low), KD)
    value_low = heads_of(kv[:, query_width:].astype(low), VD)
    log_rate = log_decay(head_index * local_heads, local_heads)
    position = jnp.arange(length).astype(wide)
    reach = jnp.exp(log_rate[:, None] * (position + 1.0))
    tail = jnp.exp(log_rate[:, None] * (length - 1.0 - position))
    state = jnp.einsum(
        "hjd,hje->hde",
        (key_low.astype(wide) * tail[:, :, None]).astype(low),
        value_low,
        preferred_element_type=wide,
    )
    incoming = carried_from(state, log_rate, length, False)
    qs = project(normed, w_qs)
    query_low = heads_of(qs[:, :query_width].astype(low), KD)
    swish_pre = qs[:, query_width:]
    retained, mixing, decay = retain_forward(query_low, key_low, value_low, incoming, log_rate)
    grouped = rows_of(group_norm(retained).astype(low)).astype(wide)
    gated_low = swish_gate(grouped, swish_pre).astype(low)

    def out_part(start):
        return project(lax.dynamic_slice_in_dim(gated_low, start, own_rows, 0), out_rows)

    hidden = x_own.astype(wide) + scatter_head(out_part, own_rows)
    second_own = layer_norm(hidden, gain_two, shift_two).astype(low)
    second = gather_head(second_own)
    cot = gather_head(cot_own)
    gate_pre = project(second, gate_cols)
    up_pre = project(second, up_cols)
    inner_low = gelu_gate(gate_pre, up_pre).astype(low)

    def down_part(start):
        return project(lax.dynamic_slice_in_dim(inner_low, start, own_rows, 0), down_rows)

    grad_inner = back_project(cot, down_rows)
    _, gelu_back = jax.vjp(gelu_gate, gate_pre, up_pre)
    gate_grad, up_grad = gelu_back(grad_inner)
    gate_low = gate_grad.astype(low)
    up_low = up_grad.astype(low)

    def second_part(start):
        return back_project(
            lax.dynamic_slice_in_dim(gate_low, start, own_rows, 0), gate_cols
        ) + back_project(lax.dynamic_slice_in_dim(up_low, start, own_rows, 0), up_cols)

    second_grad = scatter_head(second_part, own_rows)
    _, second_back = jax.vjp(layer_norm, hidden, gain_two, shift_two)
    hidden_part, gain_two_part, shift_two_part = second_back(second_grad)
    grad_hidden = cot_own.astype(wide) + hidden_part
    branch_low = gather_head(grad_hidden.astype(low))
    result = (hidden + scatter_head(down_part, own_rows)).astype(low)

    gated_grad = back_project(branch_low, out_rows)
    _, swish_back = jax.vjp(swish_gate, grouped, swish_pre)
    grouped_grad, swish_grad = swish_back(gated_grad)
    swish_low = swish_grad.astype(low)
    grouped_grad = heads_of(grouped_grad.astype(low).astype(wide), VD)
    _, group_back = jax.vjp(group_norm, retained)
    retained_grad = group_back(grouped_grad)[0].astype(low)

    crossed = jnp.einsum(
        "hid,hie->hde",
        (query_low.astype(wide) * reach[:, :, None]).astype(low),
        retained_grad,
        preferred_element_type=wide,
    )
    returned = carried_from(crossed, log_rate, length, True).astype(low)
    mixing_grad = jnp.einsum("hie,hje->hij", retained_grad, value_low, preferred_element_type=wide)
    scores_grad = (mixing_grad * decay).astype(low)
    query_grad = jnp.einsum("hij,hjd->hid", scores_grad, key_low, preferred_element_type=wide)
    query_grad = query_grad + reach[:, :, None] * jnp.einsum(
        "hie,hde->hid", retained_grad, incoming.astype(low), preferred_element_type=wide
    )
    keys_grad = jnp.einsum("hij,hid->hjd", scores_grad, query_low, preferred_element_type=wide)
    keys_grad = keys_grad + tail[:, :, None] * jnp.einsum(
        "hje,hde->hjd", value_low, returned, preferred_element_type=wide
    )
    values_grad = jnp.einsum("hij,hie->hje", mixing, retained_grad, preferred_element_type=wide)
    values_grad = values_grad + tail[:, :, None] * jnp.einsum(
        "hjd,hde->hje", key_low, returned, preferred_element_type=wide
    )
    query_back = rows_of(query_grad.astype(low))
    key_back = rows_of(keys_grad.astype(low)) * key_scale
    value_back = rows_of(values_grad.astype(low))
    kv_back = jnp.concatenate([key_back.astype(low), value_back], axis=1)
    qs_back = jnp.concatenate([query_back, swish_low], axis=1)

    def normed_part(start):
        return back_project(
            lax.dynamic_slice_in_dim(kv_back, start, own_rows, 0), w_kv
        ) + back_project(lax.dynamic_slice_in_dim(qs_back, start, own_rows, 0), w_qs)

    normed_grad = scatter_head(normed_part, own_rows)
    _, first_back = jax.vjp(layer_norm, x_own.astype(wide), gain_one, shift_one)
    input_part, gain_one_part, shift_one_part = first_back(normed_grad)
    grad_in = grad_hidden + input_part

    half = x_own.shape[1] // 2

    def half_of(values, part):
        return lax.slice_in_dim(values, part * half, (part + 1) * half, axis=1)

    grad_down = scatter_sq(lambda p: outer_sum(inner_low, half_of(cot, p)), 1, True)
    grad_gate = scatter_sq(lambda p: outer_sum(half_of(second, p), gate_low), 0, False)
    grad_up = scatter_sq(lambda p: outer_sum(half_of(second, p), up_low), 0, True)
    grad_out = scatter_sq(lambda p: outer_sum(gated_low, half_of(branch_low, p)), 1, False)
    grad_kv = scatter_sq(lambda p: outer_sum(half_of(normed, p), kv_back), 0, False)
    grad_qs = scatter_sq(lambda p: outer_sum(half_of(normed, p), qs_back), 0, True)

    second_norm = sum_all(true_order(jnp.stack([gain_two_part, shift_two_part])))
    second_norm = lax.dynamic_slice_in_dim(
        second_norm, sq_index * norm2_gain.shape[0], norm2_gain.shape[0], 1
    )
    first_norm = sum_all(true_order(jnp.stack([gain_one_part, shift_one_part])))
    piece = first_norm.shape[1] // (count_sq * count_head)
    first_norm = lax.dynamic_slice_in_dim(
        first_norm, (head_index * count_sq + sq_index) * piece, piece, 1
    )
    return (
        true_order(result),
        true_order(grad_in),
        first_norm[0],
        first_norm[1],
        grad_qs[:, :query_width],
        grad_kv[:, :query_width],
        grad_kv[:, query_width:],
        grad_qs[:, query_width:],
        grad_out,
        second_norm[0],
        second_norm[1],
        grad_gate,
        grad_up,
        grad_down,
    )


def solution(mesh):
    return jax.shard_map(
        shards,
        mesh=mesh,
        in_specs=(
            P(("sq", "head"), None),
            P("sq"),
            P("sq"),
            P("sq", "head"),
            P("sq", "head"),
            P("sq", "head"),
            P("sq", "head"),
            P("head", "sq"),
            P("sq"),
            P("sq"),
            P("sq", "head"),
            P("sq", "head"),
            P("head", "sq"),
            P(("sq", "head"), None),
        ),
        out_specs=(
            P(("sq", "head"), None),
            P(("sq", "head"), None),
            P(("head", "sq")),
            P(("head", "sq")),
            P("sq", "head"),
            P("sq", "head"),
            P("sq", "head"),
            P("sq", "head"),
            P("head", "sq"),
            P("sq"),
            P("sq"),
            P("sq", "head"),
            P("sq", "head"),
            P("head", "sq"),
        ),
        check_vma=False,
    )
```

```python
import functools

import jax
import jax.numpy as jnp
from jax import lax
from jax.experimental import pallas as pl
from jax.experimental.pallas import tpu as pltpu
from jax.sharding import PartitionSpec as P

KD = 256
VD = 512
CHUNK = 256


eps_layer = 1e-05
eps_group = 1e-06
low = jnp.bfloat16
wide = jnp.float32


def mask_of(slot, count):
    bits = count.bit_length() - 1
    return ((slot << 1) & (count - 1)) | (slot >> (bits - 1))


def slot_of(mask, count):
    bits = count.bit_length() - 1
    return (mask >> 1) | ((mask & 1) << (bits - 1))


def flip(value, mask):
    count = lax.axis_size("sq")
    return lax.ppermute(value, "sq", [(i, i ^ mask) for i in range(count)])


def route(swapped):
    count = lax.axis_size("sq")
    lower = list(range(count.bit_length() - 2))
    return lower[::-1] if swapped else lower


def own_order(values):
    count = lax.axis_size("sq")
    width = values.shape[-1] // count
    place = lax.axis_index("sq")
    return jnp.concatenate(
        [
            lax.dynamic_slice_in_dim(values, (place ^ mask_of(s, count)) * width, width, -1)
            for s in range(count)
        ],
        axis=-1,
    )


def true_order(values):
    count = lax.axis_size("sq")
    width = values.shape[-1] // count
    place = lax.axis_index("sq")
    return jnp.concatenate(
        [
            lax.dynamic_slice_in_dim(values, slot_of(place ^ b, count) * width, width, -1)
            for b in range(count)
        ],
        axis=-1,
    )


class Box:
    def __init__(self, value):
        self.value = value

    def get(self):
        return [self.value]

    def put(self, values):
        (self.value,) = values


class Gather:
    def __init__(self, *shards):
        self.count = lax.axis_size("sq")
        self.top = self.count // 2
        self.pieces = [{0: shard} for shard in shards]
        self.todo = []
        for swapped in (False, True):
            slots, units = [0], []
            for bit in route(swapped):
                units += [(s, bit) for s in slots]
                slots += [s | 1 << bit for s in slots]
            self.todo.append(units)

    def send(self, times=1):
        for k, held in enumerate(self.pieces):
            for slot, bit in self.todo[k][:times]:
                held[slot | 1 << bit] = flip(held[slot], mask_of(1 << bit, self.count))
            self.todo[k] = self.todo[k][times:]

    def rest(self):
        self.send(len(self.todo[0]))

    def core(self, most=None):
        for held in self.pieces:
            for slot in [s for s in held if s < self.top and s | self.top not in held][:most]:
                held[slot | self.top] = flip(held[slot], mask_of(self.top, self.count))

    def core_whole(self):
        lacks = [
            (held, s) for held in self.pieces for s in range(self.top) if s | self.top not in held
        ]
        near = jnp.stack([held[s] for held, s in lacks])
        far = flip(near, mask_of(self.top, self.count))
        for k, (held, s) in enumerate(lacks):
            held[s | self.top] = far[k]

    def list(self, k):
        return [self.pieces[k][s] for s in range(self.count)]

    def get(self):
        return [held[s] for held in self.pieces for s in sorted(held)]

    def put(self, values):
        values = iter(values)
        self.pieces = [{s: next(values) for s in sorted(held)} for held in self.pieces]


class Scatter:
    def __init__(self, product, axis, swapped):
        self.count = lax.axis_size("sq")
        self.axis = axis
        self.product = product
        self.todo = route(swapped)[::-1]
        self.pieces = {-1: flip(product(1).astype(low), mask_of(self.count // 2, self.count))}

    def near(self):
        top = self.count // 2
        total = (self.product(0) + self.pieces[-1].astype(wide)).astype(low)
        width = total.shape[self.axis] // top
        self.pieces = {
            s: lax.slice_in_dim(total, s * width, (s + 1) * width, axis=self.axis)
            for s in range(top)
        }

    def send(self):
        if -1 in self.pieces:
            self.near()
        bit, self.todo = self.todo[0], self.todo[1:]
        keep = [s for s in self.pieces if not s >> bit & 1]
        sent = jnp.concatenate([self.pieces[s | 1 << bit] for s in keep], axis=self.axis)
        got = flip(sent, mask_of(1 << bit, self.count))
        width = got.shape[self.axis] // len(keep)
        parts = {}
        for k, s in enumerate(keep):
            part = lax.slice_in_dim(got, k * width, (k + 1) * width, axis=self.axis)
            part = self.pieces[s].astype(wide) + part.astype(wide)
            parts[s] = part.astype(low) if self.todo else part
        self.pieces = parts

    def rest(self):
        while self.todo:
            self.send()
        return self.pieces[0]

    def get(self):
        return [self.pieces[s] for s in sorted(self.pieces)]

    def put(self, values):
        self.pieces = dict(zip(sorted(self.pieces), values))


def settle(*things):
    values = lax.optimization_barrier(tuple(v for t in things for v in t.get()))
    values = list(values)
    for thing in things:
        size = len(thing.get())
        thing.put(values[:size])
        values = values[size:]


def ring_step(value):
    count = lax.axis_size("head")
    return lax.ppermute(value, "head", [(i, (i + 1) % count) for i in range(count)])


def sum_all(values):
    for axis in ("sq", "head"):
        count = lax.axis_size(axis)
        step = 1
        while step < count:
            values = values + lax.ppermute(values, axis, [(i, i ^ step) for i in range(count)])
            step *= 2
    return values


def layer_norm(values, weight_gain, weight_shift):
    centered = values - jnp.mean(values, axis=-1, keepdims=True)
    spread = lax.rsqrt(jnp.mean(centered * centered, axis=-1, keepdims=True) + eps_layer)
    return centered * spread * weight_gain + weight_shift


def gelu_gate(pre_gate, pre_up):
    return jax.nn.gelu(pre_gate) * pre_up


def log_decay(first_head, head_count):
    head_ids = (first_head + jnp.arange(head_count)).astype(jnp.float32)
    return jnp.log(1.0 - jnp.exp2(-5.0 - head_ids))


def project(left_side, right_side):
    return jnp.dot(left_side, right_side, preferred_element_type=jnp.float32)


def outer_sum(left_side, right_side):
    return lax.dot_general(
        left_side, right_side, (((0,), (0,)), ((), ())), preferred_element_type=jnp.float32
    )


def back_project(gradient, weight):
    return lax.dot_general(
        gradient, weight, (((1,), (1,)), ((), ())), preferred_element_type=jnp.float32
    )


def swap_head(value, mask):
    count = lax.axis_size("head")
    return lax.ppermute(value, "head", [(i, i ^ mask) for i in range(count)])


def combine_kernel(heads, factor_ref, *refs):
    total_ref = refs[-1]
    pieces = refs[:-1]
    count = len(pieces) // 2
    size = pieces[0].shape[0]
    for part in range(2):
        for begin in range(0, size, KD // 2):
            h, row = divmod(part * size + begin, KD)
            total = jnp.zeros((KD // 2, VD), wide)
            for k in range(count):
                piece = pieces[part * count + k][pl.ds(begin, KD // 2), :]
                total = total + factor_ref[k * heads + h] * piece.astype(wide)
            total_ref[h, pl.ds(row, KD // 2), :] = total


def combine(gather, log_rate, length, backward):
    count = lax.axis_size("sq")
    place = lax.axis_index("sq")
    heads = log_rate.shape[0]
    factors = []
    for slot in range(1, count):
        other = place ^ mask_of(slot, count)
        ahead = (other - place) if backward else (place - other)
        between = jnp.maximum(ahead - 1, 0).astype(wide) * length
        factors.append(jnp.where(ahead > 0, jnp.exp(log_rate * between), 0.0))
    pieces = gather.list(0)[1:] + gather.list(1)[1:]
    return call(
        functools.partial(combine_kernel, heads),
        (1,),
        in_specs=[smem] + [pl.BlockSpec(pieces[0].shape, lambda i: (0, 0))] * len(pieces),
        out_specs=pl.BlockSpec((heads, KD, VD), lambda i: (0, 0, 0)),
        out_shape=jax.ShapeDtypeStruct((heads, KD, VD), wide),
    )(jnp.concatenate(factors), *pieces)


def gather_states(state):
    rows = state.astype(low).reshape(-1, VD)
    return Gather(rows[: rows.shape[0] // 2], rows[rows.shape[0] // 2 :])


def call(kernel, grid, **options):
    return pl.pallas_call(
        kernel,
        grid=grid,
        compiler_params=pltpu.CompilerParams(
            dimension_semantics=("arbitrary",) * len(grid), vmem_limit_bytes=50 * 2**20
        ),
        **options,
    )


def dot(left_side, right_side, left_dim=1, right_dim=0):
    return lax.dot_general(
        left_side,
        right_side,
        (((left_dim,), (right_dim,)), ((), ())),
        preferred_element_type=wide,
    )


smem = pl.BlockSpec(memory_space=pltpu.SMEM)


def reach_of(rate):
    place = lax.broadcasted_iota(jnp.int32, (CHUNK, 1), 0).astype(wide)
    return jnp.exp(rate * (place + 1.0))


def tail_of(rate):
    place = lax.broadcasted_iota(jnp.int32, (CHUNK, 1), 0).astype(wide)
    return jnp.exp(rate * (CHUNK - 1.0 - place))


def decay_of(rate):
    row = lax.broadcasted_iota(jnp.int32, (CHUNK, CHUNK), 0)
    column = lax.broadcasted_iota(jnp.int32, (CHUNK, CHUNK), 1)
    spacing = (row - column).astype(wide)
    return jnp.where(spacing >= 0, jnp.exp(rate * jnp.maximum(spacing, 0.0)), 0.0)


def norm_kernel(count, order, start, *refs):
    row_refs = refs[:-2]
    norm_ref, normed_ref = refs[-2:]
    width = normed_ref.shape[1] // count
    size = row_refs[0].shape[0]
    for turn, ref in enumerate(row_refs):
        for part in range(0, size, 128):
            rows = pl.ds(part, 128)
            values = [
                ref[rows, pl.ds(pl.multiple_of(order[s] * width, width), width)].astype(wide)
                for s in range(count)
            ]
            mean = sum(jnp.sum(v, axis=1, keepdims=True) for v in values) / (count * width)
            values = [v - mean for v in values]
            square = sum(jnp.sum(v * v, axis=1, keepdims=True) for v in values)
            spread = lax.rsqrt(square / (count * width) + eps_layer)
            target = pl.ds(pl.multiple_of(start[turn] + part, 128), 128)
            for s in range(count):
                columns = pl.ds(s * width, width)
                normed_ref[target, columns] = (
                    values[s] * spread * norm_ref[0:1, columns] + norm_ref[1:2, columns]
                ).astype(low)


def norm_rows(slots, norms, order, start):
    size, depth = slots[0].shape
    length = size * len(slots)
    return call(
        functools.partial(norm_kernel, lax.axis_size("sq")),
        (1,),
        in_specs=[smem, smem]
        + [pl.BlockSpec((size, depth), lambda i: (0, 0))] * len(slots)
        + [pl.BlockSpec(norms.shape, lambda i: (0, 0))],
        out_specs=pl.BlockSpec((length, depth), lambda i: (0, 0)),
        out_shape=jax.ShapeDtypeStruct((length, depth), low),
    )(order, start, *slots, norms)


def parts_of(heads):
    values = [pl.ds(h * VD, VD) for h in range(heads)]
    keys = [pl.ds(heads * VD + h * KD, KD) for h in range(heads)]
    return values, keys


def state_kernel(heads, chunks, rate_ref, kv_ref, state_ref):
    values, keys = parts_of(heads)
    turn = pl.program_id(0)

    @pl.when(turn == 0)
    def _():
        state_ref[...] = jnp.zeros_like(state_ref)

    for h in range(heads):
        rate = rate_ref[h]
        scaled = (kv_ref[:, keys[h]].astype(wide) * tail_of(rate)).astype(low)
        kept = state_ref[h] * jnp.exp(jnp.full((1, 1), rate * CHUNK, wide))
        state_ref[h] = kept + dot(scaled, kv_ref[:, values[h]], 0, 0)


def final_state(kv, log_rate, heads):
    length, columns = kv.shape
    chunks = length // CHUNK
    return call(
        functools.partial(state_kernel, heads, chunks),
        (chunks,),
        in_specs=[smem, pl.BlockSpec((CHUNK, columns), lambda c: (c, 0))],
        out_specs=pl.BlockSpec((heads, KD, VD), lambda c: (0, 0, 0)),
        out_shape=jax.ShapeDtypeStruct((heads, KD, VD), wide),
    )(log_rate, kv)


def retain_kernel(
    heads, rate_ref, kv_ref, qs_ref, first_ref, gated_ref, grouped_ref, factor_ref, states_ref, held, table
):
    values, keys = parts_of(heads)

    @pl.when(pl.program_id(0) == 0)
    def _():
        held[...] = first_ref[...]
        for h in range(heads):
            table[h] = decay_of(rate_ref[h])

    for h in range(heads):
        rate = rate_ref[h]
        query, key = qs_ref[:, keys[h]], kv_ref[:, keys[h]]
        value = kv_ref[:, values[h]]
        state = held[h]
        state_low = state.astype(low)
        states_ref[0, h] = state_low
        mixing = (dot(query, key, 1, 1) * table[h]).astype(low)
        retained = dot(mixing, value) + reach_of(rate) * dot(query, state_low)
        scaled = (key.astype(wide) * tail_of(rate)).astype(low)
        held[h] = state * jnp.exp(jnp.full((1, 1), rate * CHUNK, wide)) + dot(scaled, value, 0, 0)
        factor = lax.rsqrt(jnp.mean(retained * retained, axis=1, keepdims=True) + eps_group)
        grouped = (retained * factor).astype(low)
        factor_ref[h] = factor
        grouped_ref[:, values[h]] = grouped
        pre = qs_ref[:, values[h]].astype(wide)
        gated_ref[:, values[h]] = (grouped.astype(wide) * (pre * jax.nn.sigmoid(pre))).astype(low)


def retain(kv, qs, first, log_rate, heads):
    length, columns = kv.shape
    chunks = length // CHUNK
    rows = pl.BlockSpec((CHUNK, columns), lambda c: (c, 0))
    out = pl.BlockSpec((CHUNK, heads * VD), lambda c: (c, 0))
    return call(
        functools.partial(retain_kernel, heads),
        (chunks,),
        in_specs=[smem, rows, rows, pl.BlockSpec((heads, KD, VD), lambda c: (0, 0, 0))],
        out_specs=[
            out,
            out,
            pl.BlockSpec((heads, CHUNK, 1), lambda c: (0, c, 0)),
            pl.BlockSpec((1, heads, KD, VD), lambda c: (c, 0, 0, 0)),
        ],
        out_shape=[
            jax.ShapeDtypeStruct((length, heads * VD), low),
            jax.ShapeDtypeStruct((length, heads * VD), low),
            jax.ShapeDtypeStruct((heads, length, 1), wide),
            jax.ShapeDtypeStruct((chunks, heads, KD, VD), low),
        ],
        scratch_shapes=[pltpu.VMEM((heads, KD, VD), wide), pltpu.VMEM((heads, CHUNK, CHUNK), wide)],
    )(log_rate, kv, qs, first)


def gate_back_kernel(
    heads, rate_ref, branch_ref, out_ref, grouped_ref, factor_ref, qs_ref, swish_ref, retained_ref, crossed_ref
):
    values, keys = parts_of(heads)
    turn = pl.program_id(0)

    @pl.when(turn == 0)
    def _():
        crossed_ref[...] = jnp.zeros_like(crossed_ref)

    for h in range(heads):
        rate = rate_ref[h]
        gated_grad = dot(branch_ref[...], out_ref[values[h], :], 1, 1)
        grouped = grouped_ref[:, values[h]].astype(wide)
        pre = qs_ref[:, values[h]].astype(wide)
        sigma = jax.nn.sigmoid(pre)
        swish_ref[:, values[h]] = (
            gated_grad * grouped * (sigma * (1.0 + pre * (1.0 - sigma)))
        ).astype(low)
        grouped_grad = (gated_grad * (pre * sigma)).astype(low).astype(wide)
        factor = factor_ref[h]
        mean = jnp.mean(grouped_grad * grouped, axis=1, keepdims=True)
        retained_grad = (factor * (grouped_grad - grouped * mean)).astype(low)
        retained_ref[:, values[h]] = retained_grad
        start = (turn * CHUNK).astype(wide)
        scale = reach_of(rate) * jnp.exp(jnp.full((1, 1), rate * start, wide))
        scaled = (qs_ref[:, keys[h]].astype(wide) * scale).astype(low)
        crossed_ref[h] += dot(scaled, retained_grad, 0, 0)


def gate_back(branch, out_rows, grouped, factor, qs, log_rate, heads):
    length, columns = qs.shape
    depth = branch.shape[1]
    chunks = length // CHUNK
    part = pl.BlockSpec((CHUNK, heads * VD), lambda c: (c, 0))
    return call(
        functools.partial(gate_back_kernel, heads),
        (chunks,),
        in_specs=[
            smem,
            pl.BlockSpec((CHUNK, depth), lambda c: (c, 0)),
            pl.BlockSpec((heads * VD, depth), lambda c: (0, 0)),
            part,
            pl.BlockSpec((heads, CHUNK, 1), lambda c: (0, c, 0)),
            pl.BlockSpec((CHUNK, columns), lambda c: (c, 0)),
        ],
        out_specs=[part, part, pl.BlockSpec((heads, KD, VD), lambda c: (0, 0, 0))],
        out_shape=[
            jax.ShapeDtypeStruct((length, heads * VD), low),
            jax.ShapeDtypeStruct((length, heads * VD), low),
            jax.ShapeDtypeStruct((heads, KD, VD), wide),
        ],
    )(log_rate, branch, out_rows, grouped, factor, qs)


def retain_back_kernel(
    heads, rate_ref, kv_ref, qs_ref, swish_ref, grad_ref, states_ref, last_ref, kv_back_ref, qs_back_ref, held, table
):
    values, keys = parts_of(heads)

    @pl.when(pl.program_id(0) == 0)
    def _():
        held[...] = last_ref[...]
        for h in range(heads):
            table[h] = decay_of(rate_ref[h])

    for h in range(heads):
        rate = rate_ref[h]
        query, key = qs_ref[:, keys[h]], kv_ref[:, keys[h]]
        value, grad = kv_ref[:, values[h]], grad_ref[:, values[h]]
        decay = table[h]
        reach, tail = reach_of(rate), tail_of(rate)
        later = held[h]
        later_low = later.astype(low)
        mixing = (dot(query, key, 1, 1) * decay).astype(low)
        scores_grad = (dot(grad, value, 1, 1) * decay).astype(low)
        qs_back_ref[:, keys[h]] = (
            dot(scores_grad, key) + reach * dot(grad, states_ref[0, h], 1, 1)
        ).astype(low)
        kv_back_ref[:, keys[h]] = (
            dot(scores_grad, query, 0, 0) + tail * dot(value, later_low, 1, 1)
        ).astype(low)
        kv_back_ref[:, values[h]] = (
            dot(mixing, grad, 0, 0) + tail * dot(key, later_low)
        ).astype(low)
        scaled = (query.astype(wide) * reach).astype(low)
        held[h] = later * jnp.exp(jnp.full((1, 1), rate * CHUNK, wide)) + dot(scaled, grad, 0, 0)
        qs_back_ref[:, values[h]] = swish_ref[:, values[h]]


def retain_back(kv, qs, swish_grad, retained_grad, states, last, log_rate, heads):
    length, columns = kv.shape
    chunks = length // CHUNK
    rows = pl.BlockSpec((CHUNK, columns), lambda c: (chunks - 1 - c, 0))
    part = pl.BlockSpec((CHUNK, heads * VD), lambda c: (chunks - 1 - c, 0))
    return call(
        functools.partial(retain_back_kernel, heads),
        (chunks,),
        in_specs=[
            smem,
            rows,
            rows,
            part,
            part,
            pl.BlockSpec((1, heads, KD, VD), lambda c: (chunks - 1 - c, 0, 0, 0)),
            pl.BlockSpec((heads, KD, VD), lambda c: (0, 0, 0)),
        ],
        out_specs=[rows, rows],
        out_shape=[jax.ShapeDtypeStruct((length, columns), low)] * 2,
        scratch_shapes=[pltpu.VMEM((heads, KD, VD), wide), pltpu.VMEM((heads, CHUNK, CHUNK), wide)],
    )(log_rate, kv, qs, swish_grad, retained_grad, states, last)


def shards(
    layer_in,
    norm1_gain,
    norm1_bias,
    w_query,
    w_key,
    w_value,
    w_swish,
    w_out,
    norm2_gain,
    norm2_bias,
    w_gate,
    w_up,
    w_down,
    cotangent,
):
    count_sq = lax.axis_size("sq")
    count_head = lax.axis_size("head")
    sq_index = lax.axis_index("sq")
    head_index = lax.axis_index("head")
    own_rows = layer_in.shape[0]
    length = own_rows * count_head
    key_scale = KD ** (-0.5)
    value_width = w_value.shape[1]
    heads = value_width // VD
    log_rate = log_decay(head_index * heads, heads)
    order = jnp.stack([sq_index ^ mask_of(s, count_sq) for s in range(count_sq)]).astype(jnp.int32)
    start = [lax.rem(head_index - t + count_head, count_head) * own_rows for t in range(count_head)]
    kin_steps = []
    while 2 << len(kin_steps) < count_head:
        kin_steps.append(2 << len(kin_steps))

    key_width = w_key.shape[1]
    weight_rows = w_key.shape[0]
    pair_width = value_width + key_width

    def fold(weight):
        parts = weight.shape[0] // weight_rows
        return jnp.concatenate(
            [weight[c * weight_rows : (c + 1) * weight_rows] for c in range(parts)], axis=1
        )

    def unfold(first, second):
        columns = first[0].shape[1]
        return jnp.concatenate(
            [
                jnp.concatenate([p[:, c : c + weight_rows] for p in side], axis=1)
                for side in (first, second)
                for c in range(0, columns, weight_rows)
            ],
            axis=0,
        )

    folded_out = fold(w_out)
    out_half = folded_out.shape[1] // 2
    norm_rows_in = jnp.stack([norm1_gain, norm1_bias, norm2_gain, norm2_bias])
    norm_rows_in = jnp.pad(
        norm_rows_in, ((0, 12), (0, pair_width + out_half - norm_rows_in.shape[1]))
    )
    first_pack = jnp.concatenate(
        [w_value, (w_key.astype(wide) * key_scale).astype(low), folded_out[:, :out_half]], axis=1
    )
    first = Gather(
        jnp.concatenate([first_pack, norm_rows_in], axis=0),
        jnp.concatenate([w_swish, w_query, folded_out[:, out_half:]], axis=1),
    )
    feed_shard = Box((w_gate, w_up, w_down, cotangent))
    feed_shard.get = lambda: list(feed_shard.value)
    feed_shard.put = lambda values: setattr(feed_shard, "value", tuple(values))
    slots = [Box(layer_in)]
    for turn in range(1, count_head):
        slots.append(Box(ring_step(slots[-1].value)))
        first.core(1)
        first.send()
        settle(first, slots[-1], feed_shard)
    first.rest()
    first.core()

    def kin(value):
        held = [value]
        for step in kin_steps:
            held += [swap_head(v, step) for v in held]
        return held

    gate_shard, up_shard, down_shard, cot_shard = feed_shard.value
    quarter_width = gate_shard.shape[1]
    feed_packs = kin(jnp.concatenate([gate_shard, up_shard, fold(down_shard)], axis=1))
    quarters = len(feed_packs)

    def gather_feed(pack):
        gate, up, down = jnp.split(pack, 3, axis=1)
        middle = quarter_width // 2
        return Gather(
            jnp.concatenate([gate, down[:, :middle]], axis=1),
            jnp.concatenate([up, down[:, middle:]], axis=1),
        )

    feeds = [gather_feed(feed_packs[0])]
    feeds[0].send()
    cot_own = own_order(cot_shard)
    cot_far = swap_head(cot_own, 1)
    x_own = own_order(layer_in)
    norms = jnp.concatenate([p[weight_rows : weight_rows + 4, :weight_rows] for p in first.list(0)], axis=1)
    norms = norms.astype(wide)
    gain_one, shift_one, gain_two, shift_two = norms[0], norms[1], norms[2], norms[3]
    w_kv = jnp.concatenate([p[:weight_rows, :pair_width] for p in first.list(0)], axis=0)
    w_qs = jnp.concatenate([p[:, :pair_width] for p in first.list(1)], axis=0)
    out_rows = unfold(
        [p[:weight_rows, pair_width:] for p in first.list(0)],
        [p[:, pair_width:] for p in first.list(1)],
    )
    normed = norm_rows(
        [b.value for b in slots], norms, order, jnp.stack(start).astype(jnp.int32)
    )
    kv = project(normed, w_kv).astype(low)
    state = final_state(kv, log_rate, heads)

    passed = gather_states(state)
    settle(feeds[0], passed)
    passed.send()
    settle(passed)
    passed.rest()
    settle(feeds[0], passed)
    passed.core_whole()
    feeds[0].core(1)
    feeds[0].send()
    incoming = combine(passed, log_rate, length, False)
    qs = project(normed, w_qs).astype(low)
    gated_low, grouped, factor, states = retain(kv, qs, incoming, log_rate, heads)

    def out_part(turn):
        turn = turn % count_head
        return project(lax.dynamic_slice_in_dim(gated_low, start[turn], own_rows, 0), out_rows)

    total = Box(out_part(1).astype(low))
    settle(feeds[0], total)
    for turn in range(2, count_head + 1):
        got = Box(ring_step(total.value))
        part = Box(out_part(turn))
        feeds[0].core(1)
        if turn == 2:
            feeds[0].send()
        elif turn == 3:
            feeds += [gather_feed(p) for p in feed_packs[1:]]
        for thing in feeds[1:]:
            thing.send()
        settle(got, part, *feeds)
        part = part.value + got.value.astype(wide)
        total = Box(part.astype(low) if turn < count_head else part)
    hidden = x_own.astype(wide) + total.value
    second_own = layer_norm(hidden, gain_two, shift_two).astype(low)
    near = Box(second_own)
    settle(near, *feeds)
    second_far = Box(swap_head(near.value, 1))
    for thing in feeds[1:]:
        thing.core(1)
    for thing in feeds:
        thing.rest()
    feeds[0].core()
    settle(second_far, *feeds[1:])
    second_far = second_far.value
    for thing in feeds[1:]:
        thing.core_whole()
    gate_full, up_full, down_full = [], [], []
    for thing in feeds:
        one, two = thing.list(0), thing.list(1)
        gate_full.append(jnp.concatenate([p[:, :quarter_width] for p in one], axis=0))
        up_full.append(jnp.concatenate([p[:, :quarter_width] for p in two], axis=0))
        down_full.append(
            unfold([p[:, quarter_width:] for p in one], [p[:, quarter_width:] for p in two])
        )

    def feed(second, cot, t):
        gate_pre = project(second, gate_full[t])
        up_pre = project(second, up_full[t])
        grad_inner = back_project(cot, down_full[t])
        inner = gelu_gate(gate_pre, up_pre).astype(low)
        _, gelu_back = jax.vjp(gelu_gate, gate_pre, up_pre)
        gate_grad, up_grad = gelu_back(grad_inner)
        gate_grad, up_grad = gate_grad.astype(low), up_grad.astype(low)
        second_grad = back_project(gate_grad, gate_full[t]) + back_project(up_grad, up_full[t])
        return inner, gate_grad, up_grad, second_grad

    fed_own = [feed(second_own, cot_own, 0)]
    fed_far = [feed(second_far, cot_far, t) for t in range(quarters)]
    grad_far = Box(sum(f[3] for f in fed_far).astype(low))
    near = Box(second_own)
    settle(grad_far, near)
    grad_far = Box(swap_head(grad_far.value, 1))
    fed_own += [feed(near.value, cot_own, t) for t in range(1, quarters)]
    inner_low, gate_low, up_low = [
        [jnp.concatenate([fed_own[t][k], fed_far[t][k]]) for t in range(quarters)] for k in range(3)
    ]
    second = jnp.concatenate([second_own, second_far])
    cot = jnp.concatenate([cot_own, cot_far])
    depth = x_own.shape[1]

    def half_of(values, part):
        return lax.slice_in_dim(values, part * depth // 2, (part + 1) * depth // 2, axis=1)

    def scatter_gate(t):
        return Scatter(lambda p: outer_sum(half_of(second, p), gate_low[t]), 0, False)

    def scatter_up(t):
        return Scatter(lambda p: outer_sum(half_of(second, p), up_low[t]), 0, True)

    def scatter_down(t):
        return Scatter(lambda p: outer_sum(inner_low[t], half_of(cot, p)), 1, t % 2 == 1)

    late = range(1, quarters)
    gate_sums, up_sums, down_sums = [None] * quarters, [None] * quarters, [None] * quarters
    for t in late:
        gate_sums[t], up_sums[t] = scatter_gate(t), scatter_up(t)
    settle(grad_far, *gate_sums[1:], *up_sums[1:])
    second_grad = sum(f[3] for f in fed_own) + grad_far.value.astype(wide)
    _, second_back = jax.vjp(layer_norm, hidden, gain_two, shift_two)
    hidden_part, gain_two_part, shift_two_part = second_back(second_grad)
    grad_hidden = cot_own.astype(wide) + hidden_part

    slots = [Box(grad_hidden.astype(low))]
    waits = gate_sums[1:] + up_sums[1:]
    for turn in range(1, count_head):
        slots.append(Box(ring_step(slots[-1].value)))
        if turn == 1:
            for thing in waits:
                thing.send()
            for t in late:
                down_sums[t] = scatter_down(t)
            down_sums[0] = scatter_down(0)
            waits += down_sums
        elif turn == 2:
            for thing in down_sums:
                thing.send()
            gate_sums[0], up_sums[0] = scatter_gate(0), scatter_up(0)
            waits += [gate_sums[0], up_sums[0]]
        elif turn == 3:
            for thing in gate_sums[1:] + up_sums[1:] + down_sums:
                thing.rest()
        settle(slots[-1], *waits)
    branch_low = jnp.zeros((length, depth), low)
    for turn, rows in enumerate(slots):
        branch_low = lax.dynamic_update_slice_in_dim(branch_low, rows.value, start[turn], 0)
    down_own = sum(project(fed_own[t][0], down_full[t]) for t in range(quarters))
    down_far = sum(project(fed_far[t][0], down_full[t]) for t in range(quarters))
    result = (hidden + down_own + swap_head(down_far.astype(low), 1).astype(wide)).astype(low)

    def kin_sum(held):
        total = 0.0
        held = [None] + [h.astype(low) for h in held]
        for step in kin_steps[::-1]:
            size = len(held) // 2
            got = [swap_head(h, step).astype(wide) for h in held[size:]]
            total = total + got[0]
            held = [None] + [(h.astype(wide) + g).astype(low) for h, g in zip(held[1:size], got[1:])]
        return total

    swish_grad, retained_grad, crossed = gate_back(
        branch_low, out_rows, grouped, factor, qs, log_rate, heads
    )
    late_sums = [jnp.stack([gate_sums[t].rest(), up_sums[t].rest(), fold(down_sums[t].rest())]) for t in late]
    early_sums = kin_sum(late_sums)
    passed = gather_states(crossed)
    settle(passed, gate_sums[0], up_sums[0])
    passed.send()
    settle(passed)
    passed.rest()
    settle(passed, gate_sums[0], up_sums[0])
    passed.core_whole()
    gate_sums[0].send()
    up_sums[0].send()
    returned = combine(passed, log_rate, length, True)
    kv_back, qs_back = retain_back(
        kv, qs, swish_grad, retained_grad, states, returned, log_rate, heads
    )

    def normed_part(turn):
        begin = start[turn % count_head]
        return back_project(
            lax.dynamic_slice_in_dim(kv_back, begin, own_rows, 0), w_kv
        ) + back_project(lax.dynamic_slice_in_dim(qs_back, begin, own_rows, 0), w_qs)

    total = Box(normed_part(1).astype(low))
    waits = [gate_sums[0], up_sums[0]]
    out_parts = [gated_low[:, : value_width // 2], gated_low[:, value_width // 2 :]]
    for turn in range(2, count_head + 1):
        got = Box(ring_step(total.value))
        part = Box(normed_part(turn))
        if turn == 2:
            out_sums = [
                Scatter(lambda p, rows=rows: outer_sum(rows, half_of(branch_low, p)), 1, k == 1)
                for k, rows in enumerate(out_parts)
            ]
            kv_sum = Scatter(lambda p: outer_sum(half_of(normed, p), kv_back), 0, False)
            qs_sum = Scatter(lambda p: outer_sum(half_of(normed, p), qs_back), 0, True)
            for thing in waits:
                thing.rest()
            waits += [kv_sum, qs_sum, *out_sums]
        elif turn == 3:
            kv_sum.send()
            qs_sum.send()
        elif turn == 4:
            for thing in waits:
                thing.rest()
        settle(got, part, *waits)
        part = part.value + got.value.astype(wide)
        total = Box(part.astype(low) if turn < count_head else part)
    grad_gate = gate_sums[0].rest() + early_sums[0]
    grad_up = up_sums[0].rest() + early_sums[1]
    grad_down = down_sums[0].rest() + jnp.concatenate(
        jnp.split(early_sums[2], early_sums.shape[2] // weight_rows, axis=1), axis=0
    )
    grad_kv, grad_qs = kv_sum.rest(), qs_sum.rest()
    grad_out = jnp.concatenate([s.rest() for s in out_sums], axis=0)
    _, first_back = jax.vjp(layer_norm, x_own.astype(wide), gain_one, shift_one)
    input_part, gain_one_part, shift_one_part = first_back(total.value)
    grad_in = grad_hidden + input_part

    norm_sums = sum_all(
        true_order(jnp.stack([gain_one_part, shift_one_part, gain_two_part, shift_two_part]))
    )
    piece = depth // (count_sq * count_head)
    first_norm = lax.dynamic_slice_in_dim(
        norm_sums[:2], (head_index * count_sq + sq_index) * piece, piece, 1
    )
    piece = depth // count_sq
    second_norm = lax.dynamic_slice_in_dim(norm_sums[2:], sq_index * piece, piece, 1)
    return (
        true_order(result),
        true_order(grad_in),
        first_norm[0],
        first_norm[1],
        grad_qs[:, value_width:],
        grad_kv[:, value_width:] * key_scale,
        grad_kv[:, :value_width],
        grad_qs[:, :value_width],
        grad_out,
        second_norm[0],
        second_norm[1],
        grad_gate,
        grad_up,
        grad_down,
    )


def solution(mesh):
    return jax.shard_map(
        shards,
        mesh=mesh,
        in_specs=(
            P(("sq", "head"), None),
            P("sq"),
            P("sq"),
            P("sq", "head"),
            P("sq", "head"),
            P("sq", "head"),
            P("sq", "head"),
            P("head", "sq"),
            P("sq"),
            P("sq"),
            P("sq", "head"),
            P("sq", "head"),
            P("head", "sq"),
            P(("sq", "head"), None),
        ),
        out_specs=(
            P(("sq", "head"), None),
            P(("sq", "head"), None),
            P(("head", "sq")),
            P(("head", "sq")),
            P("sq", "head"),
            P("sq", "head"),
            P("sq", "head"),
            P("sq", "head"),
            P("head", "sq"),
            P("sq"),
            P("sq"),
            P("sq", "head"),
            P("sq", "head"),
            P("head", "sq"),
        ),
        check_vma=False,
    )
```

```python
import functools

import jax
import jax.numpy as jnp
from jax import lax
from jax.experimental import pallas as pl
from jax.experimental.pallas import tpu as pltpu
from jax.sharding import PartitionSpec as P

KD = 256
VD = 512
CHUNK = 256


eps_layer = 1e-05
eps_group = 1e-06
low = jnp.bfloat16
wide = jnp.float32


def mask_of(slot, count):
    bits = count.bit_length() - 1
    return ((slot << 1) & (count - 1)) | (slot >> (bits - 1))


def slot_of(mask, count):
    bits = count.bit_length() - 1
    return (mask >> 1) | ((mask & 1) << (bits - 1))


def flip(value, mask):
    count = lax.axis_size("sq")
    return lax.ppermute(value, "sq", [(i, i ^ mask) for i in range(count)])


def route(swapped):
    count = lax.axis_size("sq")
    lower = list(range(count.bit_length() - 2))
    return lower[::-1] if swapped else lower


def own_order(values):
    count = lax.axis_size("sq")
    width = values.shape[-1] // count
    place = lax.axis_index("sq")
    return jnp.concatenate(
        [
            lax.dynamic_slice_in_dim(values, (place ^ mask_of(s, count)) * width, width, -1)
            for s in range(count)
        ],
        axis=-1,
    )


def true_order(values):
    count = lax.axis_size("sq")
    width = values.shape[-1] // count
    place = lax.axis_index("sq")
    return jnp.concatenate(
        [
            lax.dynamic_slice_in_dim(values, slot_of(place ^ b, count) * width, width, -1)
            for b in range(count)
        ],
        axis=-1,
    )


class Box:
    def __init__(self, value):
        self.value = value

    def get(self):
        return [self.value]

    def put(self, values):
        (self.value,) = values


class Many:
    def __init__(self, *values):
        self.value = list(values)

    def get(self):
        return self.value

    def put(self, values):
        self.value = list(values)


class Gather:
    def __init__(self, *shards):
        self.count = lax.axis_size("sq")
        self.top = self.count // 2
        self.pieces = [{0: shard} for shard in shards]
        self.far = []
        self.todo = []
        for swapped in (False, True):
            slots, units = [0], []
            for bit in route(swapped):
                units += [(s, bit) for s in slots]
                slots += [s | 1 << bit for s in slots]
            self.todo.append(units)

    def send(self, times=1):
        for k, held in enumerate(self.pieces):
            for slot, bit in self.todo[k][:times]:
                held[slot | 1 << bit] = flip(held[slot], mask_of(1 << bit, self.count))
            self.todo[k] = self.todo[k][times:]

    def rest(self):
        self.send(len(self.todo[0]))

    def core(self):
        sent = [s for slots, _ in self.far for s in slots]
        ready = [s for s in range(self.top) if s not in sent and all(s in h for h in self.pieces)]
        if ready:
            both = stack([held[s] for s in ready for held in self.pieces])
            self.far.append((ready, flip(both, mask_of(self.top, self.count))))

    def refs(self):
        operands = [held[s] for held in self.pieces for s in range(self.top)]
        places = [[(k * self.top + s, None) for s in range(self.top)] for k in range(2)]
        for k in range(2):
            for s in range(self.top):
                for g, (slots, _) in enumerate(self.far):
                    if s in slots:
                        places[k].append((2 * self.top + g, 2 * slots.index(s) + k))
        return operands + [array for _, array in self.far], places

    def get(self):
        near = [held[s] for held in self.pieces for s in sorted(held)]
        return near + [array for _, array in self.far]

    def put(self, values):
        values = iter(values)
        self.pieces = [{s: next(values) for s in sorted(held)} for held in self.pieces]
        self.far = [(slots, next(values)) for slots, _ in self.far]


class Small:
    def __init__(self, shard):
        self.count = lax.axis_size("sq")
        self.pieces = {0: shard}
        bits = self.count.bit_length() - 1
        self.todo = [bits - 1, *range(bits - 1)]

    def send(self):
        if self.todo:
            bit, self.todo = self.todo[0], self.todo[1:]
            slots = sorted(self.pieces)
            far = flip(jnp.stack([self.pieces[s] for s in slots]), mask_of(1 << bit, self.count))
            for k, s in enumerate(slots):
                self.pieces[s | 1 << bit] = far[k]

    def rest(self):
        while self.todo:
            self.send()

    def get(self):
        return [self.pieces[s] for s in sorted(self.pieces)]

    def put(self, values):
        self.pieces = dict(zip(sorted(self.pieces), values))


class Scatter:
    def __init__(self, lefts, rights):
        self.count = lax.axis_size("sq")
        top = self.count // 2
        self.rows = lefts[0].shape[1] // self.count
        self.todo = [route(k == 1)[::-1] for k in range(2)]
        self.slots = [list(range(top)) for _ in range(2)]
        self.arrived = False
        self.sources = lefts, rights
        self.held = [outer_half(lefts, rights, 1)]

    def core(self):
        self.held = [flip(self.held[0], mask_of(self.count // 2, self.count))]

    def near(self):
        self.held = outer_half(*self.sources, 0, self.held[0], self.rows, self.part())

    def part(self):
        return [[s >> self.todo[k][0] & 1 for s in self.slots[k]] for k in range(2)]

    def send(self, lazy=False):
        self.merge()
        for k in range(2):
            bit, self.todo[k] = self.todo[k][0], self.todo[k][1:]
            self.held[2 * k + 1] = flip(self.held[2 * k + 1], mask_of(1 << bit, self.count))
            self.slots[k] = [s for s in self.slots[k] if not s >> bit & 1]
        self.arrived = True
        if not lazy:
            self.merge()

    def merge(self):
        if self.arrived:
            bits = self.part() if self.todo[0] else None
            self.held = list(split(self.held[::2], self.held[1::2], self.rows, bits))
            self.arrived = False

    def rest(self):
        self.merge()
        while self.todo[0]:
            self.send()
        return self.held

    def get(self):
        return list(self.held)

    def put(self, values):
        self.held = list(values)


def settle(*things):
    values = lax.optimization_barrier(tuple(v for t in things for v in t.get()))
    values = list(values)
    for thing in things:
        size = len(thing.get())
        thing.put(values[:size])
        values = values[size:]


def ring_step(value):
    count = lax.axis_size("head")
    return lax.ppermute(value, "head", [(i, (i + 1) % count) for i in range(count)])


def sum_others(values, axis, masks):
    count = lax.axis_size(axis)
    held = [values]
    held += [lax.ppermute(values, axis, [(i, i ^ m) for i in range(count)]) for m in masks]
    while len(held) > 1:
        held = [a + b for a, b in zip(held[::2], held[1::2])]
    return held[0]


def layer_norm(values, weight_gain, weight_shift):
    centered = values - jnp.mean(values, axis=-1, keepdims=True)
    spread = lax.rsqrt(jnp.mean(centered * centered, axis=-1, keepdims=True) + eps_layer)
    return centered * spread * weight_gain + weight_shift


def gelu_gate(pre_gate, pre_up):
    return jax.nn.gelu(pre_gate) * pre_up


def log_decay(first_head, head_count):
    head_ids = (first_head + jnp.arange(head_count)).astype(jnp.float32)
    return jnp.log(1.0 - jnp.exp2(-5.0 - head_ids))


def project(left_side, right_side):
    return jnp.dot(left_side, right_side, preferred_element_type=jnp.float32)


def outer_sum(left_side, right_side):
    return lax.dot_general(
        left_side, right_side, (((0,), (0,)), ((), ())), preferred_element_type=jnp.float32
    )


def back_project(gradient, weight):
    return lax.dot_general(
        gradient, weight, (((1,), (1,)), ((), ())), preferred_element_type=jnp.float32
    )


def swap_head(value, mask):
    count = lax.axis_size("head")
    return lax.ppermute(value, "head", [(i, i ^ mask) for i in range(count)])


def stack_kernel(*refs):
    for k, ref in enumerate(refs[:-1]):
        refs[-1][k] = ref[...]


def stack(pieces):
    vmem = pl.BlockSpec(memory_space=pltpu.VMEM)
    return pl.pallas_call(
        stack_kernel,
        in_specs=[vmem] * len(pieces),
        out_specs=vmem,
        out_shape=jax.ShapeDtypeStruct((len(pieces),) + pieces[0].shape, pieces[0].dtype),
        compiler_params=pltpu.CompilerParams(vmem_limit_bytes=16 * 2**20),
        cost_estimate=brief,
    )(*pieces)


def beside_kernel(*refs):
    begin = 0
    for ref in refs[:-1]:
        refs[-1][:, pl.ds(begin, ref.shape[1])] = ref[...]
        begin += ref.shape[1]


def beside(pieces):
    vmem = pl.BlockSpec(memory_space=pltpu.VMEM)
    columns = sum(p.shape[1] for p in pieces)
    return pl.pallas_call(
        beside_kernel,
        in_specs=[vmem] * len(pieces),
        out_specs=vmem,
        out_shape=jax.ShapeDtypeStruct((pieces[0].shape[0], columns), pieces[0].dtype),
        compiler_params=pltpu.CompilerParams(vmem_limit_bytes=16 * 2**20),
        cost_estimate=brief,
    )(*pieces)


def add_rows_kernel(whole_ref, got_ref, out_ref):
    total = whole_ref[...].astype(wide) + got_ref[...].astype(wide)
    out_ref[...] = total.astype(out_ref.dtype)


def add_rows(whole, place, got, kind):
    rows, columns = got.shape
    block = min(columns, 1024)
    part = pl.BlockSpec((rows, block), lambda j: (0, j))
    return call(
        add_rows_kernel,
        (columns // block,),
        in_specs=[pl.BlockSpec((rows, block), lambda j: (place, j)), part],
        out_specs=part,
        out_shape=jax.ShapeDtypeStruct(got.shape, kind),
    )(whole, got)


def split_kernel(rows, bits, *refs):
    ins, outs = refs[:4], refs[4:]
    for k in range(2):
        kept, got = ins[2 * k : 2 * k + 2]
        total = kept[...].astype(wide) + got[...].astype(wide)
        if bits is None:
            outs[k][...] = total
        else:
            taken = [0, 0]
            for i, side in enumerate(bits[k]):
                place = pl.ds(taken[side] * rows, rows)
                outs[2 * k + side][place, :] = total[i * rows : (i + 1) * rows].astype(low)
                taken[side] += 1


def split(kept, got, rows, bits):
    size, columns = kept[0].shape
    block = 512 if columns % 512 == 0 else 256
    part = pl.BlockSpec((size, block), lambda j: (0, j))
    half = pl.BlockSpec((size // 2, block), lambda j: (0, j))
    if bits is None:
        out_specs = [part] * 2
        out_shape = [jax.ShapeDtypeStruct((size, columns), wide)] * 2
    else:
        out_specs = [half] * 4
        out_shape = [jax.ShapeDtypeStruct((size // 2, columns), low)] * 4
    return call(
        functools.partial(split_kernel, rows, bits),
        (columns // block,),
        in_specs=[part] * 4,
        out_specs=out_specs,
        out_shape=out_shape,
    )(kept[0], got[0], kept[1], got[1])


def combine_kernel(heads, places, factor_ref, *refs):
    *piece_refs, total_ref = refs
    size = heads * KD // 2
    for part in range(2):
        for begin in range(0, size, KD // 2):
            h, row = divmod(part * size + begin, KD)
            rows = pl.ds(begin, KD // 2)
            total = jnp.zeros((KD // 2, VD), wide)
            for k, (operand, index) in enumerate(places[part][1:]):
                ref = piece_refs[operand]
                piece = ref[rows, :] if index is None else ref[index, rows, :]
                total = total + factor_ref[k * heads + h] * piece.astype(wide)
            total_ref[h, pl.ds(row, KD // 2), :] = total


def combine(gather, log_rate, length, backward):
    count = lax.axis_size("sq")
    place = lax.axis_index("sq")
    heads = log_rate.shape[0]
    factors = []
    for slot in range(1, count):
        other = place ^ mask_of(slot, count)
        ahead = (other - place) if backward else (place - other)
        between = jnp.maximum(ahead - 1, 0).astype(wide) * length
        factors.append(jnp.where(ahead > 0, jnp.exp(log_rate * between), 0.0))
    operands, places = gather.refs()
    vmem = pl.BlockSpec(memory_space=pltpu.VMEM)
    return pl.pallas_call(
        functools.partial(combine_kernel, heads, places),
        in_specs=[smem] + [vmem] * len(operands),
        out_specs=vmem,
        out_shape=jax.ShapeDtypeStruct((heads, KD, VD), wide),
        compiler_params=pltpu.CompilerParams(vmem_limit_bytes=56 * 2**20),
        cost_estimate=brief,
    )(jnp.concatenate(factors), *operands)


def call(kernel, grid, **options):
    return pl.pallas_call(
        kernel,
        grid=grid,
        cost_estimate=brief,
        compiler_params=pltpu.CompilerParams(
            dimension_semantics=("arbitrary",) * len(grid), vmem_limit_bytes=20 * 2**20
        ),
        **options,
    )


def dot(left_side, right_side, left_dim=1, right_dim=0):
    return lax.dot_general(
        left_side,
        right_side,
        (((left_dim,), (right_dim,)), ((), ())),
        preferred_element_type=wide,
    )


smem = pl.BlockSpec(memory_space=pltpu.SMEM)


def reach_of(rate):
    place = lax.broadcasted_iota(jnp.int32, (CHUNK, 1), 0).astype(wide)
    return jnp.exp(rate * (place + 1.0))


def tail_of(rate):
    place = lax.broadcasted_iota(jnp.int32, (CHUNK, 1), 0).astype(wide)
    return jnp.exp(rate * (CHUNK - 1.0 - place))


def decay_of(rate):
    row = lax.broadcasted_iota(jnp.int32, (CHUNK, CHUNK), 0)
    column = lax.broadcasted_iota(jnp.int32, (CHUNK, CHUNK), 1)
    spacing = (row - column).astype(wide)
    return jnp.where(spacing >= 0, jnp.exp(rate * jnp.maximum(spacing, 0.0)), 0.0)


brief = pl.CostEstimate(flops=1, bytes_accessed=1, transcendentals=0)


def bring(copies):
    for copy in copies:
        copy.start()
    return copies


def bring_pieces(refs, places, whole, sems, first):
    rows = whole.shape[0] // len(places)
    return bring(
        [
            pltpu.make_async_copy(
                refs[operand] if index is None else refs[operand].at[index],
                whole.at[pl.ds(k * rows, rows), :],
                sems.at[first + k],
            )
            for k, (operand, index) in enumerate(places)
        ]
    )


def wait_all(copies):
    for copy in copies:
        copy.wait()


def project_blocks(left, weight, product_ref):
    block = 256

    def one(j, carry):
        columns = pl.ds(pl.multiple_of(j * block, block), block)
        product_ref[:, columns] = dot(left[...], weight[:, columns]).astype(low)
        return carry

    lax.fori_loop(0, product_ref.shape[1] // block, one, 0)


def norm_project_kernel(count, slots, places, order, start, *refs):
    row_refs = refs[:slots]
    norm_ref = refs[slots]
    piece_refs = refs[slots + 1 : -8]
    normed_ref, xhat_ref, product_ref, full_ref, weight, normed, xhat, sems = refs[-8:]
    width = normed.shape[1] // count
    size = row_refs[0].shape[0]
    tile = 64
    copies = bring_pieces(piece_refs, places, weight, sems, 0)
    for turn, ref in enumerate(row_refs):

        def tile_of(t, carry, ref=ref, turn=turn):
            rows = pl.ds(pl.multiple_of(t * tile, tile), tile)
            values = [
                ref[rows, pl.ds(pl.multiple_of(order[s] * width, width), width)].astype(wide)
                for s in range(count)
            ]
            total = values[0]
            for v in values[1:]:
                total = total + v
            mean = jnp.sum(total, axis=1, keepdims=True) / (count * width)
            values = [v - mean for v in values]
            square = values[0] * values[0]
            for v in values[1:]:
                square = square + v * v
            square = jnp.sum(square, axis=1, keepdims=True)
            spread = lax.rsqrt(square / (count * width) + eps_layer)
            target = pl.ds(pl.multiple_of(start[turn] + t * tile, tile), tile)
            for s in range(count):
                columns = pl.ds(s * width, width)
                scaled = values[s] * spread
                xhat[target, columns] = scaled.astype(low)
                normed[target, columns] = (
                    scaled * norm_ref[0:1, columns] + norm_ref[1:2, columns]
                ).astype(low)
            return carry

        lax.fori_loop(0, size // tile, tile_of, 0)

    away = bring(
        [
            pltpu.make_async_copy(normed, normed_ref, sems.at[count]),
            pltpu.make_async_copy(xhat, xhat_ref, sems.at[count + 1]),
        ]
    )
    wait_all(copies)
    away += bring([pltpu.make_async_copy(weight, full_ref, sems.at[count + 2])])
    project_blocks(normed, weight, product_ref)
    wait_all(away)


def norm_project(slots, norms, gather, columns, order, start):
    count = gather.count
    pieces, places = gather.refs()
    size, depth = slots[0].shape
    length = size * len(slots)
    width = pieces[0].shape[1]
    vmem = pl.BlockSpec(memory_space=pltpu.VMEM)
    whole = pl.BlockSpec(memory_space=pl.ANY)
    return pl.pallas_call(
        functools.partial(norm_project_kernel, count, len(slots), places[0]),
        in_specs=[smem, smem] + [vmem] * (len(slots) + 1) + [whole] * len(pieces),
        out_specs=[whole, whole, vmem, whole],
        out_shape=[
            jax.ShapeDtypeStruct((length, depth), low),
            jax.ShapeDtypeStruct((length, depth), low),
            jax.ShapeDtypeStruct((length, columns), low),
            jax.ShapeDtypeStruct((depth, width), low),
        ],
        scratch_shapes=[
            pltpu.VMEM((depth, width), low),
            pltpu.VMEM((length, depth), low),
            pltpu.VMEM((length, depth), low),
            pltpu.SemaphoreType.DMA((count + 3,)),
        ],
        compiler_params=pltpu.CompilerParams(vmem_limit_bytes=36 * 2**20),
        cost_estimate=brief,
    )(order, start, *slots, norms, *pieces)


def project_kernel(count, places, left_ref, *refs):
    product_ref, full_ref, weight, sems = refs[-4:]
    wait_all(bring_pieces(refs[:-4], places, weight, sems, 0))
    away = bring([pltpu.make_async_copy(weight, full_ref, sems.at[count])])
    project_blocks(left_ref, weight, product_ref)
    wait_all(away)


def project_pieces(left_side, gather, columns):
    length, depth = left_side.shape
    count = gather.count
    pieces, places = gather.refs()
    width = pieces[0].shape[1]
    vmem = pl.BlockSpec(memory_space=pltpu.VMEM)
    whole = pl.BlockSpec(memory_space=pl.ANY)
    return pl.pallas_call(
        functools.partial(project_kernel, count, places[1]),
        in_specs=[vmem] + [whole] * len(pieces),
        out_specs=[vmem, whole],
        out_shape=[
            jax.ShapeDtypeStruct((length, columns), low),
            jax.ShapeDtypeStruct((depth, width), low),
        ],
        scratch_shapes=[pltpu.VMEM((depth, width), low), pltpu.SemaphoreType.DMA((count + 1,))],
        compiler_params=pltpu.CompilerParams(vmem_limit_bytes=20 * 2**20),
        cost_estimate=brief,
    )(left_side, *pieces)


def feed_kernel(top, quarter, places, sizes, has_prior, second_ref, cot_ref, *refs):
    quarters = len(places)
    piece_refs = []
    for size in sizes:
        piece_refs.append(refs[:size])
        refs = refs[size:]
    if has_prior:
        prior_grad, prior_down, *refs = refs
    hidden_refs = [refs[2 * t : 2 * t + 2] for t in range(quarters)]
    grad_ref, down_part_ref = refs[2 * quarters : 2 * quarters + 2]
    first, later, gate_pre, up_pre, grad_inner, sums, sems = refs[2 * quarters + 2 :]
    rows, depth = second_ref.shape
    middle = quarter // 2
    hidden = pl.ds(0, quarter)
    hidden_up = pl.ds(quarter, quarter)
    down = pl.ds(quarter, middle)
    sides = [pl.ds(0, middle), pl.ds(middle, middle)]
    halves = [pl.ds(0, depth // 2), pl.ds(depth // 2, depth // 2)]
    copies = []
    for t in range(quarters):
        for k, whole in enumerate((first, later)):
            index = (t * 2 + k) * 2 * top
            some = bring_pieces(piece_refs[t], places[t][k], whole.at[t], sems, index)
            copies += [some[:top], some[top:]]
    tile = 16
    scale = 0.7978845608028654
    for t in range(quarters):
        inner_ref, grads_ref = hidden_refs[t]
        for k, (whole, target) in enumerate(((first, gate_pre), (later, up_pre))):
            for h in range(2):
                wait_all(copies[(t * 2 + k) * 2 + h])
                part = dot(second_ref[:, halves[h]], whole[t, halves[h], hidden])
                side = dot(cot_ref[:, halves[h]], whole[t, halves[h], down])
                target[...] = part if h == 0 else target[...] + part
                grad_inner[:, sides[k]] = side if h == 0 else grad_inner[:, sides[k]] + side

        def activate(i, carry, inner_ref=inner_ref, grads_ref=grads_ref):
            at = pl.ds(pl.multiple_of(i * tile, tile), tile)
            v, u, g = gate_pre[at, :], up_pre[at, :], grad_inner[at, :]
            square = v * v
            bent = jnp.tanh(scale * v * (1.0 + 0.044715 * square))
            shared = 0.5 * (1.0 + bent)
            gelu = v * shared
            slope = shared + (0.5 * scale) * v * (1.0 - bent * bent) * (1.0 + 0.134145 * square)
            inner_ref[at, :] = (gelu * u).astype(low)
            grads_ref[at, hidden] = (g * u * slope).astype(low)
            grads_ref[at, hidden_up] = (g * gelu).astype(low)
            return carry

        lax.fori_loop(0, rows // tile, activate, 0)
        for half in halves:
            grad = dot(grads_ref[:, hidden], first[t, half, hidden], 1, 1)
            grad = grad + dot(grads_ref[:, hidden_up], later[t, half, hidden], 1, 1)
            down_part = dot(inner_ref[:, sides[0]], first[t, half, down], 1, 1)
            down_part = down_part + dot(inner_ref[:, sides[1]], later[t, half, down], 1, 1)
            if t > 0:
                grad = grad + sums[0, :, half]
                down_part = down_part + sums[1, :, half]
            elif has_prior:
                grad = grad + prior_grad[:, half]
                down_part = down_part + prior_down[:, half]
            if t < quarters - 1:
                sums[0, :, half] = grad
                sums[1, :, half] = down_part
            else:
                grad_ref[:, half] = grad.astype(grad_ref.dtype)
                down_part_ref[:, half] = down_part.astype(down_part_ref.dtype)


def feed_part(second, cot, gathers, quarter, prior, kind):
    top = gathers[0].top
    quarters = len(gathers)
    rows, depth = second.shape
    pieces, places, sizes = [], [], []
    for gather in gathers:
        operands, where = gather.refs()
        pieces += operands
        places.append(where)
        sizes.append(len(operands))
    width = pieces[0].shape[1]
    vmem = pl.BlockSpec(memory_space=pltpu.VMEM)
    out = jax.ShapeDtypeStruct((rows, depth), kind)
    hidden = [
        jax.ShapeDtypeStruct((rows, quarter), low),
        jax.ShapeDtypeStruct((rows, 2 * quarter), low),
    ]
    return pl.pallas_call(
        functools.partial(feed_kernel, top, quarter, places, sizes, bool(prior)),
        in_specs=[vmem] * 2
        + [pl.BlockSpec(memory_space=pl.ANY)] * len(pieces)
        + [vmem] * len(prior),
        out_specs=[vmem] * (2 * quarters + 2),
        out_shape=hidden * quarters + [out, out],
        scratch_shapes=[
            pltpu.VMEM((quarters, depth, width), low),
            pltpu.VMEM((quarters, depth, width), low),
            pltpu.VMEM((rows, quarter), wide),
            pltpu.VMEM((rows, quarter), wide),
            pltpu.VMEM((rows, quarter), wide),
            pltpu.VMEM((2, rows, depth), wide),
            pltpu.SemaphoreType.DMA((4 * top * quarters,)),
        ],
        compiler_params=pltpu.CompilerParams(vmem_limit_bytes=(22 + 12 * quarters) * 2**20),
        cost_estimate=brief,
    )(second, cot, *pieces, *prior)


def outer_kernel(count, added, rows, bits, *refs):
    lefts, rights, refs = refs[:count], refs[count : 2 * count], refs[2 * count :]
    got = refs[0] if added else None
    outs, flipped = refs[added:-1], refs[-1]
    turn = pl.program_id(0)
    starts = [sum(ref.shape[0] for ref in lefts[:i]) for i in range(count)]

    @pl.when(turn == 0)
    def _():
        for begin, ref in zip(starts, lefts):
            flipped[:, pl.ds(begin, ref.shape[0])] = ref[...].T

    total = 0.0
    for begin, ref in zip(starts, rights):
        total = total + dot(flipped[:, pl.ds(begin, ref.shape[0])], ref[...])
    if added:
        total = total + got[...].astype(wide)
    if bits is None:
        outs[0][...] = total.astype(low)
    else:
        for k in range(2):

            @pl.when(turn // (pl.num_programs(0) // 2) == k)
            def _(k=k):
                taken = [0, 0]
                for i, side in enumerate(bits[k]):
                    place = pl.ds(taken[side] * rows, rows)
                    outs[2 * k + side][place, :] = total[i * rows : (i + 1) * rows].astype(low)
                    taken[side] += 1


def outer_half(lefts, rights, part, got=None, rows=None, bits=None):
    depth = lefts[0].shape[1] // 2
    columns = rights[0].shape[1]
    block = 512 if columns % 1024 == 0 else 256
    blocks = columns // block
    whole = pl.BlockSpec((depth, block), lambda j: (0, j))
    extra = [] if got is None else [got]
    if bits is None:
        out_specs, out_shape = [whole], [jax.ShapeDtypeStruct((depth, columns), low)]
    else:
        early = pl.BlockSpec((depth // 2, block), lambda j: (0, jnp.minimum(j, blocks // 2 - 1)))
        late = pl.BlockSpec((depth // 2, block), lambda j: (0, jnp.maximum(j - blocks // 2, 0)))
        out_specs = [early, early, late, late]
        out_shape = [jax.ShapeDtypeStruct((depth // 2, columns // 2), low)] * 4
    result = call(
        functools.partial(outer_kernel, len(lefts), len(extra), rows, bits),
        (blocks,),
        in_specs=[pl.BlockSpec((v.shape[0], depth), lambda j: (0, part)) for v in lefts]
        + [pl.BlockSpec((v.shape[0], block), lambda j: (0, j)) for v in rights]
        + [whole] * len(extra),
        out_specs=out_specs,
        out_shape=out_shape,
        scratch_shapes=[pltpu.VMEM((depth, sum(v.shape[0] for v in lefts)), low)],
    )(*lefts, *rights, *extra)
    return result[0] if bits is None else list(result)


def rows_kernel(parts, sides, sums, size, begin_ref, *refs):
    lefts = [refs[p * sides : (p + 1) * sides] for p in range(parts)]
    refs = refs[parts * sides :]
    xhats, weights, out_ref = refs[: parts * sums], refs[parts * sums :][:sides], refs[parts * sums + sides]
    for p in range(parts):
        part = dot(lefts[p][0][...], weights[0][...], 1, 1)
        for k in range(1, sides):
            part = part + dot(lefts[p][k][...], weights[k][...], 1, 1)
        out_ref[pl.ds(p * size, size), :] = part.astype(out_ref.dtype)
        if sums:
            sums_ref = refs[-1]
            gain = jnp.sum(part * xhats[p][...].astype(wide), axis=0, keepdims=True)
            shift = jnp.sum(part, axis=0, keepdims=True)
            sums_ref[0:1, :] = gain if p == 0 else sums_ref[0:1, :] + gain
            sums_ref[1:2, :] = shift if p == 0 else sums_ref[1:2, :] + shift


def rows_back(lefts, weights, begins, size, xhat=None):
    depth = weights[0][0].shape[0]
    block = 512
    parts, sides = len(begins), len(lefts)
    in_specs, operands = [], []
    for p in range(parts):
        for (left, column), (_, _, columns) in zip(lefts, weights):
            in_specs.append(pl.BlockSpec((size, columns), lambda j, b, p=p, column=column: (b[p], column)))
            operands.append(left)
    if xhat is not None:
        for p in range(parts):
            in_specs.append(pl.BlockSpec((size, block), lambda j, b, p=p: (b[p], j)))
            operands.append(xhat)
    for weight, column, columns in weights:
        in_specs.append(pl.BlockSpec((block, columns), lambda j, b, column=column: (j, column)))
        operands.append(weight)
    out_specs = [pl.BlockSpec((parts * size, block), lambda j, b: (0, j))]
    out_shape = [jax.ShapeDtypeStruct((parts * size, depth), low)]
    if xhat is not None:
        out_specs.append(pl.BlockSpec((2, block), lambda j, b: (0, j)))
        out_shape.append(jax.ShapeDtypeStruct((2, depth), wide))
    return pl.pallas_call(
        functools.partial(rows_kernel, parts, sides, int(xhat is not None), size),
        grid_spec=pltpu.PrefetchScalarGridSpec(
            num_scalar_prefetch=1, grid=(depth // block,), in_specs=in_specs, out_specs=out_specs
        ),
        out_shape=out_shape,
        compiler_params=pltpu.CompilerParams(vmem_limit_bytes=56 * 2**20),
        cost_estimate=brief,
    )(jnp.stack(begins) // size, *operands)


def parts_of(heads):
    values = [pl.ds(h * VD, VD) for h in range(heads)]
    keys = [pl.ds(heads * VD + h * KD, KD) for h in range(heads)]
    return values, keys


def state_halves(state, heads, refs):
    if heads == 2:
        for h in range(2):
            refs[h][...] = state[h].astype(low)
    else:
        for k in range(2):
            refs[k][...] = state[0, pl.ds(k * KD // 2, KD // 2), :].astype(low)


def state_kernel(heads, chunks, rate_ref, kv_ref, one_ref, two_ref, state):
    values, keys = parts_of(heads)
    turn = pl.program_id(0)

    @pl.when(turn == 0)
    def _():
        state[...] = jnp.zeros_like(state)

    for h in range(heads):
        rate = rate_ref[h]
        scaled = (kv_ref[:, keys[h]].astype(wide) * tail_of(rate)).astype(low)
        kept = state[h] * jnp.exp(jnp.full((1, 1), rate * CHUNK, wide))
        state[h] = kept + dot(scaled, kv_ref[:, values[h]], 0, 0)

    @pl.when(turn == chunks - 1)
    def _():
        state_halves(state, heads, [one_ref, two_ref])


def final_state(kv, log_rate, heads):
    length, columns = kv.shape
    chunks = length // CHUNK
    half = jax.ShapeDtypeStruct((heads * KD // 2, VD), low)
    return call(
        functools.partial(state_kernel, heads, chunks),
        (chunks,),
        in_specs=[smem, pl.BlockSpec((CHUNK, columns), lambda c: (c, 0))],
        out_specs=[pl.BlockSpec(half.shape, lambda c: (0, 0))] * 2,
        out_shape=[half, half],
        scratch_shapes=[pltpu.VMEM((heads, KD, VD), wide)],
    )(log_rate, kv)


def retain_kernel(
    heads, rate_ref, kv_ref, qs_ref, first_ref, gated_ref, grouped_ref, factor_ref, states_ref, held, table
):
    values, keys = parts_of(heads)

    @pl.when(pl.program_id(0) == 0)
    def _():
        held[...] = first_ref[...]
        for h in range(heads):
            table[h] = decay_of(rate_ref[h])

    for h in range(heads):
        rate = rate_ref[h]
        query, key = qs_ref[:, keys[h]], kv_ref[:, keys[h]]
        value = kv_ref[:, values[h]]
        state = held[h]
        state_low = state.astype(low)
        states_ref[0, h] = state_low
        mixing = (dot(query, key, 1, 1) * table[h]).astype(low)
        retained = dot(mixing, value) + reach_of(rate) * dot(query, state_low)
        scaled = (key.astype(wide) * tail_of(rate)).astype(low)
        held[h] = state * jnp.exp(jnp.full((1, 1), rate * CHUNK, wide)) + dot(scaled, value, 0, 0)
        factor = lax.rsqrt(jnp.mean(retained * retained, axis=1, keepdims=True) + eps_group)
        grouped = (retained * factor).astype(low)
        factor_ref[h] = factor
        grouped_ref[:, values[h]] = grouped
        pre = qs_ref[:, values[h]].astype(wide)
        gated_ref[:, values[h]] = (grouped.astype(wide) * (pre * jax.nn.sigmoid(pre))).astype(low)


def retain(kv, qs, first, log_rate, heads):
    length, columns = kv.shape
    chunks = length // CHUNK
    rows = pl.BlockSpec((CHUNK, columns), lambda c: (c, 0))
    out = pl.BlockSpec((CHUNK, heads * VD), lambda c: (c, 0))
    return call(
        functools.partial(retain_kernel, heads),
        (chunks,),
        in_specs=[smem, rows, rows, pl.BlockSpec((heads, KD, VD), lambda c: (0, 0, 0))],
        out_specs=[
            out,
            out,
            pl.BlockSpec((heads, CHUNK, 1), lambda c: (0, c, 0)),
            pl.BlockSpec((1, heads, KD, VD), lambda c: (c, 0, 0, 0)),
        ],
        out_shape=[
            jax.ShapeDtypeStruct((length, heads * VD), low),
            jax.ShapeDtypeStruct((length, heads * VD), low),
            jax.ShapeDtypeStruct((heads, length, 1), wide),
            jax.ShapeDtypeStruct((chunks, heads, KD, VD), low),
        ],
        scratch_shapes=[pltpu.VMEM((heads, KD, VD), wide), pltpu.VMEM((heads, CHUNK, CHUNK), wide)],
    )(log_rate, kv, qs, first)


def gate_back_kernel(
    heads, first, last, place_ref, rate_ref, branch_ref, left_ref, right_ref, grouped_ref, factor_ref, qs_ref, *refs
):
    values, keys = parts_of(heads)
    if not first:
        _, _, prior_ref, *refs = refs
    swish_ref, retained_ref, *halves, crossed_ref = refs
    start = (place_ref[0] * CHUNK).astype(wide)
    sides = [dot(branch_ref[...], ref[...]) for ref in (left_ref, right_ref)]
    gated = sides if heads == 2 else [jnp.concatenate(sides, axis=1)]
    for h in range(heads):
        rate = rate_ref[h]
        gated_grad = gated[h]
        grouped = grouped_ref[:, values[h]].astype(wide)
        pre = qs_ref[:, values[h]].astype(wide)
        sigma = jax.nn.sigmoid(pre)
        swish_ref[:, values[h]] = (
            gated_grad * grouped * (sigma * (1.0 + pre * (1.0 - sigma)))
        ).astype(low)
        grouped_grad = (gated_grad * (pre * sigma)).astype(low).astype(wide)
        factor = factor_ref[h]
        mean = jnp.mean(grouped_grad * grouped, axis=1, keepdims=True)
        retained_grad = (factor * (grouped_grad - grouped * mean)).astype(low)
        retained_ref[:, values[h]] = retained_grad
        scale = reach_of(rate) * jnp.exp(jnp.full((1, 1), rate * start, wide))
        scaled = (qs_ref[:, keys[h]].astype(wide) * scale).astype(low)
        crossed = dot(scaled, retained_grad, 0, 0)
        crossed_ref[h] = crossed if first else prior_ref[h] + crossed
    if last:
        state_halves(crossed_ref, heads, halves)


def gate_back(branch, left, right, column, grouped, factor, qs, log_rate, heads, place, prior, last):
    length, columns = qs.shape
    depth = branch.shape[1]
    part = pl.BlockSpec((CHUNK, heads * VD), lambda i, p: (p[0], 0))
    total = pl.BlockSpec((heads, KD, VD), lambda i, p: (0, 0, 0))
    whole = pl.BlockSpec(memory_space=pl.ANY)
    half = pl.BlockSpec((heads * KD // 2, VD), lambda i, p: (0, 0))
    grid_spec = pltpu.PrefetchScalarGridSpec(
        num_scalar_prefetch=1,
        grid=(1,),
        in_specs=[
            smem,
            pl.BlockSpec((CHUNK, depth), lambda i, p: (0, 0)),
            pl.BlockSpec((depth, heads * VD // 2), lambda i, p: (0, column)),
            pl.BlockSpec((depth, heads * VD // 2), lambda i, p: (0, column)),
            part,
            pl.BlockSpec((heads, CHUNK, 1), lambda i, p: (0, p[0], 0)),
            pl.BlockSpec((CHUNK, columns), lambda i, p: (p[0], 0)),
        ]
        + [whole, whole, total][: len(prior)],
        out_specs=[part, part] + ([half] * 2 if last else [total]),
        scratch_shapes=[pltpu.VMEM((heads, KD, VD), wide)] if last else [],
    )
    return pl.pallas_call(
        functools.partial(gate_back_kernel, heads, not prior, last),
        grid_spec=grid_spec,
        out_shape=[
            jax.ShapeDtypeStruct((length, heads * VD), low),
            jax.ShapeDtypeStruct((length, heads * VD), low),
        ]
        + (
            [jax.ShapeDtypeStruct((heads * KD // 2, VD), low)] * 2
            if last
            else [jax.ShapeDtypeStruct((heads, KD, VD), wide)]
        ),
        input_output_aliases={8: 0, 9: 1} if prior else {},
        compiler_params=pltpu.CompilerParams(vmem_limit_bytes=56 * 2**20),
        cost_estimate=brief,
    )(place.reshape(1), log_rate, branch, left, right, grouped, factor, qs, *prior)


def retain_back_kernel(
    heads, rate_ref, kv_ref, qs_ref, grad_ref, states_ref, last_ref, back_ref, held, table
):
    values, keys = parts_of(heads)
    queries = [pl.ds(heads * (VD + KD) + h * KD, KD) for h in range(heads)]

    @pl.when(pl.program_id(0) == 0)
    def _():
        held[...] = last_ref[...]
        for h in range(heads):
            table[h] = decay_of(rate_ref[h])

    for h in range(heads):
        rate = rate_ref[h]
        query, key = qs_ref[:, keys[h]], kv_ref[:, keys[h]]
        value, grad = kv_ref[:, values[h]], grad_ref[:, values[h]]
        decay = table[h]
        reach, tail = reach_of(rate), tail_of(rate)
        later = held[h]
        later_low = later.astype(low)
        mixing = (dot(query, key, 1, 1) * decay).astype(low)
        scores_grad = (dot(grad, value, 1, 1) * decay).astype(low)
        back_ref[:, queries[h]] = (
            dot(scores_grad, key) + reach * dot(grad, states_ref[0, h], 1, 1)
        ).astype(low)
        back_ref[:, keys[h]] = (
            dot(scores_grad, query, 0, 0) + tail * dot(value, later_low, 1, 1)
        ).astype(low)
        back_ref[:, values[h]] = (
            dot(mixing, grad, 0, 0) + tail * dot(key, later_low)
        ).astype(low)
        scaled = (query.astype(wide) * reach).astype(low)
        held[h] = later * jnp.exp(jnp.full((1, 1), rate * CHUNK, wide)) + dot(scaled, grad, 0, 0)


def retain_back(kv, qs, retained_grad, states, last, log_rate, heads):
    length, columns = kv.shape
    chunks = length // CHUNK
    rows = pl.BlockSpec((CHUNK, columns), lambda c: (chunks - 1 - c, 0))
    part = pl.BlockSpec((CHUNK, heads * VD), lambda c: (chunks - 1 - c, 0))
    return call(
        functools.partial(retain_back_kernel, heads),
        (chunks,),
        in_specs=[
            smem,
            rows,
            rows,
            part,
            pl.BlockSpec((1, heads, KD, VD), lambda c: (chunks - 1 - c, 0, 0, 0)),
            pl.BlockSpec((heads, KD, VD), lambda c: (0, 0, 0)),
        ],
        out_specs=pl.BlockSpec((CHUNK, columns + heads * KD), lambda c: (chunks - 1 - c, 0)),
        out_shape=jax.ShapeDtypeStruct((length, columns + heads * KD), low),
        scratch_shapes=[pltpu.VMEM((heads, KD, VD), wide), pltpu.VMEM((heads, CHUNK, CHUNK), wide)],
    )(log_rate, kv, qs, retained_grad, states, last)


def shards(
    layer_in,
    norm1_gain,
    norm1_bias,
    w_query,
    w_key,
    w_value,
    w_swish,
    w_out,
    norm2_gain,
    norm2_bias,
    w_gate,
    w_up,
    w_down,
    cotangent,
):
    count_sq = lax.axis_size("sq")
    count_head = lax.axis_size("head")
    sq_index = lax.axis_index("sq")
    head_index = lax.axis_index("head")
    own_rows = layer_in.shape[0]
    length = own_rows * count_head
    key_scale = KD ** (-0.5)
    value_width = w_value.shape[1]
    depth = layer_in.shape[1]
    heads = value_width // VD
    log_rate = log_decay(head_index * heads, heads)
    order = jnp.stack([sq_index ^ mask_of(s, count_sq) for s in range(count_sq)]).astype(jnp.int32)
    start = [lax.rem(head_index - t + count_head, count_head) * own_rows for t in range(count_head)]
    kin_steps = []
    while 2 << len(kin_steps) < count_head:
        kin_steps.append(2 << len(kin_steps))

    key_width = w_key.shape[1]
    pair_width = value_width + key_width

    norm = Small(jnp.stack([norm1_gain, norm1_bias, norm2_gain, norm2_bias]))
    out_shard = w_out.T
    out_half = out_shard.shape[1] // 2
    first = Gather(
        jnp.concatenate(
            [w_value, (w_key.astype(wide) * key_scale).astype(low), out_shard[:, :out_half]], axis=1
        ),
        jnp.concatenate([w_swish, w_query, out_shard[:, out_half:]], axis=1),
    )
    quarter_width = w_gate.shape[1]
    middle = quarter_width // 2
    down_shard = w_down.T
    feed_first = Box(jnp.concatenate([w_gate, down_shard[:, :middle]], axis=1))
    feed_later = Box(jnp.concatenate([w_up, down_shard[:, middle:]], axis=1))
    cot_own = Box(own_order(cotangent))
    x_own = Box(own_order(layer_in))
    slots = [Box(layer_in)]
    settle(slots[0], first, norm)
    for turn in range(1, count_head):
        slots.append(Box(ring_step(slots[-1].value)))
        first.core()
        first.send()
        norm.send()
        settle(slots[-1], first, norm, feed_first, feed_later, cot_own, x_own)
    norm.rest()
    first.rest()
    first.core()

    def kin(value):
        held = [value]
        for step in kin_steps:
            held += [swap_head(v, step) for v in held]
        return held

    x_own = x_own.value
    kin_parts = [
        Box(feed_first.value[:, :quarter_width]),
        Box(feed_later.value[:, :quarter_width]),
        Box(jnp.concatenate([v.value[:, quarter_width:] for v in (feed_first, feed_later)], axis=1)),
    ]
    packs = [Many(*kin(kin_parts[0].value)[1:])]
    cot_far = Box(swap_head(cot_own.value, 1))
    feeds = [Gather(feed_first.value, feed_later.value)]
    feeds[0].send()
    norms = jnp.concatenate([norm.pieces[s] for s in range(count_sq)], axis=1).astype(wide)
    gain_one, shift_one, gain_two, shift_two = norms[0], norms[1], norms[2], norms[3]
    normed, xhat, kv, first_full = norm_project(
        [b.value for b in slots],
        norms,
        first,
        pair_width,
        order,
        jnp.stack(start).astype(jnp.int32),
    )
    passed = Gather(*final_state(kv, log_rate, heads))
    settle(passed, *packs, cot_far, feeds[0], cot_own, *kin_parts[1:])

    passed.send()
    packs.append(Many(*kin(kin_parts[1].value)[1:]))
    settle(passed)
    passed.rest()
    qs, later_full = project_pieces(normed, first, pair_width)
    qs = Box(qs)
    settle(passed, packs[1], cot_far, feeds[0], cot_own, kin_parts[2], qs)
    qs, cot_own = qs.value, cot_own.value
    passed.core()
    packs.append(Many(*kin(kin_parts[2].value)[1:]))
    feeds[0].core()
    feeds[0].send()
    incoming = combine(passed, log_rate, length, False)
    gated_low, grouped, factor, states = retain(kv, qs, incoming, log_rate, heads)

    out_column = pair_width // out_half

    def out_part(turns):
        (parts,) = rows_back(
            [(gated_low, 0), (gated_low, 1)],
            [(first_full, out_column, out_half), (later_full, out_column, out_half)],
            [start[turn % count_head] for turn in turns],
            own_rows,
        )
        return parts

    total = Box(out_part([1]))
    gated = Box(gated_low)
    settle(total, feeds[0], packs[2], gated)
    gated_low = gated.value
    quarters = 1 + len(packs[0].value)
    parts = Box(out_part(range(2, count_head + 1)))
    for turn in range(2, count_head + 1):
        got = ring_step(total.value)
        feeds[0].core()
        if turn == 2:
            feeds[0].send()
            feeds += [
                Gather(
                    jnp.concatenate([gate, down[:, :middle]], axis=1),
                    jnp.concatenate([up, down[:, middle:]], axis=1),
                )
                for gate, up, down in zip(*[p.value for p in packs])
            ]
        else:
            for thing in feeds[1:]:
                thing.core()
                thing.send()
        total = Box(add_rows(parts.value, turn - 2, got, low if turn < count_head else wide))
        settle(total, *feeds, parts)
    hidden = x_own.astype(wide) + total.value
    second_own = Box(layer_norm(hidden, gain_two, shift_two).astype(low))

    settle(second_own, *feeds)
    second_own = second_own.value
    second_far = Box(swap_head(second_own, 1))
    for thing in feeds:
        thing.core()
        thing.rest()
    feeds[0].core()
    fed = feed_part(second_own, cot_own, feeds[:1], quarter_width, [], wide)
    inner_own, grads_own, fed_sums = [fed[0]], [fed[1]], Many(*fed[2:])
    settle(second_far, *feeds[1:], cot_far, fed_sums)
    second_far, cot_far = second_far.value, cot_far.value
    for thing in feeds[1:]:
        thing.core()
    fed = feed_part(second_far, cot_far, feeds, quarter_width, [], low)
    inner_far, grads_far = fed[: 2 * quarters : 2], fed[1 : 2 * quarters : 2]
    grad_far, down_far, near = Box(fed[-2]), Box(fed[-1]), Box(second_own)
    settle(grad_far, near, down_far)

    grad_far = Box(swap_head(grad_far.value, 1))
    fed = feed_part(near.value, cot_own, feeds[1:], quarter_width, fed_sums.value, wide)
    inner_own += fed[: 2 * quarters - 2 : 2]
    grads_own += fed[1 : 2 * quarters - 2 : 2]
    second = Many(near.value, second_far)
    cot = Many(cot_own, cot_far)
    inner = Many(beside(inner_own), beside(inner_far))
    grads = [Many(a, b) for a, b in zip(grads_own, grads_far)]
    early_sum = Scatter(second.value, grads[0].value)
    early_sum.core()
    early_sum.near()
    late_sums = [Scatter(second.value, g.value) for g in grads[1:]]
    settle(grad_far, early_sum, *late_sums, cot, inner)
    second_grad = fed[-2] + grad_far.value.astype(wide)
    _, second_back = jax.vjp(layer_norm, hidden, gain_two, shift_two)
    hidden_part, gain_two_part, shift_two_part = second_back(second_grad)
    grad_hidden = cot_own.astype(wide) + hidden_part

    slots = [Box(grad_hidden.astype(low))]
    settle(slots[0], early_sum, *late_sums, cot, inner)
    passing = []
    for turn in range(count_head):
        rows = slots[-1]
        if turn < count_head - 1:
            slots.append(Box(ring_step(rows.value)))
        if turn == 0:
            early_sum.send(True)
            for thing in late_sums:
                thing.core()
                thing.near()
            down_sum = Scatter(cot.value, inner.value)
            waits = [early_sum, *late_sums, down_sum]
        elif turn == 1:
            for thing in late_sums:
                thing.send()
            down_sum.core()
            down_sum.near()
        elif turn == 2:
            for thing in late_sums:
                thing.rest()
            down_sum.send()
        passing = gate_back(
            rows.value,
            first_full,
            later_full,
            out_column,
            grouped,
            factor,
            qs,
            log_rate,
            heads,
            start[turn] // own_rows,
            passing,
            turn == count_head - 1,
        )
        if turn < count_head - 1:
            passing = Many(*passing)
            settle(slots[-1], *waits, cot, inner, passing)
            passing = passing.value
    swish_grad, retained_grad, *crossed = passing

    def kin_sum(held):
        parts = []
        held = [None] + list(held)
        for step in kin_steps[::-1]:
            size = len(held) // 2
            got = [swap_head(h, step) for h in held[size:]]
            parts.append(got[0])
            held = [None] + [
                (h.astype(wide) + g.astype(wide)).astype(low) for h, g in zip(held[1:size], got[1:])
            ]
        return parts

    branch_low = jnp.zeros((length, depth), low)
    for turn, rows in enumerate(slots):
        branch_low = lax.dynamic_update_slice_in_dim(branch_low, rows.value, start[turn], 0)
    branch, gated = Box(branch_low), Box(gated_low)
    ups = [thing.rest()[1].astype(low) for thing in late_sums]
    early = [
        Many(
            *kin_sum(
                [
                    jnp.concatenate([thing.rest()[0].astype(low), up[:, :middle]], axis=1)
                    for thing, up in zip(late_sums, ups)
                ]
            )
        )
    ]
    ups = Many(*[up[:, middle:] for up in ups])
    passed = Gather(*crossed)
    swish = Box(swish_grad)
    settle(passed, early_sum, down_sum, ups, branch, gated, swish)
    passed.send()
    settle(passed, down_sum, ups, swish)
    passed.rest()
    down_sum.rest()
    swish_sum = Scatter([normed], [swish.value])
    settle(passed, early[0], early_sum, down_sum, ups, swish_sum)
    passed.core()
    down_parts = jnp.split(jnp.concatenate(down_sum.rest(), axis=1), quarters, axis=1)
    early.append(
        Many(
            *kin_sum(
                [
                    jnp.concatenate([up, part.astype(low)], axis=1)
                    for up, part in zip(ups.value, down_parts[1:])
                ]
            )
        )
    )
    early_sum.send(True)
    swish_sum.core()
    returned = combine(passed, log_rate, length, True)
    backs = retain_back(kv, qs, retained_grad, states, returned, log_rate, heads)

    def normed_part(turns, backs):
        query = 2 + value_width // key_width - 1
        return rows_back(
            [(backs, 0), (swish_grad, 0), (backs, query)],
            [
                (first_full, 0, pair_width),
                (later_full, 0, value_width),
                (later_full, query - 1, key_width),
            ],
            [start[turn % count_head] for turn in turns],
            own_rows,
            xhat,
        )

    total, norm_sums = normed_part([1], backs)
    total, backs, norm_sums = Box(total), Box(backs), Box(norm_sums)
    settle(total, early_sum, swish_sum, backs, norm_sums, branch, gated, down_far, early[1])
    parts, more_sums = normed_part(range(2, count_head + 1), backs.value)
    parts = Box(parts)
    more_sums = Box(more_sums)
    waits = [early_sum]
    for turn in range(2, count_head + 1):
        got = ring_step(total.value)
        if turn == 2:
            early_sum.rest()
            swish_sum.near()
            swish_sum.send(True)
            back_sum = Scatter([normed], [backs.value])
            back_sum.core()
            back_sum.near()
            waits = [early_sum, swish_sum, back_sum, more_sums]
        elif turn == 3:
            back_sum.send()
            out_sum = Scatter([branch.value], [gated.value])
            out_sum.core()
            out_sum.near()
            waits = [swish_sum, back_sum, out_sum, more_sums]
        elif turn == 4:
            back_sum.rest()
            swish_sum.rest()
            norm_sums = norm_sums.value + more_sums.value
            norm_sums = true_order(
                jnp.concatenate([norm_sums, jnp.stack([gain_two_part, shift_two_part])])
            )
            norm_sums = Box(sum_others(norm_sums, "sq", [1]))
            waits = [back_sum, swish_sum, out_sum, norm_sums]
        total = Box(add_rows(parts.value, turn - 2, got, low if turn < count_head else wide))
        settle(total, *waits, parts, branch, gated, down_far)
    down_far = swap_head(down_far.value, 1)
    _, first_back = jax.vjp(lambda v: layer_norm(v, gain_one, shift_one), x_own.astype(wide))
    grad_in = grad_hidden + first_back(total.value)[0]
    norm_sums = sum_others(norm_sums.value, "sq", range(2, count_sq, 2))
    norm_sums = sum_others(norm_sums, "head", range(1, count_head))
    first_sum, later_sum = early_sum.rest()
    early = [sum(p.astype(wide) for p in e.value) for e in early]
    grad_gate = first_sum + early[0][:, :quarter_width]
    grad_up = later_sum + jnp.concatenate(
        [early[0][:, quarter_width:], early[1][:, :middle]], axis=1
    )
    grad_down = (down_parts[0] + early[1][:, middle:]).T
    grad_value, grad_key_query = back_sum.rest()
    grad_swish = jnp.concatenate(swish_sum.rest(), axis=1)
    grad_out = jnp.concatenate(out_sum.rest(), axis=1).T
    result = (hidden + fed[-1] + down_far.astype(wide)).astype(low)

    piece = depth // (count_sq * count_head)
    first_norm = lax.dynamic_slice_in_dim(
        norm_sums[:2], (head_index * count_sq + sq_index) * piece, piece, 1
    )
    piece = depth // count_sq
    second_norm = lax.dynamic_slice_in_dim(norm_sums[2:], sq_index * piece, piece, 1)
    return (
        true_order(result),
        true_order(grad_in),
        first_norm[0],
        first_norm[1],
        grad_key_query[:, key_width:],
        grad_key_query[:, :key_width] * key_scale,
        grad_value,
        grad_swish,
        grad_out,
        second_norm[0],
        second_norm[1],
        grad_gate,
        grad_up,
        grad_down,
    )


def solution(mesh):
    return jax.shard_map(
        shards,
        mesh=mesh,
        in_specs=(
            P(("sq", "head"), None),
            P("sq"),
            P("sq"),
            P("sq", "head"),
            P("sq", "head"),
            P("sq", "head"),
            P("sq", "head"),
            P("head", "sq"),
            P("sq"),
            P("sq"),
            P("sq", "head"),
            P("sq", "head"),
            P("head", "sq"),
            P(("sq", "head"), None),
        ),
        out_specs=(
            P(("sq", "head"), None),
            P(("sq", "head"), None),
            P(("head", "sq")),
            P(("head", "sq")),
            P("sq", "head"),
            P("sq", "head"),
            P("sq", "head"),
            P("sq", "head"),
            P("head", "sq"),
            P("sq"),
            P("sq"),
            P("sq", "head"),
            P("sq", "head"),
            P("head", "sq"),
        ),
        check_vma=False,
    )
```

```python
import functools

import jax
import jax.numpy as jnp
from jax import lax
from jax.experimental import pallas as pl
from jax.experimental.pallas import tpu as pltpu
from jax.sharding import PartitionSpec as P

KD = 256
VD = 512
CHUNK = 256


eps_layer = 1e-05
eps_group = 1e-06
low = jnp.bfloat16
wide = jnp.float32


def mask_of(slot, count):
    bits = count.bit_length() - 1
    return ((slot << 1) & (count - 1)) | (slot >> (bits - 1))


def slot_of(mask, count):
    bits = count.bit_length() - 1
    return (mask >> 1) | ((mask & 1) << (bits - 1))


def flip(value, mask):
    count = lax.axis_size("sq")
    return lax.ppermute(value, "sq", [(i, i ^ mask) for i in range(count)])


def route(swapped):
    count = lax.axis_size("sq")
    lower = list(range(count.bit_length() - 2))
    return lower[::-1] if swapped else lower


def own_order(values):
    count = lax.axis_size("sq")
    width = values.shape[-1] // count
    place = lax.axis_index("sq")
    return jnp.concatenate(
        [
            lax.dynamic_slice_in_dim(values, (place ^ mask_of(s, count)) * width, width, -1)
            for s in range(count)
        ],
        axis=-1,
    )


def true_order(values):
    count = lax.axis_size("sq")
    width = values.shape[-1] // count
    place = lax.axis_index("sq")
    return jnp.concatenate(
        [
            lax.dynamic_slice_in_dim(values, slot_of(place ^ b, count) * width, width, -1)
            for b in range(count)
        ],
        axis=-1,
    )


class Box:
    def __init__(self, value):
        self.value = value

    def get(self):
        return [self.value]

    def put(self, values):
        (self.value,) = values


class Many:
    def __init__(self, *values):
        self.value = list(values)

    def get(self):
        return self.value

    def put(self, values):
        self.value = list(values)


class Gather:
    def __init__(self, *shards):
        self.count = lax.axis_size("sq")
        self.top = self.count // 2
        self.pieces = [{0: shard} for shard in shards]
        self.far = []
        self.todo = []
        for swapped in (False, True):
            slots, units = [0], []
            for bit in route(swapped):
                units += [(s, bit) for s in slots]
                slots += [s | 1 << bit for s in slots]
            self.todo.append(units)

    def send(self, times=1):
        for k, held in enumerate(self.pieces):
            for slot, bit in self.todo[k][:times]:
                held[slot | 1 << bit] = flip(held[slot], mask_of(1 << bit, self.count))
            self.todo[k] = self.todo[k][times:]

    def rest(self):
        self.send(len(self.todo[0]))

    def rest_grouped(self):
        for k, held in enumerate(self.pieces):
            while self.todo[k]:
                bit = self.todo[k][0][1]
                slots = [s for s, b in self.todo[k] if b == bit]
                self.todo[k] = self.todo[k][len(slots) :]
                got = flip(stack([held[s] for s in slots]), mask_of(1 << bit, self.count))
                for i, slot in enumerate(slots):
                    held[slot | 1 << bit] = got[i]

    def core(self):
        sent = [s for slots, _ in self.far for s in slots]
        ready = [s for s in range(self.top) if s not in sent and all(s in h for h in self.pieces)]
        if ready:
            both = stack([held[s] for s in ready for held in self.pieces])
            self.far.append((ready, flip(both, mask_of(self.top, self.count))))

    def refs(self):
        operands = [held[s] for held in self.pieces for s in range(self.top)]
        places = [[(k * self.top + s, None) for s in range(self.top)] for k in range(2)]
        for k in range(2):
            for s in range(self.top):
                for g, (slots, _) in enumerate(self.far):
                    if s in slots:
                        places[k].append((2 * self.top + g, 2 * slots.index(s) + k))
        return operands + [array for _, array in self.far], places

    def get(self):
        near = [held[s] for held in self.pieces for s in sorted(held)]
        return near + [array for _, array in self.far]

    def put(self, values):
        values = iter(values)
        self.pieces = [{s: next(values) for s in sorted(held)} for held in self.pieces]
        self.far = [(slots, next(values)) for slots, _ in self.far]


class Small:
    def __init__(self, shard):
        self.count = lax.axis_size("sq")
        self.pieces = {0: shard}
        bits = self.count.bit_length() - 1
        self.todo = [bits - 1, *range(bits - 1)]

    def send(self):
        if self.todo:
            bit, self.todo = self.todo[0], self.todo[1:]
            slots = sorted(self.pieces)
            far = flip(jnp.stack([self.pieces[s] for s in slots]), mask_of(1 << bit, self.count))
            for k, s in enumerate(slots):
                self.pieces[s | 1 << bit] = far[k]

    def rest(self):
        while self.todo:
            self.send()

    def get(self):
        return [self.pieces[s] for s in sorted(self.pieces)]

    def put(self, values):
        self.pieces = dict(zip(sorted(self.pieces), values))


class Scatter:
    def __init__(self, lefts, rights):
        self.count = lax.axis_size("sq")
        top = self.count // 2
        self.rows = lefts[0].shape[1] // self.count
        self.todo = [route(k == 1)[::-1] for k in range(2)]
        self.slots = [list(range(top)) for _ in range(2)]
        self.arrived = False
        self.sources = lefts, rights
        self.held = [outer_half(lefts, rights, 1)]

    def core(self):
        self.held = [flip(self.held[0], mask_of(self.count // 2, self.count))]

    def near(self):
        self.held = outer_half(*self.sources, 0, self.held[0], self.rows, self.part())

    def part(self):
        return [[s >> self.todo[k][0] & 1 for s in self.slots[k]] for k in range(2)]

    def send(self, lazy=False):
        self.merge()
        for k in range(2):
            bit, self.todo[k] = self.todo[k][0], self.todo[k][1:]
            self.held[2 * k + 1] = flip(self.held[2 * k + 1], mask_of(1 << bit, self.count))
            self.slots[k] = [s for s in self.slots[k] if not s >> bit & 1]
        self.arrived = True
        if not lazy:
            self.merge()

    def merge(self):
        if self.arrived:
            bits = self.part() if self.todo[0] else None
            self.held = list(split(self.held[::2], self.held[1::2], self.rows, bits))
            self.arrived = False

    def rest(self):
        self.merge()
        while self.todo[0]:
            self.send()
        return self.held

    def get(self):
        return list(self.held)

    def put(self, values):
        self.held = list(values)


def send_together(*sums):
    wanted = {}
    for thing in sums:
        thing.merge()
        for k in range(2):
            wanted.setdefault(thing.todo[k][0], []).append((thing, k))
    for bit, group in wanted.items():
        parts = [thing.held[2 * k + 1] for thing, k in group]
        got = flip(above(parts) if len(parts) > 1 else parts[0], mask_of(1 << bit, sums[0].count))
        begin = 0
        for (thing, k), part in zip(group, parts):
            thing.held[2 * k + 1] = got[begin : begin + part.shape[0]]
            begin += part.shape[0]
            thing.todo[k] = thing.todo[k][1:]
            thing.slots[k] = [s for s in thing.slots[k] if not s >> bit & 1]
    for thing in sums:
        thing.arrived = True
        thing.merge()


def settle(*things):
    values = lax.optimization_barrier(tuple(v for t in things for v in t.get()))
    values = list(values)
    for thing in things:
        size = len(thing.get())
        thing.put(values[:size])
        values = values[size:]


def ring_step(value):
    count = lax.axis_size("head")
    return lax.ppermute(value, "head", [(i, (i + 1) % count) for i in range(count)])


def sum_others(values, axis, masks):
    count = lax.axis_size(axis)
    held = [values]
    held += [lax.ppermute(values, axis, [(i, i ^ m) for i in range(count)]) for m in masks]
    while len(held) > 1:
        held = [a + b for a, b in zip(held[::2], held[1::2])]
    return held[0]


def layer_norm(values, weight_gain, weight_shift):
    centered = values - jnp.mean(values, axis=-1, keepdims=True)
    spread = lax.rsqrt(jnp.mean(centered * centered, axis=-1, keepdims=True) + eps_layer)
    return centered * spread * weight_gain + weight_shift


def gelu_gate(pre_gate, pre_up):
    return jax.nn.gelu(pre_gate) * pre_up


def log_decay(first_head, head_count):
    head_ids = (first_head + jnp.arange(head_count)).astype(jnp.float32)
    return jnp.log(1.0 - jnp.exp2(-5.0 - head_ids))


def project(left_side, right_side):
    return jnp.dot(left_side, right_side, preferred_element_type=jnp.float32)


def outer_sum(left_side, right_side):
    return lax.dot_general(
        left_side, right_side, (((0,), (0,)), ((), ())), preferred_element_type=jnp.float32
    )


def back_project(gradient, weight):
    return lax.dot_general(
        gradient, weight, (((1,), (1,)), ((), ())), preferred_element_type=jnp.float32
    )


def swap_head(value, mask):
    count = lax.axis_size("head")
    return lax.ppermute(value, "head", [(i, i ^ mask) for i in range(count)])


def stack_kernel(*refs):
    for k, ref in enumerate(refs[:-1]):
        refs[-1][k] = ref[...]


def stack(pieces):
    vmem = pl.BlockSpec(memory_space=pltpu.VMEM)
    return pl.pallas_call(
        stack_kernel,
        in_specs=[vmem] * len(pieces),
        out_specs=vmem,
        out_shape=jax.ShapeDtypeStruct((len(pieces),) + pieces[0].shape, pieces[0].dtype),
        compiler_params=pltpu.CompilerParams(vmem_limit_bytes=16 * 2**20),
        cost_estimate=brief,
    )(*pieces)


def beside_kernel(*refs):
    begin = 0
    for ref in refs[:-1]:
        refs[-1][:, pl.ds(begin, ref.shape[1])] = ref[...]
        begin += ref.shape[1]


def beside(pieces):
    vmem = pl.BlockSpec(memory_space=pltpu.VMEM)
    columns = sum(p.shape[1] for p in pieces)
    return pl.pallas_call(
        beside_kernel,
        in_specs=[vmem] * len(pieces),
        out_specs=vmem,
        out_shape=jax.ShapeDtypeStruct((pieces[0].shape[0], columns), pieces[0].dtype),
        compiler_params=pltpu.CompilerParams(vmem_limit_bytes=16 * 2**20),
        cost_estimate=brief,
    )(*pieces)


def above_kernel(*refs):
    begin = 0
    for ref in refs[:-1]:
        refs[-1][pl.ds(begin, ref.shape[0]), :] = ref[...]
        begin += ref.shape[0]


def above(pieces):
    vmem = pl.BlockSpec(memory_space=pltpu.VMEM)
    rows = sum(p.shape[0] for p in pieces)
    return pl.pallas_call(
        above_kernel,
        in_specs=[vmem] * len(pieces),
        out_specs=vmem,
        out_shape=jax.ShapeDtypeStruct((rows, pieces[0].shape[1]), pieces[0].dtype),
        compiler_params=pltpu.CompilerParams(vmem_limit_bytes=16 * 2**20),
        cost_estimate=brief,
    )(*pieces)


def add_rows_kernel(whole_ref, got_ref, out_ref):
    total = whole_ref[...].astype(wide) + got_ref[...].astype(wide)
    out_ref[...] = total.astype(out_ref.dtype)


def add_rows(whole, place, got, kind):
    rows, columns = got.shape
    block = min(columns, 1024)
    part = pl.BlockSpec((rows, block), lambda j: (0, j))
    return call(
        add_rows_kernel,
        (columns // block,),
        in_specs=[pl.BlockSpec((rows, block), lambda j: (place, j)), part],
        out_specs=part,
        out_shape=jax.ShapeDtypeStruct(got.shape, kind),
    )(whole, got)


def split_kernel(rows, bits, *refs):
    ins, outs = refs[:4], refs[4:]
    for k in range(2):
        kept, got = ins[2 * k : 2 * k + 2]
        total = kept[...].astype(wide) + got[...].astype(wide)
        if bits is None:
            outs[k][...] = total
        else:
            taken = [0, 0]
            for i, side in enumerate(bits[k]):
                place = pl.ds(taken[side] * rows, rows)
                outs[2 * k + side][place, :] = total[i * rows : (i + 1) * rows].astype(low)
                taken[side] += 1


def split(kept, got, rows, bits):
    size, columns = kept[0].shape
    block = 512 if columns % 512 == 0 else 256
    part = pl.BlockSpec((size, block), lambda j: (0, j))
    half = pl.BlockSpec((size // 2, block), lambda j: (0, j))
    if bits is None:
        out_specs = [part] * 2
        out_shape = [jax.ShapeDtypeStruct((size, columns), wide)] * 2
    else:
        out_specs = [half] * 4
        out_shape = [jax.ShapeDtypeStruct((size // 2, columns), low)] * 4
    return call(
        functools.partial(split_kernel, rows, bits),
        (columns // block,),
        in_specs=[part] * 4,
        out_specs=out_specs,
        out_shape=out_shape,
    )(kept[0], got[0], kept[1], got[1])


def combine_kernel(heads, places, factor_ref, *refs):
    *piece_refs, total_ref = refs
    size = heads * KD // 2
    for part in range(2):
        for begin in range(0, size, KD // 2):
            h, row = divmod(part * size + begin, KD)
            rows = pl.ds(begin, KD // 2)
            total = jnp.zeros((KD // 2, VD), wide)
            for k, (operand, index) in enumerate(places[part][1:]):
                ref = piece_refs[operand]
                piece = ref[rows, :] if index is None else ref[index, rows, :]
                total = total + factor_ref[k * heads + h] * piece.astype(wide)
            total_ref[h, pl.ds(row, KD // 2), :] = total


def combine(gather, log_rate, length, backward):
    count = lax.axis_size("sq")
    place = lax.axis_index("sq")
    heads = log_rate.shape[0]
    factors = []
    for slot in range(1, count):
        other = place ^ mask_of(slot, count)
        ahead = (other - place) if backward else (place - other)
        between = jnp.maximum(ahead - 1, 0).astype(wide) * length
        factors.append(jnp.where(ahead > 0, jnp.exp(log_rate * between), 0.0))
    operands, places = gather.refs()
    vmem = pl.BlockSpec(memory_space=pltpu.VMEM)
    return pl.pallas_call(
        functools.partial(combine_kernel, heads, places),
        in_specs=[smem] + [vmem] * len(operands),
        out_specs=vmem,
        out_shape=jax.ShapeDtypeStruct((heads, KD, VD), wide),
        compiler_params=pltpu.CompilerParams(vmem_limit_bytes=56 * 2**20),
        cost_estimate=brief,
    )(jnp.concatenate(factors), *operands)


def call(kernel, grid, **options):
    return pl.pallas_call(
        kernel,
        grid=grid,
        cost_estimate=brief,
        compiler_params=pltpu.CompilerParams(
            dimension_semantics=("arbitrary",) * len(grid), vmem_limit_bytes=20 * 2**20
        ),
        **options,
    )


def dot(left_side, right_side, left_dim=1, right_dim=0):
    return lax.dot_general(
        left_side,
        right_side,
        (((left_dim,), (right_dim,)), ((), ())),
        preferred_element_type=wide,
    )


smem = pl.BlockSpec(memory_space=pltpu.SMEM)


def reach_of(rate):
    place = lax.broadcasted_iota(jnp.int32, (CHUNK, 1), 0).astype(wide)
    return jnp.exp(rate * (place + 1.0))


def tail_of(rate):
    place = lax.broadcasted_iota(jnp.int32, (CHUNK, 1), 0).astype(wide)
    return jnp.exp(rate * (CHUNK - 1.0 - place))


def decay_of(rate):
    row = lax.broadcasted_iota(jnp.int32, (CHUNK, CHUNK), 0)
    column = lax.broadcasted_iota(jnp.int32, (CHUNK, CHUNK), 1)
    spacing = (row - column).astype(wide)
    return jnp.where(spacing >= 0, jnp.exp(rate * jnp.maximum(spacing, 0.0)), 0.0)


brief = pl.CostEstimate(flops=1, bytes_accessed=1, transcendentals=0)


def bring(copies):
    for copy in copies:
        copy.start()
    return copies


def bring_pieces(refs, places, whole, sems, first):
    rows = whole.shape[0] // len(places)
    return bring(
        [
            pltpu.make_async_copy(
                refs[operand] if index is None else refs[operand].at[index],
                whole.at[pl.ds(k * rows, rows), :],
                sems.at[first + k],
            )
            for k, (operand, index) in enumerate(places)
        ]
    )


def wait_all(copies):
    for copy in copies:
        copy.wait()


def project_blocks(left, weight, product_ref):
    block = 256

    def one(j, carry):
        columns = pl.ds(pl.multiple_of(j * block, block), block)
        product_ref[:, columns] = dot(left[...], weight[:, columns]).astype(low)
        return carry

    lax.fori_loop(0, product_ref.shape[1] // block, one, 0)


def norm_project_kernel(count, slots, places, order, start, *refs):
    row_refs = refs[:slots]
    norm_ref = refs[slots]
    piece_refs = refs[slots + 1 : -8]
    normed_ref, xhat_ref, product_ref, full_ref, weight, normed, xhat, sems = refs[-8:]
    width = normed.shape[1] // count
    size = row_refs[0].shape[0]
    tile = 64
    copies = bring_pieces(piece_refs, places, weight, sems, 0)
    for turn, ref in enumerate(row_refs):

        def tile_of(t, carry, ref=ref, turn=turn):
            rows = pl.ds(pl.multiple_of(t * tile, tile), tile)
            values = [
                ref[rows, pl.ds(pl.multiple_of(order[s] * width, width), width)].astype(wide)
                for s in range(count)
            ]
            total = values[0]
            for v in values[1:]:
                total = total + v
            mean = jnp.sum(total, axis=1, keepdims=True) / (count * width)
            values = [v - mean for v in values]
            square = values[0] * values[0]
            for v in values[1:]:
                square = square + v * v
            square = jnp.sum(square, axis=1, keepdims=True)
            spread = lax.rsqrt(square / (count * width) + eps_layer)
            target = pl.ds(pl.multiple_of(start[turn] + t * tile, tile), tile)
            for s in range(count):
                columns = pl.ds(s * width, width)
                scaled = values[s] * spread
                xhat[target, columns] = scaled.astype(low)
                normed[target, columns] = (
                    scaled * norm_ref[0:1, columns] + norm_ref[1:2, columns]
                ).astype(low)
            return carry

        lax.fori_loop(0, size // tile, tile_of, 0)

    away = bring(
        [
            pltpu.make_async_copy(normed, normed_ref, sems.at[count]),
            pltpu.make_async_copy(xhat, xhat_ref, sems.at[count + 1]),
        ]
    )
    wait_all(copies)
    away += bring([pltpu.make_async_copy(weight, full_ref, sems.at[count + 2])])
    project_blocks(normed, weight, product_ref)
    wait_all(away)


def norm_project(slots, norms, gather, columns, order, start):
    count = gather.count
    pieces, places = gather.refs()
    size, depth = slots[0].shape
    length = size * len(slots)
    width = pieces[0].shape[1]
    vmem = pl.BlockSpec(memory_space=pltpu.VMEM)
    whole = pl.BlockSpec(memory_space=pl.ANY)
    return pl.pallas_call(
        functools.partial(norm_project_kernel, count, len(slots), places[0]),
        in_specs=[smem, smem] + [vmem] * (len(slots) + 1) + [whole] * len(pieces),
        out_specs=[whole, whole, vmem, whole],
        out_shape=[
            jax.ShapeDtypeStruct((length, depth), low),
            jax.ShapeDtypeStruct((length, depth), low),
            jax.ShapeDtypeStruct((length, columns), low),
            jax.ShapeDtypeStruct((depth, width), low),
        ],
        scratch_shapes=[
            pltpu.VMEM((depth, width), low),
            pltpu.VMEM((length, depth), low),
            pltpu.VMEM((length, depth), low),
            pltpu.SemaphoreType.DMA((count + 3,)),
        ],
        compiler_params=pltpu.CompilerParams(vmem_limit_bytes=36 * 2**20),
        cost_estimate=brief,
    )(order, start, *slots, norms, *pieces)


def project_kernel(count, places, left_ref, *refs):
    product_ref, full_ref, weight, sems = refs[-4:]
    wait_all(bring_pieces(refs[:-4], places, weight, sems, 0))
    away = bring([pltpu.make_async_copy(weight, full_ref, sems.at[count])])
    project_blocks(left_ref, weight, product_ref)
    wait_all(away)


def project_pieces(left_side, gather, columns):
    length, depth = left_side.shape
    count = gather.count
    pieces, places = gather.refs()
    width = pieces[0].shape[1]
    vmem = pl.BlockSpec(memory_space=pltpu.VMEM)
    whole = pl.BlockSpec(memory_space=pl.ANY)
    return pl.pallas_call(
        functools.partial(project_kernel, count, places[1]),
        in_specs=[vmem] + [whole] * len(pieces),
        out_specs=[vmem, whole],
        out_shape=[
            jax.ShapeDtypeStruct((length, columns), low),
            jax.ShapeDtypeStruct((depth, width), low),
        ],
        scratch_shapes=[pltpu.VMEM((depth, width), low), pltpu.SemaphoreType.DMA((count + 1,))],
        compiler_params=pltpu.CompilerParams(vmem_limit_bytes=20 * 2**20),
        cost_estimate=brief,
    )(left_side, *pieces)


def feed_kernel(top, quarter, places, sizes, has_prior, second_ref, cot_ref, *refs):
    quarters = len(places)
    piece_refs = []
    for size in sizes:
        piece_refs.append(refs[:size])
        refs = refs[size:]
    if has_prior:
        prior_grad, prior_down, *refs = refs
    hidden_refs = [refs[2 * t : 2 * t + 2] for t in range(quarters)]
    grad_ref, down_part_ref = refs[2 * quarters : 2 * quarters + 2]
    first, later, gate_pre, up_pre, grad_inner, sums, sems = refs[2 * quarters + 2 :]
    rows, depth = second_ref.shape
    middle = quarter // 2
    hidden = pl.ds(0, quarter)
    hidden_up = pl.ds(quarter, quarter)
    down = pl.ds(quarter, middle)
    sides = [pl.ds(0, middle), pl.ds(middle, middle)]
    halves = [pl.ds(0, depth // 2), pl.ds(depth // 2, depth // 2)]
    copies = []
    for t in range(quarters):
        for k, whole in enumerate((first, later)):
            index = (t * 2 + k) * 2 * top
            some = bring_pieces(piece_refs[t], places[t][k], whole.at[t], sems, index)
            copies += [some[:top], some[top:]]
    tile = 16
    scale = 0.7978845608028654
    for t in range(quarters):
        inner_ref, grads_ref = hidden_refs[t]
        for k, (whole, target) in enumerate(((first, gate_pre), (later, up_pre))):
            for h in range(2):
                wait_all(copies[(t * 2 + k) * 2 + h])
                part = dot(second_ref[:, halves[h]], whole[t, halves[h], hidden])
                side = dot(cot_ref[:, halves[h]], whole[t, halves[h], down])
                target[...] = part if h == 0 else target[...] + part
                grad_inner[:, sides[k]] = side if h == 0 else grad_inner[:, sides[k]] + side

        def activate(i, carry, inner_ref=inner_ref, grads_ref=grads_ref):
            at = pl.ds(pl.multiple_of(i * tile, tile), tile)
            v, u, g = gate_pre[at, :], up_pre[at, :], grad_inner[at, :]
            square = v * v
            bent = jnp.tanh(scale * v * (1.0 + 0.044715 * square))
            shared = 0.5 * (1.0 + bent)
            gelu = v * shared
            slope = shared + (0.5 * scale) * v * (1.0 - bent * bent) * (1.0 + 0.134145 * square)
            inner_ref[at, :] = (gelu * u).astype(low)
            grads_ref[at, hidden] = (g * u * slope).astype(low)
            grads_ref[at, hidden_up] = (g * gelu).astype(low)
            return carry

        lax.fori_loop(0, rows // tile, activate, 0)
        for half in halves:
            grad = dot(grads_ref[:, hidden], first[t, half, hidden], 1, 1)
            grad = grad + dot(grads_ref[:, hidden_up], later[t, half, hidden], 1, 1)
            down_part = dot(inner_ref[:, sides[0]], first[t, half, down], 1, 1)
            down_part = down_part + dot(inner_ref[:, sides[1]], later[t, half, down], 1, 1)
            if t > 0:
                grad = grad + sums[0, :, half]
                down_part = down_part + sums[1, :, half]
            elif has_prior:
                grad = grad + prior_grad[:, half]
                down_part = down_part + prior_down[:, half]
            if t < quarters - 1:
                sums[0, :, half] = grad
                sums[1, :, half] = down_part
            else:
                grad_ref[:, half] = grad.astype(grad_ref.dtype)
                down_part_ref[:, half] = down_part.astype(down_part_ref.dtype)


def feed_part(second, cot, gathers, quarter, prior, kind):
    top = gathers[0].top
    quarters = len(gathers)
    rows, depth = second.shape
    pieces, places, sizes = [], [], []
    for gather in gathers:
        operands, where = gather.refs()
        pieces += operands
        places.append(where)
        sizes.append(len(operands))
    width = pieces[0].shape[1]
    vmem = pl.BlockSpec(memory_space=pltpu.VMEM)
    out = jax.ShapeDtypeStruct((rows, depth), kind)
    hidden = [
        jax.ShapeDtypeStruct((rows, quarter), low),
        jax.ShapeDtypeStruct((rows, 2 * quarter), low),
    ]
    return pl.pallas_call(
        functools.partial(feed_kernel, top, quarter, places, sizes, bool(prior)),
        in_specs=[vmem] * 2
        + [pl.BlockSpec(memory_space=pl.ANY)] * len(pieces)
        + [vmem] * len(prior),
        out_specs=[vmem] * (2 * quarters + 2),
        out_shape=hidden * quarters + [out, out],
        scratch_shapes=[
            pltpu.VMEM((quarters, depth, width), low),
            pltpu.VMEM((quarters, depth, width), low),
            pltpu.VMEM((rows, quarter), wide),
            pltpu.VMEM((rows, quarter), wide),
            pltpu.VMEM((rows, quarter), wide),
            pltpu.VMEM((2, rows, depth), wide),
            pltpu.SemaphoreType.DMA((4 * top * quarters,)),
        ],
        compiler_params=pltpu.CompilerParams(vmem_limit_bytes=(22 + 12 * quarters) * 2**20),
        cost_estimate=brief,
    )(second, cot, *pieces, *prior)


def outer_kernel(count, added, rows, bits, *refs):
    lefts, rights, refs = refs[:count], refs[count : 2 * count], refs[2 * count :]
    got = refs[0] if added else None
    outs, flipped = refs[added:-1], refs[-1]
    turn = pl.program_id(0)
    starts = [sum(ref.shape[0] for ref in lefts[:i]) for i in range(count)]

    @pl.when(turn == 0)
    def _():
        for begin, ref in zip(starts, lefts):
            flipped[:, pl.ds(begin, ref.shape[0])] = ref[...].T

    total = 0.0
    for begin, ref in zip(starts, rights):
        total = total + dot(flipped[:, pl.ds(begin, ref.shape[0])], ref[...])
    if added:
        total = total + got[...].astype(wide)
    if bits is None:
        outs[0][...] = total.astype(low)
    else:
        for k in range(2):

            @pl.when(turn // (pl.num_programs(0) // 2) == k)
            def _(k=k):
                taken = [0, 0]
                for i, side in enumerate(bits[k]):
                    place = pl.ds(taken[side] * rows, rows)
                    outs[2 * k + side][place, :] = total[i * rows : (i + 1) * rows].astype(low)
                    taken[side] += 1


def outer_half(lefts, rights, part, got=None, rows=None, bits=None):
    depth = lefts[0].shape[1] // 2
    columns = rights[0].shape[1]
    block = 512 if columns % 1024 == 0 else 256
    blocks = columns // block
    whole = pl.BlockSpec((depth, block), lambda j: (0, j))
    extra = [] if got is None else [got]
    if bits is None:
        out_specs, out_shape = [whole], [jax.ShapeDtypeStruct((depth, columns), low)]
    else:
        early = pl.BlockSpec((depth // 2, block), lambda j: (0, jnp.minimum(j, blocks // 2 - 1)))
        late = pl.BlockSpec((depth // 2, block), lambda j: (0, jnp.maximum(j - blocks // 2, 0)))
        out_specs = [early, early, late, late]
        out_shape = [jax.ShapeDtypeStruct((depth // 2, columns // 2), low)] * 4
    result = call(
        functools.partial(outer_kernel, len(lefts), len(extra), rows, bits),
        (blocks,),
        in_specs=[pl.BlockSpec((v.shape[0], depth), lambda j: (0, part)) for v in lefts]
        + [pl.BlockSpec((v.shape[0], block), lambda j: (0, j)) for v in rights]
        + [whole] * len(extra),
        out_specs=out_specs,
        out_shape=out_shape,
        scratch_shapes=[pltpu.VMEM((depth, sum(v.shape[0] for v in lefts)), low)],
    )(*lefts, *rights, *extra)
    return result[0] if bits is None else list(result)


def rows_kernel(parts, sides, sums, size, begin_ref, *refs):
    lefts = [refs[p * sides : (p + 1) * sides] for p in range(parts)]
    refs = refs[parts * sides :]
    xhats, weights, out_ref = refs[: parts * sums], refs[parts * sums :][:sides], refs[parts * sums + sides]
    for p in range(parts):
        part = dot(lefts[p][0][...], weights[0][...], 1, 1)
        for k in range(1, sides):
            part = part + dot(lefts[p][k][...], weights[k][...], 1, 1)
        out_ref[pl.ds(p * size, size), :] = part.astype(out_ref.dtype)
        if sums:
            sums_ref = refs[-1]
            gain = jnp.sum(part * xhats[p][...].astype(wide), axis=0, keepdims=True)
            shift = jnp.sum(part, axis=0, keepdims=True)
            sums_ref[0:1, :] = gain if p == 0 else sums_ref[0:1, :] + gain
            sums_ref[1:2, :] = shift if p == 0 else sums_ref[1:2, :] + shift


def rows_back(lefts, weights, begins, size, xhat=None):
    depth = weights[0][0].shape[0]
    block = 512
    parts, sides = len(begins), len(lefts)
    in_specs, operands = [], []
    for p in range(parts):
        for (left, column), (_, _, columns) in zip(lefts, weights):
            in_specs.append(pl.BlockSpec((size, columns), lambda j, b, p=p, column=column: (b[p], column)))
            operands.append(left)
    if xhat is not None:
        for p in range(parts):
            in_specs.append(pl.BlockSpec((size, block), lambda j, b, p=p: (b[p], j)))
            operands.append(xhat)
    for weight, column, columns in weights:
        in_specs.append(pl.BlockSpec((block, columns), lambda j, b, column=column: (j, column)))
        operands.append(weight)
    out_specs = [pl.BlockSpec((parts * size, block), lambda j, b: (0, j))]
    out_shape = [jax.ShapeDtypeStruct((parts * size, depth), low)]
    if xhat is not None:
        out_specs.append(pl.BlockSpec((2, block), lambda j, b: (0, j)))
        out_shape.append(jax.ShapeDtypeStruct((2, depth), wide))
    return pl.pallas_call(
        functools.partial(rows_kernel, parts, sides, int(xhat is not None), size),
        grid_spec=pltpu.PrefetchScalarGridSpec(
            num_scalar_prefetch=1, grid=(depth // block,), in_specs=in_specs, out_specs=out_specs
        ),
        out_shape=out_shape,
        compiler_params=pltpu.CompilerParams(vmem_limit_bytes=56 * 2**20),
        cost_estimate=brief,
    )(jnp.stack(begins) // size, *operands)


def parts_of(heads):
    values = [pl.ds(h * VD, VD) for h in range(heads)]
    keys = [pl.ds(heads * VD + h * KD, KD) for h in range(heads)]
    return values, keys


def state_halves(state, heads, refs):
    if heads == 2:
        for h in range(2):
            refs[h][...] = state[h].astype(low)
    else:
        for k in range(2):
            refs[k][...] = state[0, pl.ds(k * KD // 2, KD // 2), :].astype(low)


def state_kernel(heads, chunks, rate_ref, kv_ref, one_ref, two_ref, state):
    values, keys = parts_of(heads)
    turn = pl.program_id(0)

    @pl.when(turn == 0)
    def _():
        state[...] = jnp.zeros_like(state)

    for h in range(heads):
        rate = rate_ref[h]
        scaled = (kv_ref[:, keys[h]].astype(wide) * tail_of(rate)).astype(low)
        kept = state[h] * jnp.exp(jnp.full((1, 1), rate * CHUNK, wide))
        state[h] = kept + dot(scaled, kv_ref[:, values[h]], 0, 0)

    @pl.when(turn == chunks - 1)
    def _():
        state_halves(state, heads, [one_ref, two_ref])


def final_state(kv, log_rate, heads):
    length, columns = kv.shape
    chunks = length // CHUNK
    half = jax.ShapeDtypeStruct((heads * KD // 2, VD), low)
    return call(
        functools.partial(state_kernel, heads, chunks),
        (chunks,),
        in_specs=[smem, pl.BlockSpec((CHUNK, columns), lambda c: (c, 0))],
        out_specs=[pl.BlockSpec(half.shape, lambda c: (0, 0))] * 2,
        out_shape=[half, half],
        scratch_shapes=[pltpu.VMEM((heads, KD, VD), wide)],
    )(log_rate, kv)


def retain_kernel(
    heads, rate_ref, kv_ref, qs_ref, first_ref, gated_ref, grouped_ref, factor_ref, states_ref, held, table
):
    values, keys = parts_of(heads)

    @pl.when(pl.program_id(0) == 0)
    def _():
        held[...] = first_ref[...]
        for h in range(heads):
            table[h] = decay_of(rate_ref[h])

    for h in range(heads):
        rate = rate_ref[h]
        query, key = qs_ref[:, keys[h]], kv_ref[:, keys[h]]
        value = kv_ref[:, values[h]]
        state = held[h]
        state_low = state.astype(low)
        states_ref[0, h] = state_low
        mixing = (dot(query, key, 1, 1) * table[h]).astype(low)
        retained = dot(mixing, value) + reach_of(rate) * dot(query, state_low)
        scaled = (key.astype(wide) * tail_of(rate)).astype(low)
        held[h] = state * jnp.exp(jnp.full((1, 1), rate * CHUNK, wide)) + dot(scaled, value, 0, 0)
        factor = lax.rsqrt(jnp.mean(retained * retained, axis=1, keepdims=True) + eps_group)
        grouped = (retained * factor).astype(low)
        factor_ref[h] = factor
        grouped_ref[:, values[h]] = grouped
        pre = qs_ref[:, values[h]].astype(wide)
        gated_ref[:, values[h]] = (grouped.astype(wide) * (pre * jax.nn.sigmoid(pre))).astype(low)


def retain(kv, qs, first, log_rate, heads):
    length, columns = kv.shape
    chunks = length // CHUNK
    rows = pl.BlockSpec((CHUNK, columns), lambda c: (c, 0))
    out = pl.BlockSpec((CHUNK, heads * VD), lambda c: (c, 0))
    return call(
        functools.partial(retain_kernel, heads),
        (chunks,),
        in_specs=[smem, rows, rows, pl.BlockSpec((heads, KD, VD), lambda c: (0, 0, 0))],
        out_specs=[
            out,
            out,
            pl.BlockSpec((heads, CHUNK, 1), lambda c: (0, c, 0)),
            pl.BlockSpec((1, heads, KD, VD), lambda c: (c, 0, 0, 0)),
        ],
        out_shape=[
            jax.ShapeDtypeStruct((length, heads * VD), low),
            jax.ShapeDtypeStruct((length, heads * VD), low),
            jax.ShapeDtypeStruct((heads, length, 1), wide),
            jax.ShapeDtypeStruct((chunks, heads, KD, VD), low),
        ],
        scratch_shapes=[pltpu.VMEM((heads, KD, VD), wide), pltpu.VMEM((heads, CHUNK, CHUNK), wide)],
    )(log_rate, kv, qs, first)


def gate_back_kernel(
    heads, first, last, place_ref, rate_ref, branch_ref, left_ref, right_ref, grouped_ref, factor_ref, qs_ref, *refs
):
    values, keys = parts_of(heads)
    if not first:
        _, _, prior_ref, *refs = refs
    swish_ref, retained_ref, *halves, crossed_ref = refs
    start = (place_ref[0] * CHUNK).astype(wide)
    sides = [dot(branch_ref[...], ref[...]) for ref in (left_ref, right_ref)]
    gated = sides if heads == 2 else [jnp.concatenate(sides, axis=1)]
    for h in range(heads):
        rate = rate_ref[h]
        gated_grad = gated[h]
        grouped = grouped_ref[:, values[h]].astype(wide)
        pre = qs_ref[:, values[h]].astype(wide)
        sigma = jax.nn.sigmoid(pre)
        swish_ref[:, values[h]] = (
            gated_grad * grouped * (sigma * (1.0 + pre * (1.0 - sigma)))
        ).astype(low)
        grouped_grad = (gated_grad * (pre * sigma)).astype(low).astype(wide)
        factor = factor_ref[h]
        mean = jnp.mean(grouped_grad * grouped, axis=1, keepdims=True)
        retained_grad = (factor * (grouped_grad - grouped * mean)).astype(low)
        retained_ref[:, values[h]] = retained_grad
        scale = reach_of(rate) * jnp.exp(jnp.full((1, 1), rate * start, wide))
        scaled = (qs_ref[:, keys[h]].astype(wide) * scale).astype(low)
        crossed = dot(scaled, retained_grad, 0, 0)
        crossed_ref[h] = crossed if first else prior_ref[h] + crossed
    if last:
        state_halves(crossed_ref, heads, halves)


def gate_back(branch, left, right, column, grouped, factor, qs, log_rate, heads, place, prior, last):
    length, columns = qs.shape
    depth = branch.shape[1]
    part = pl.BlockSpec((CHUNK, heads * VD), lambda i, p: (p[0], 0))
    total = pl.BlockSpec((heads, KD, VD), lambda i, p: (0, 0, 0))
    whole = pl.BlockSpec(memory_space=pl.ANY)
    half = pl.BlockSpec((heads * KD // 2, VD), lambda i, p: (0, 0))
    grid_spec = pltpu.PrefetchScalarGridSpec(
        num_scalar_prefetch=1,
        grid=(1,),
        in_specs=[
            smem,
            pl.BlockSpec((CHUNK, depth), lambda i, p: (0, 0)),
            pl.BlockSpec((depth, heads * VD // 2), lambda i, p: (0, column)),
            pl.BlockSpec((depth, heads * VD // 2), lambda i, p: (0, column)),
            part,
            pl.BlockSpec((heads, CHUNK, 1), lambda i, p: (0, p[0], 0)),
            pl.BlockSpec((CHUNK, columns), lambda i, p: (p[0], 0)),
        ]
        + [whole, whole, total][: len(prior)],
        out_specs=[part, part] + ([half] * 2 if last else [total]),
        scratch_shapes=[pltpu.VMEM((heads, KD, VD), wide)] if last else [],
    )
    return pl.pallas_call(
        functools.partial(gate_back_kernel, heads, not prior, last),
        grid_spec=grid_spec,
        out_shape=[
            jax.ShapeDtypeStruct((length, heads * VD), low),
            jax.ShapeDtypeStruct((length, heads * VD), low),
        ]
        + (
            [jax.ShapeDtypeStruct((heads * KD // 2, VD), low)] * 2
            if last
            else [jax.ShapeDtypeStruct((heads, KD, VD), wide)]
        ),
        input_output_aliases={8: 0, 9: 1} if prior else {},
        compiler_params=pltpu.CompilerParams(vmem_limit_bytes=56 * 2**20),
        cost_estimate=brief,
    )(place.reshape(1), log_rate, branch, left, right, grouped, factor, qs, *prior)


def retain_back_kernel(
    heads, rate_ref, kv_ref, qs_ref, grad_ref, states_ref, last_ref, back_ref, held, table
):
    values, keys = parts_of(heads)
    queries = [pl.ds(heads * (VD + KD) + h * KD, KD) for h in range(heads)]

    @pl.when(pl.program_id(0) == 0)
    def _():
        held[...] = last_ref[...]
        for h in range(heads):
            table[h] = decay_of(rate_ref[h])

    for h in range(heads):
        rate = rate_ref[h]
        query, key = qs_ref[:, keys[h]], kv_ref[:, keys[h]]
        value, grad = kv_ref[:, values[h]], grad_ref[:, values[h]]
        decay = table[h]
        reach, tail = reach_of(rate), tail_of(rate)
        later = held[h]
        later_low = later.astype(low)
        mixing = (dot(query, key, 1, 1) * decay).astype(low)
        scores_grad = (dot(grad, value, 1, 1) * decay).astype(low)
        back_ref[:, queries[h]] = (
            dot(scores_grad, key) + reach * dot(grad, states_ref[0, h], 1, 1)
        ).astype(low)
        back_ref[:, keys[h]] = (
            dot(scores_grad, query, 0, 0) + tail * dot(value, later_low, 1, 1)
        ).astype(low)
        back_ref[:, values[h]] = (
            dot(mixing, grad, 0, 0) + tail * dot(key, later_low)
        ).astype(low)
        scaled = (query.astype(wide) * reach).astype(low)
        held[h] = later * jnp.exp(jnp.full((1, 1), rate * CHUNK, wide)) + dot(scaled, grad, 0, 0)


def retain_back(kv, qs, retained_grad, states, last, log_rate, heads):
    length, columns = kv.shape
    chunks = length // CHUNK
    rows = pl.BlockSpec((CHUNK, columns), lambda c: (chunks - 1 - c, 0))
    part = pl.BlockSpec((CHUNK, heads * VD), lambda c: (chunks - 1 - c, 0))
    return call(
        functools.partial(retain_back_kernel, heads),
        (chunks,),
        in_specs=[
            smem,
            rows,
            rows,
            part,
            pl.BlockSpec((1, heads, KD, VD), lambda c: (chunks - 1 - c, 0, 0, 0)),
            pl.BlockSpec((heads, KD, VD), lambda c: (0, 0, 0)),
        ],
        out_specs=pl.BlockSpec((CHUNK, columns + heads * KD), lambda c: (chunks - 1 - c, 0)),
        out_shape=jax.ShapeDtypeStruct((length, columns + heads * KD), low),
        scratch_shapes=[pltpu.VMEM((heads, KD, VD), wide), pltpu.VMEM((heads, CHUNK, CHUNK), wide)],
    )(log_rate, kv, qs, retained_grad, states, last)


def shards(
    layer_in,
    norm1_gain,
    norm1_bias,
    w_query,
    w_key,
    w_value,
    w_swish,
    w_out,
    norm2_gain,
    norm2_bias,
    w_gate,
    w_up,
    w_down,
    cotangent,
):
    count_sq = lax.axis_size("sq")
    count_head = lax.axis_size("head")
    sq_index = lax.axis_index("sq")
    head_index = lax.axis_index("head")
    own_rows = layer_in.shape[0]
    length = own_rows * count_head
    key_scale = KD ** (-0.5)
    value_width = w_value.shape[1]
    depth = layer_in.shape[1]
    heads = value_width // VD
    log_rate = log_decay(head_index * heads, heads)
    order = jnp.stack([sq_index ^ mask_of(s, count_sq) for s in range(count_sq)]).astype(jnp.int32)
    start = [lax.rem(head_index - t + count_head, count_head) * own_rows for t in range(count_head)]
    kin_steps = []
    while 2 << len(kin_steps) < count_head:
        kin_steps.append(2 << len(kin_steps))

    key_width = w_key.shape[1]
    pair_width = value_width + key_width

    norm = Small(jnp.stack([norm1_gain, norm1_bias, norm2_gain, norm2_bias]))
    out_shard = w_out.T
    out_half = out_shard.shape[1] // 2
    first = Gather(
        jnp.concatenate(
            [w_value, (w_key.astype(wide) * key_scale).astype(low), out_shard[:, :out_half]], axis=1
        ),
        jnp.concatenate([w_swish, w_query, out_shard[:, out_half:]], axis=1),
    )
    quarter_width = w_gate.shape[1]
    middle = quarter_width // 2
    down_shard = w_down.T
    feed_first = Box(jnp.concatenate([w_gate, down_shard[:, :middle]], axis=1))
    feed_later = Box(jnp.concatenate([w_up, down_shard[:, middle:]], axis=1))
    kin_parts = [
        Box(w_gate),
        Box(w_up),
        Box(down_shard),
    ]
    cot_own = Box(own_order(cotangent))
    x_own = Box(own_order(layer_in))
    slots = [Box(layer_in)]
    settle(slots[0], first, norm)
    for turn in range(1, count_head):
        slots.append(Box(ring_step(slots[-1].value)))
        first.core()
        first.send()
        norm.send()
        settle(slots[-1], first, norm, feed_first, feed_later, cot_own, x_own, *kin_parts)
    norm.rest()
    first.rest()
    first.core()

    def kin(value):
        held = [value]
        for step in kin_steps:
            held += [swap_head(v, step) for v in held]
        return held

    x_own = x_own.value
    packs = [Many(*kin(kin_parts[0].value)[1:])]
    cot_far = Box(swap_head(cot_own.value, 1))
    feeds = [Gather(feed_first.value, feed_later.value)]
    feeds[0].send()
    norms = jnp.concatenate([norm.pieces[s] for s in range(count_sq)], axis=1).astype(wide)
    gain_one, shift_one, gain_two, shift_two = norms[0], norms[1], norms[2], norms[3]
    normed, xhat, kv, first_full = norm_project(
        [b.value for b in slots],
        norms,
        first,
        pair_width,
        order,
        jnp.stack(start).astype(jnp.int32),
    )
    passed = Gather(*final_state(kv, log_rate, heads))
    settle(passed, *packs, cot_far, feeds[0], cot_own, *kin_parts[1:])

    passed.send()
    packs.append(Many(*kin(kin_parts[1].value)[1:]))
    settle(passed)
    passed.rest()
    qs, later_full = project_pieces(normed, first, pair_width)
    qs = Box(qs)
    settle(passed, packs[1], cot_far, feeds[0], cot_own, kin_parts[2], qs)
    qs, cot_own = qs.value, cot_own.value
    passed.core()
    packs.append(Many(*kin(kin_parts[2].value)[1:]))
    feeds[0].core()
    feeds[0].send()
    incoming = combine(passed, log_rate, length, False)
    gated_low, grouped, factor, states = retain(kv, qs, incoming, log_rate, heads)

    out_column = pair_width // out_half

    def out_part(turns):
        (parts,) = rows_back(
            [(gated_low, 0), (gated_low, 1)],
            [(first_full, out_column, out_half), (later_full, out_column, out_half)],
            [start[turn % count_head] for turn in turns],
            own_rows,
        )
        return parts

    total = Box(out_part([1]))
    gated = Box(gated_low)
    settle(packs[2], total, feeds[0], gated)
    gated_low = gated.value
    quarters = 1 + len(packs[0].value)
    parts = Box(out_part(range(2, count_head + 1)))
    for turn in range(2, count_head + 1):
        got = ring_step(total.value)
        feeds[0].core()
        if turn == 2:
            feeds[0].send()
            feeds += [
                Gather(
                    jnp.concatenate([gate, down[:, :middle]], axis=1),
                    jnp.concatenate([up, down[:, middle:]], axis=1),
                )
                for gate, up, down in zip(*[p.value for p in packs])
            ]
        else:
            for thing in feeds[1:]:
                thing.core()
                thing.send()
        total = Box(add_rows(parts.value, turn - 2, got, low if turn < count_head else wide))
        settle(total, *feeds, parts)
    hidden = x_own.astype(wide) + total.value
    second_own = Box(layer_norm(hidden, gain_two, shift_two).astype(low))

    settle(second_own, *feeds)
    second_own = second_own.value
    second_far = Box(swap_head(second_own, 1))
    for thing in feeds:
        thing.core()
        thing.rest()
    feeds[0].core()
    fed = feed_part(second_own, cot_own, feeds[:1], quarter_width, [], wide)
    inner_own, grads_own, fed_sums = [fed[0]], [fed[1]], Many(*fed[2:])
    settle(second_far, *feeds[1:], cot_far, fed_sums)
    second_far, cot_far = second_far.value, cot_far.value
    for thing in feeds[1:]:
        thing.core()
    fed = feed_part(second_far, cot_far, feeds, quarter_width, [], low)
    inner_far, grads_far = fed[: 2 * quarters : 2], fed[1 : 2 * quarters : 2]
    grad_far, down_far, near = Box(fed[-2]), Box(fed[-1]), Box(second_own)
    settle(grad_far, near, down_far)

    grad_far = Box(swap_head(grad_far.value, 1))
    fed = feed_part(near.value, cot_own, feeds[1:], quarter_width, fed_sums.value, wide)
    inner_own += fed[: 2 * quarters - 2 : 2]
    grads_own += fed[1 : 2 * quarters - 2 : 2]
    second = Many(near.value, second_far)
    cot = Many(cot_own, cot_far)
    inner = Many(beside(inner_own), beside(inner_far))
    grads = [Many(a, b) for a, b in zip(grads_own, grads_far)]
    late_sums = [Scatter(second.value, g.value) for g in grads[1:]]
    down_sum = Scatter(cot.value, inner.value)
    settle(grad_far, *late_sums, down_sum, second, grads[0], down_far)
    second_grad = fed[-2] + grad_far.value.astype(wide)
    _, second_back = jax.vjp(layer_norm, hidden, gain_two, shift_two)
    hidden_part, gain_two_part, shift_two_part = second_back(second_grad)
    grad_hidden = cot_own.astype(wide) + hidden_part

    slots = [Box(grad_hidden.astype(low))]
    settle(slots[0], *late_sums, down_sum, second, grads[0], down_far)
    waits = [*late_sums, down_sum, down_far]
    passing = []
    for turn in range(count_head):
        rows = slots[-1]
        if turn < count_head - 1:
            slots.append(Box(ring_step(rows.value)))
        if turn == 0:
            for thing in [*late_sums, down_sum]:
                thing.core()
                thing.near()
            early_sum = Scatter(second.value, grads[0].value)
            waits.append(early_sum)
        elif turn == 1:
            for thing in late_sums:
                thing.send()
            early_sum.core()
        elif turn == 2:
            send_together(down_sum, late_sums[0])
            for thing in late_sums:
                thing.rest()
            early_sum.near()
            down_far = Box(swap_head(down_far.value, 1))
            waits.append(down_far)
        passing = gate_back(
            rows.value,
            first_full,
            later_full,
            out_column,
            grouped,
            factor,
            qs,
            log_rate,
            heads,
            start[turn] // own_rows,
            passing,
            turn == count_head - 1,
        )
        if turn < count_head - 1:
            passing = Many(*passing)
            settle(slots[-1], *waits, passing)
            passing = passing.value
    swish_grad, retained_grad, *crossed = passing

    def kin_sum(held):
        parts = []
        held = [None] + list(held)
        for step in kin_steps[::-1]:
            size = len(held) // 2
            got = [swap_head(h, step) for h in held[size:]]
            parts.append(got[0])
            held = [None] + [
                (h.astype(wide) + g.astype(wide)).astype(low) for h, g in zip(held[1:size], got[1:])
            ]
        return parts

    branch_low = jnp.zeros((length, depth), low)
    for turn, rows in enumerate(slots):
        branch_low = lax.dynamic_update_slice_in_dim(branch_low, rows.value, start[turn], 0)
    branch, gated = Box(branch_low), Box(gated_low)
    cut = 3 * quarter_width // 4
    gates = [thing.rest()[0].astype(low) for thing in late_sums]
    ups = [thing.rest()[1].astype(low) for thing in late_sums]
    early = [Many(*kin_sum([gate[:, :cut] for gate in gates]))]
    kin_next = Many(
        *[beside([gate[:, cut:], up[:, :cut]]) for gate, up in zip(gates, ups)]
    )
    ups = Many(*[up[:, cut:] for up in ups])
    passed = Gather(*crossed)
    swish = Box(swish_grad)
    settle(passed, early_sum, down_sum, ups, kin_next, branch, gated, swish)
    passed.send()
    settle(passed, early[0], down_sum, ups, kin_next, swish, branch, gated)
    early.append(Many(*kin_sum(kin_next.value)))
    passed.rest_grouped()
    down_sum.rest()
    swish_sum = Scatter([normed], [swish.value])
    out_sum = Scatter([branch.value], [gated.value])
    settle(passed, early[1], early_sum, down_sum, ups, swish_sum, out_sum)
    passed.core()
    down_parts = jnp.split(jnp.concatenate(down_sum.rest(), axis=1), quarters, axis=1)
    early.append(
        Many(
            *kin_sum(
                [
                    beside([up, part.astype(low)])
                    for up, part in zip(ups.value, down_parts[1:])
                ]
            )
        )
    )
    early_sum.send(True)
    swish_sum.core()
    returned = combine(passed, log_rate, length, True)
    backs = retain_back(kv, qs, retained_grad, states, returned, log_rate, heads)

    def normed_part(turns, backs):
        query = 2 + value_width // key_width - 1
        return rows_back(
            [(backs, 0), (swish_grad, 0), (backs, query)],
            [
                (first_full, 0, pair_width),
                (later_full, 0, value_width),
                (later_full, query - 1, key_width),
            ],
            [start[turn % count_head] for turn in turns],
            own_rows,
            xhat,
        )

    total, norm_sums = normed_part([1], backs)
    total, backs, norm_sums = Box(total), Box(backs), Box(norm_sums)
    settle(total, early_sum, swish_sum, out_sum, backs, norm_sums, early[2])
    parts, more_sums = normed_part([2], backs.value)
    parts = [Box(parts)]
    norm_sums = Many(norm_sums.value, more_sums)
    for turn in range(2, count_head + 1):
        got = ring_step(total.value)
        if turn == 2:
            early_sum.rest()
            out_sum.core()
            swish_sum.near()
            back_sum = Scatter([normed], [backs.value])
            back_sum.core()
            back_sum.near()
            waits = [early_sum, swish_sum, back_sum, out_sum]
        elif turn == 3:
            back_sum.send()
            swish_sum.send(True)
            out_sum.near()
            later_parts, more_sums = normed_part(range(3, count_head + 1), backs.value)
            parts.append(Box(later_parts))
            norm_sums = Many(*norm_sums.value, more_sums)
            waits = [swish_sum, back_sum, out_sum]
        elif turn == 4:
            back_sum.rest()
            out_sum.send(True)
            norm_sums = true_order(
                jnp.concatenate(
                    [sum(norm_sums.value), jnp.stack([gain_two_part, shift_two_part])]
                )
            )
            norm_sums = Many(sum_others(norm_sums, "sq", [1]))
            waits = [back_sum, swish_sum, out_sum]
        part = (parts[0], 0) if turn == 2 else (parts[1], turn - 3)
        total = Box(
            add_rows(part[0].value, part[1], got, low if turn < count_head else wide)
        )
        settle(total, *waits, *parts, norm_sums, backs)
    _, first_back = jax.vjp(lambda v: layer_norm(v, gain_one, shift_one), x_own.astype(wide))
    grad_in = grad_hidden + first_back(total.value)[0]
    norm_sums = sum_others(norm_sums.value[0], "sq", range(2, count_sq, 2))
    norm_sums = sum_others(norm_sums, "head", range(1, count_head))
    first_sum, later_sum = early_sum.rest()
    early = [sum(p.astype(wide) for p in e.value) for e in early]
    early = jnp.concatenate(early, axis=1)
    grad_gate = first_sum + early[:, :quarter_width]
    grad_up = later_sum + early[:, quarter_width : 2 * quarter_width]
    grad_down = (down_parts[0] + early[:, 2 * quarter_width :]).T
    grad_value, grad_key_query = back_sum.rest()
    grad_swish = jnp.concatenate(swish_sum.rest(), axis=1)
    grad_out = jnp.concatenate(out_sum.rest(), axis=1).T
    result = (hidden + fed[-1] + down_far.value.astype(wide)).astype(low)

    piece = depth // (count_sq * count_head)
    first_norm = lax.dynamic_slice_in_dim(
        norm_sums[:2], (head_index * count_sq + sq_index) * piece, piece, 1
    )
    piece = depth // count_sq
    second_norm = lax.dynamic_slice_in_dim(norm_sums[2:], sq_index * piece, piece, 1)
    return (
        true_order(result),
        true_order(grad_in),
        first_norm[0],
        first_norm[1],
        grad_key_query[:, key_width:],
        grad_key_query[:, :key_width] * key_scale,
        grad_value,
        grad_swish,
        grad_out,
        second_norm[0],
        second_norm[1],
        grad_gate,
        grad_up,
        grad_down,
    )


def solution(mesh):
    return jax.shard_map(
        shards,
        mesh=mesh,
        in_specs=(
            P(("sq", "head"), None),
            P("sq"),
            P("sq"),
            P("sq", "head"),
            P("sq", "head"),
            P("sq", "head"),
            P("sq", "head"),
            P("head", "sq"),
            P("sq"),
            P("sq"),
            P("sq", "head"),
            P("sq", "head"),
            P("head", "sq"),
            P(("sq", "head"), None),
        ),
        out_specs=(
            P(("sq", "head"), None),
            P(("sq", "head"), None),
            P(("head", "sq")),
            P(("head", "sq")),
            P("sq", "head"),
            P("sq", "head"),
            P("sq", "head"),
            P("sq", "head"),
            P("head", "sq"),
            P("sq"),
            P("sq"),
            P("sq", "head"),
            P("sq", "head"),
            P("head", "sq"),
        ),
        check_vma=False,
    )
```

```python
import functools

import jax
import jax.numpy as jnp
from jax import lax
from jax.experimental import pallas as pl
from jax.experimental.pallas import tpu as pltpu
from jax.sharding import PartitionSpec as P

KD = 256
VD = 512
CHUNK = 256


eps_layer = 1e-05
eps_group = 1e-06
low = jnp.bfloat16
wide = jnp.float32


def mask_of(slot, count):
    bits = count.bit_length() - 1
    return ((slot << 1) & (count - 1)) | (slot >> (bits - 1))


def slot_of(mask, count):
    bits = count.bit_length() - 1
    return (mask >> 1) | ((mask & 1) << (bits - 1))


def flip(value, mask):
    count = lax.axis_size("sq")
    return lax.ppermute(value, "sq", [(i, i ^ mask) for i in range(count)])


def route(swapped):
    count = lax.axis_size("sq")
    lower = list(range(count.bit_length() - 2))
    return lower[::-1] if swapped else lower


def own_order(values):
    count = lax.axis_size("sq")
    width = values.shape[-1] // count
    place = lax.axis_index("sq")
    return jnp.concatenate(
        [
            lax.dynamic_slice_in_dim(values, (place ^ mask_of(s, count)) * width, width, -1)
            for s in range(count)
        ],
        axis=-1,
    )


def true_order(values):
    count = lax.axis_size("sq")
    width = values.shape[-1] // count
    place = lax.axis_index("sq")
    return jnp.concatenate(
        [
            lax.dynamic_slice_in_dim(values, slot_of(place ^ b, count) * width, width, -1)
            for b in range(count)
        ],
        axis=-1,
    )


class Box:
    def __init__(self, value):
        self.value = value

    def get(self):
        return [self.value]

    def put(self, values):
        (self.value,) = values


class Many:
    def __init__(self, *values):
        self.value = list(values)

    def get(self):
        return self.value

    def put(self, values):
        self.value = list(values)


class Gather:
    def __init__(self, *shards):
        self.count = lax.axis_size("sq")
        self.top = self.count // 2
        self.pieces = [{0: shard} for shard in shards]
        self.far = []
        self.staged = None
        self.todo = []
        for swapped in (False, True):
            slots, units = [0], []
            for bit in route(swapped):
                units += [(s, bit) for s in slots]
                slots += [s | 1 << bit for s in slots]
            self.todo.append(units)

    def send(self, times=1):
        for k, held in enumerate(self.pieces):
            for slot, bit in self.todo[k][:times]:
                held[slot | 1 << bit] = flip(held[slot], mask_of(1 << bit, self.count))
            self.todo[k] = self.todo[k][times:]

    def rest(self):
        self.send(len(self.todo[0]))

    def rest_grouped(self):
        for k, held in enumerate(self.pieces):
            while self.todo[k]:
                bit = self.todo[k][0][1]
                slots = [s for s, b in self.todo[k] if b == bit]
                self.todo[k] = self.todo[k][len(slots) :]
                got = flip(stack([held[s] for s in slots]), mask_of(1 << bit, self.count))
                for i, slot in enumerate(slots):
                    held[slot | 1 << bit] = got[i]

    def stage(self):
        sent = [s for slots, _ in self.far for s in slots]
        ready = [s for s in range(self.top) if s not in sent and all(s in h for h in self.pieces)]
        if ready:
            self.staged = ready, stack([held[s] for s in ready for held in self.pieces])

    def core(self):
        if self.staged is None:
            self.stage()
        if self.staged is not None:
            slots, both = self.staged
            self.far.append((slots, flip(both, mask_of(self.top, self.count))))
            self.staged = None

    def finish(self):
        self.rest()
        self.core()
        self.core()

    def refs(self):
        operands = [held[s] for held in self.pieces for s in range(self.top)]
        places = [[(k * self.top + s, None) for s in range(self.top)] for k in range(2)]
        for k in range(2):
            for s in range(self.top):
                for g, (slots, _) in enumerate(self.far):
                    if s in slots:
                        places[k].append((2 * self.top + g, 2 * slots.index(s) + k))
        return operands + [array for _, array in self.far], places

    def get(self):
        near = [held[s] for held in self.pieces for s in sorted(held)]
        staged = [] if self.staged is None else [self.staged[1]]
        return near + [array for _, array in self.far] + staged

    def put(self, values):
        values = iter(values)
        self.pieces = [{s: next(values) for s in sorted(held)} for held in self.pieces]
        self.far = [(slots, next(values)) for slots, _ in self.far]
        if self.staged is not None:
            self.staged = self.staged[0], next(values)


class Small:
    def __init__(self, shard):
        self.count = lax.axis_size("sq")
        self.pieces = {0: shard}
        bits = self.count.bit_length() - 1
        self.todo = [bits - 1, *range(bits - 1)]

    def send(self):
        if self.todo:
            bit, self.todo = self.todo[0], self.todo[1:]
            slots = sorted(self.pieces)
            far = flip(jnp.stack([self.pieces[s] for s in slots]), mask_of(1 << bit, self.count))
            for k, s in enumerate(slots):
                self.pieces[s | 1 << bit] = far[k]

    def rest(self):
        while self.todo:
            self.send()

    def get(self):
        return [self.pieces[s] for s in sorted(self.pieces)]

    def put(self, values):
        self.pieces = dict(zip(sorted(self.pieces), values))


class Scatter:
    def __init__(self, lefts, rights, places=None):
        self.count = lax.axis_size("sq")
        top = self.count // 2
        self.rows = lefts[0].shape[1] // self.count
        self.todo = [route(k == 1)[::-1] for k in range(2)]
        self.slots = [list(range(top)) for _ in range(2)]
        self.arrived = False
        self.sources = lefts, rights
        self.places = places
        self.held = [outer_half(lefts, rights, 1, places=places)]

    def core(self):
        self.held = [flip(self.held[0], mask_of(self.count // 2, self.count))]

    def near(self):
        self.held = outer_half(
            *self.sources, 0, self.held[0], self.rows, self.part(), self.places
        )

    def part(self):
        return [[s >> self.todo[k][0] & 1 for s in self.slots[k]] for k in range(2)]

    def send(self, lazy=False):
        self.merge()
        if not self.todo[0]:
            return
        for k in range(2):
            bit, self.todo[k] = self.todo[k][0], self.todo[k][1:]
            self.held[2 * k + 1] = flip(self.held[2 * k + 1], mask_of(1 << bit, self.count))
            self.slots[k] = [s for s in self.slots[k] if not s >> bit & 1]
        self.arrived = True
        if not lazy:
            self.merge()

    def merge(self):
        if self.arrived:
            bits = self.part() if self.todo[0] else None
            self.held = list(split(self.held[::2], self.held[1::2], self.rows, bits))
            self.arrived = False

    def rest(self):
        self.merge()
        while self.todo[0]:
            self.send()
        return self.held

    def get(self):
        return list(self.held)

    def put(self, values):
        self.held = list(values)


def send_together(*sums):
    wanted = {}
    for thing in sums:
        thing.merge()
    sums = [thing for thing in sums if thing.todo[0]]
    for thing in sums:
        for k in range(2):
            wanted.setdefault(thing.todo[k][0], []).append((thing, k))
    for bit, group in wanted.items():
        parts = [thing.held[2 * k + 1] for thing, k in group]
        got = flip(above(parts) if len(parts) > 1 else parts[0], mask_of(1 << bit, sums[0].count))
        begin = 0
        for (thing, k), part in zip(group, parts):
            thing.held[2 * k + 1] = got[begin : begin + part.shape[0]]
            begin += part.shape[0]
            thing.todo[k] = thing.todo[k][1:]
            thing.slots[k] = [s for s in thing.slots[k] if not s >> bit & 1]
    for thing in sums:
        thing.arrived = True
        thing.merge()


def settle(*things):
    values = lax.optimization_barrier(tuple(v for t in things for v in t.get()))
    values = list(values)
    for thing in things:
        size = len(thing.get())
        thing.put(values[:size])
        values = values[size:]


def ring_step(value):
    count = lax.axis_size("head")
    return lax.ppermute(value, "head", [(i, (i + 1) % count) for i in range(count)])


def sum_others(values, axis, masks):
    count = lax.axis_size(axis)
    held = [values]
    held += [lax.ppermute(values, axis, [(i, i ^ m) for i in range(count)]) for m in masks]
    while len(held) > 1:
        held = [a + b for a, b in zip(held[::2], held[1::2])]
    return held[0]


def layer_norm(values, weight_gain, weight_shift):
    centered = values - jnp.mean(values, axis=-1, keepdims=True)
    spread = lax.rsqrt(jnp.mean(centered * centered, axis=-1, keepdims=True) + eps_layer)
    return centered * spread * weight_gain + weight_shift


def gelu_gate(pre_gate, pre_up):
    return jax.nn.gelu(pre_gate) * pre_up


def log_decay(first_head, head_count):
    head_ids = (first_head + jnp.arange(head_count)).astype(jnp.float32)
    return jnp.log(1.0 - jnp.exp2(-5.0 - head_ids))


def project(left_side, right_side):
    return jnp.dot(left_side, right_side, preferred_element_type=jnp.float32)


def outer_sum(left_side, right_side):
    return lax.dot_general(
        left_side, right_side, (((0,), (0,)), ((), ())), preferred_element_type=jnp.float32
    )


def back_project(gradient, weight):
    return lax.dot_general(
        gradient, weight, (((1,), (1,)), ((), ())), preferred_element_type=jnp.float32
    )


def swap_head(value, mask):
    count = lax.axis_size("head")
    return lax.ppermute(value, "head", [(i, i ^ mask) for i in range(count)])


def stack_kernel(*refs):
    for k, ref in enumerate(refs[:-1]):
        refs[-1][k] = ref[...]


def stack(pieces):
    vmem = pl.BlockSpec(memory_space=pltpu.VMEM)
    return pl.pallas_call(
        stack_kernel,
        in_specs=[vmem] * len(pieces),
        out_specs=vmem,
        out_shape=jax.ShapeDtypeStruct((len(pieces),) + pieces[0].shape, pieces[0].dtype),
        compiler_params=pltpu.CompilerParams(vmem_limit_bytes=16 * 2**20),
        cost_estimate=brief,
    )(*pieces)


def beside_kernel(*refs):
    begin = 0
    for ref in refs[:-1]:
        refs[-1][:, pl.ds(begin, ref.shape[1])] = ref[...]
        begin += ref.shape[1]


def beside(pieces):
    vmem = pl.BlockSpec(memory_space=pltpu.VMEM)
    columns = sum(p.shape[1] for p in pieces)
    return pl.pallas_call(
        beside_kernel,
        in_specs=[vmem] * len(pieces),
        out_specs=vmem,
        out_shape=jax.ShapeDtypeStruct((pieces[0].shape[0], columns), pieces[0].dtype),
        compiler_params=pltpu.CompilerParams(vmem_limit_bytes=16 * 2**20),
        cost_estimate=brief,
    )(*pieces)


def above_kernel(*refs):
    begin = 0
    for ref in refs[:-1]:
        refs[-1][pl.ds(begin, ref.shape[0]), :] = ref[...]
        begin += ref.shape[0]


def above(pieces):
    vmem = pl.BlockSpec(memory_space=pltpu.VMEM)
    rows = sum(p.shape[0] for p in pieces)
    return pl.pallas_call(
        above_kernel,
        in_specs=[vmem] * len(pieces),
        out_specs=vmem,
        out_shape=jax.ShapeDtypeStruct((rows, pieces[0].shape[1]), pieces[0].dtype),
        compiler_params=pltpu.CompilerParams(vmem_limit_bytes=16 * 2**20),
        cost_estimate=brief,
    )(*pieces)


def add_rows_kernel(whole_ref, got_ref, out_ref):
    total = whole_ref[...].astype(wide) + got_ref[...].astype(wide)
    out_ref[...] = total.astype(out_ref.dtype)


def add_rows(whole, place, got, kind):
    rows, columns = got.shape
    block = min(columns, 1024)
    part = pl.BlockSpec((rows, block), lambda j: (0, j))
    return call(
        add_rows_kernel,
        (columns // block,),
        in_specs=[pl.BlockSpec((rows, block), lambda j: (place, j)), part],
        out_specs=part,
        out_shape=jax.ShapeDtypeStruct(got.shape, kind),
    )(whole, got)


def split_kernel(rows, bits, *refs):
    ins, outs = refs[:4], refs[4:]
    for k in range(2):
        kept, got = ins[2 * k : 2 * k + 2]
        total = kept[...].astype(wide) + got[...].astype(wide)
        if bits is None:
            outs[k][...] = total
        else:
            taken = [0, 0]
            for i, side in enumerate(bits[k]):
                place = pl.ds(taken[side] * rows, rows)
                outs[2 * k + side][place, :] = total[i * rows : (i + 1) * rows].astype(low)
                taken[side] += 1


def split(kept, got, rows, bits):
    size, columns = kept[0].shape
    block = 512 if columns % 512 == 0 else 256
    part = pl.BlockSpec((size, block), lambda j: (0, j))
    half = pl.BlockSpec((size // 2, block), lambda j: (0, j))
    if bits is None:
        out_specs = [part] * 2
        out_shape = [jax.ShapeDtypeStruct((size, columns), wide)] * 2
    else:
        out_specs = [half] * 4
        out_shape = [jax.ShapeDtypeStruct((size // 2, columns), low)] * 4
    return call(
        functools.partial(split_kernel, rows, bits),
        (columns // block,),
        in_specs=[part] * 4,
        out_specs=out_specs,
        out_shape=out_shape,
    )(kept[0], got[0], kept[1], got[1])


def combine_kernel(heads, places, factor_ref, *refs):
    *piece_refs, total_ref = refs
    size = heads * KD // 2
    for part in range(2):
        for begin in range(0, size, KD // 2):
            h, row = divmod(part * size + begin, KD)
            rows = pl.ds(begin, KD // 2)
            total = jnp.zeros((KD // 2, VD), wide)
            for k, (operand, index) in enumerate(places[part][1:]):
                ref = piece_refs[operand]
                piece = ref[rows, :] if index is None else ref[index, rows, :]
                total = total + factor_ref[k * heads + h] * piece.astype(wide)
            total_ref[h, pl.ds(row, KD // 2), :] = total


def combine(gather, log_rate, length, backward):
    count = lax.axis_size("sq")
    place = lax.axis_index("sq")
    heads = log_rate.shape[0]
    factors = []
    for slot in range(1, count):
        other = place ^ mask_of(slot, count)
        ahead = (other - place) if backward else (place - other)
        between = jnp.maximum(ahead - 1, 0).astype(wide) * length
        factors.append(jnp.where(ahead > 0, jnp.exp(log_rate * between), 0.0))
    operands, places = gather.refs()
    vmem = pl.BlockSpec(memory_space=pltpu.VMEM)
    return pl.pallas_call(
        functools.partial(combine_kernel, heads, places),
        in_specs=[smem] + [vmem] * len(operands),
        out_specs=vmem,
        out_shape=jax.ShapeDtypeStruct((heads, KD, VD), wide),
        compiler_params=pltpu.CompilerParams(vmem_limit_bytes=56 * 2**20),
        cost_estimate=brief,
    )(jnp.concatenate(factors), *operands)


def call(kernel, grid, grant=20, **options):
    return pl.pallas_call(
        kernel,
        grid=grid,
        cost_estimate=brief,
        compiler_params=pltpu.CompilerParams(
            dimension_semantics=("arbitrary",) * len(grid), vmem_limit_bytes=grant * 2**20
        ),
        **options,
    )


def dot(left_side, right_side, left_dim=1, right_dim=0):
    return lax.dot_general(
        left_side,
        right_side,
        (((left_dim,), (right_dim,)), ((), ())),
        preferred_element_type=wide,
    )


smem = pl.BlockSpec(memory_space=pltpu.SMEM)


def reach_of(rate):
    place = lax.broadcasted_iota(jnp.int32, (CHUNK, 1), 0).astype(wide)
    return jnp.exp(rate * (place + 1.0))


def tail_of(rate):
    place = lax.broadcasted_iota(jnp.int32, (CHUNK, 1), 0).astype(wide)
    return jnp.exp(rate * (CHUNK - 1.0 - place))


def decay_of(rate):
    row = lax.broadcasted_iota(jnp.int32, (CHUNK, CHUNK), 0)
    column = lax.broadcasted_iota(jnp.int32, (CHUNK, CHUNK), 1)
    spacing = (row - column).astype(wide)
    return jnp.where(spacing >= 0, jnp.exp(rate * jnp.maximum(spacing, 0.0)), 0.0)


brief = pl.CostEstimate(flops=1, bytes_accessed=1, transcendentals=0)


def bring(copies):
    for copy in copies:
        copy.start()
    return copies


def bring_pieces(refs, places, whole, sems, first):
    rows = whole.shape[0] // len(places)
    return bring(
        [
            pltpu.make_async_copy(
                refs[operand] if index is None else refs[operand].at[index],
                whole.at[pl.ds(k * rows, rows), :],
                sems.at[first + k],
            )
            for k, (operand, index) in enumerate(places)
        ]
    )


def wait_all(copies):
    for copy in copies:
        copy.wait()


def project_blocks(left, weight, product_ref):
    block = 256

    def one(j, carry):
        columns = pl.ds(pl.multiple_of(j * block, block), block)
        product_ref[:, columns] = dot(left[...], weight[:, columns]).astype(low)
        return carry

    lax.fori_loop(0, product_ref.shape[1] // block, one, 0)


def norm_project_kernel(count, slots, places, order, start, *refs):
    row_refs = refs[:slots]
    norm_ref = refs[slots]
    piece_refs = refs[slots + 1 : -8]
    normed_ref, xhat_ref, product_ref, full_ref, weight, normed, xhat, sems = refs[-8:]
    width = normed.shape[1] // count
    size = row_refs[0].shape[0]
    tile = 64
    copies = bring_pieces(piece_refs, places, weight, sems, 0)
    for turn, ref in enumerate(row_refs):

        def tile_of(t, carry, ref=ref, turn=turn):
            rows = pl.ds(pl.multiple_of(t * tile, tile), tile)
            values = [
                ref[rows, pl.ds(pl.multiple_of(order[s] * width, width), width)].astype(wide)
                for s in range(count)
            ]
            total = values[0]
            for v in values[1:]:
                total = total + v
            mean = jnp.sum(total, axis=1, keepdims=True) / (count * width)
            values = [v - mean for v in values]
            square = values[0] * values[0]
            for v in values[1:]:
                square = square + v * v
            square = jnp.sum(square, axis=1, keepdims=True)
            spread = lax.rsqrt(square / (count * width) + eps_layer)
            target = pl.ds(pl.multiple_of(start[turn] + t * tile, tile), tile)
            for s in range(count):
                columns = pl.ds(s * width, width)
                scaled = values[s] * spread
                xhat[target, columns] = scaled.astype(low)
                normed[target, columns] = (
                    scaled * norm_ref[0:1, columns] + norm_ref[1:2, columns]
                ).astype(low)
            return carry

        lax.fori_loop(0, size // tile, tile_of, 0)

    away = bring(
        [
            pltpu.make_async_copy(normed, normed_ref, sems.at[count]),
            pltpu.make_async_copy(xhat, xhat_ref, sems.at[count + 1]),
        ]
    )
    wait_all(copies)
    away += bring([pltpu.make_async_copy(weight, full_ref, sems.at[count + 2])])
    project_blocks(normed, weight, product_ref)
    wait_all(away)


def norm_project(slots, norms, gather, columns, order, start):
    count = gather.count
    pieces, places = gather.refs()
    size, depth = slots[0].shape
    length = size * len(slots)
    width = pieces[0].shape[1]
    vmem = pl.BlockSpec(memory_space=pltpu.VMEM)
    whole = pl.BlockSpec(memory_space=pl.ANY)
    return pl.pallas_call(
        functools.partial(norm_project_kernel, count, len(slots), places[0]),
        in_specs=[smem, smem] + [vmem] * (len(slots) + 1) + [whole] * len(pieces),
        out_specs=[whole, whole, vmem, whole],
        out_shape=[
            jax.ShapeDtypeStruct((length, depth), low),
            jax.ShapeDtypeStruct((length, depth), low),
            jax.ShapeDtypeStruct((length, columns), low),
            jax.ShapeDtypeStruct((depth, width), low),
        ],
        scratch_shapes=[
            pltpu.VMEM((depth, width), low),
            pltpu.VMEM((length, depth), low),
            pltpu.VMEM((length, depth), low),
            pltpu.SemaphoreType.DMA((count + 3,)),
        ],
        compiler_params=pltpu.CompilerParams(vmem_limit_bytes=36 * 2**20),
        cost_estimate=brief,
    )(order, start, *slots, norms, *pieces)


def project_kernel(count, places, left_ref, *refs):
    product_ref, full_ref, weight, sems = refs[-4:]
    wait_all(bring_pieces(refs[:-4], places, weight, sems, 0))
    away = bring([pltpu.make_async_copy(weight, full_ref, sems.at[count])])
    project_blocks(left_ref, weight, product_ref)
    wait_all(away)


def project_pieces(left_side, gather, columns):
    length, depth = left_side.shape
    count = gather.count
    pieces, places = gather.refs()
    width = pieces[0].shape[1]
    vmem = pl.BlockSpec(memory_space=pltpu.VMEM)
    whole = pl.BlockSpec(memory_space=pl.ANY)
    return pl.pallas_call(
        functools.partial(project_kernel, count, places[1]),
        in_specs=[vmem] + [whole] * len(pieces),
        out_specs=[vmem, whole],
        out_shape=[
            jax.ShapeDtypeStruct((length, columns), low),
            jax.ShapeDtypeStruct((depth, width), low),
        ],
        scratch_shapes=[pltpu.VMEM((depth, width), low), pltpu.SemaphoreType.DMA((count + 1,))],
        compiler_params=pltpu.CompilerParams(vmem_limit_bytes=20 * 2**20),
        cost_estimate=brief,
    )(left_side, *pieces)


def feed_kernel(top, quarter, places, sizes, has_prior, second_ref, cot_ref, *refs):
    quarters = len(places)
    piece_refs = []
    for size in sizes:
        piece_refs.append(refs[:size])
        refs = refs[size:]
    if has_prior:
        prior_grad, prior_down, *refs = refs
    hidden_refs = [refs[2 * t : 2 * t + 2] for t in range(quarters)]
    grad_ref, down_part_ref = refs[2 * quarters : 2 * quarters + 2]
    first, later, gate_pre, up_pre, grad_inner, sums, sems = refs[2 * quarters + 2 :]
    rows, depth = second_ref.shape
    middle = quarter // 2
    hidden = pl.ds(0, quarter)
    hidden_up = pl.ds(quarter, quarter)
    down = pl.ds(quarter, middle)
    sides = [pl.ds(0, middle), pl.ds(middle, middle)]
    halves = [pl.ds(0, depth // 2), pl.ds(depth // 2, depth // 2)]
    copies = []
    for t in range(quarters):
        for k, whole in enumerate((first, later)):
            index = (t * 2 + k) * 2 * top
            some = bring_pieces(piece_refs[t], places[t][k], whole.at[t], sems, index)
            copies += [some[:top], some[top:]]
    tile = 16
    scale = 0.7978845608028654
    for t in range(quarters):
        inner_ref, grads_ref = hidden_refs[t]
        for k, (whole, target) in enumerate(((first, gate_pre), (later, up_pre))):
            for h in range(2):
                wait_all(copies[(t * 2 + k) * 2 + h])
                part = dot(second_ref[:, halves[h]], whole[t, halves[h], hidden])
                side = dot(cot_ref[:, halves[h]], whole[t, halves[h], down])
                target[...] = part if h == 0 else target[...] + part
                grad_inner[:, sides[k]] = side if h == 0 else grad_inner[:, sides[k]] + side

        def activate(i, carry, inner_ref=inner_ref, grads_ref=grads_ref):
            at = pl.ds(pl.multiple_of(i * tile, tile), tile)
            v, u, g = gate_pre[at, :], up_pre[at, :], grad_inner[at, :]
            square = v * v
            bent = jnp.tanh(scale * v * (1.0 + 0.044715 * square))
            shared = 0.5 * (1.0 + bent)
            gelu = v * shared
            slope = shared + (0.5 * scale) * v * (1.0 - bent * bent) * (1.0 + 0.134145 * square)
            inner_ref[at, :] = (gelu * u).astype(low)
            grads_ref[at, hidden] = (g * u * slope).astype(low)
            grads_ref[at, hidden_up] = (g * gelu).astype(low)
            return carry

        lax.fori_loop(0, rows // tile, activate, 0)
        for half in halves:
            grad = dot(grads_ref[:, hidden], first[t, half, hidden], 1, 1)
            grad = grad + dot(grads_ref[:, hidden_up], later[t, half, hidden], 1, 1)
            down_part = dot(inner_ref[:, sides[0]], first[t, half, down], 1, 1)
            down_part = down_part + dot(inner_ref[:, sides[1]], later[t, half, down], 1, 1)
            if t > 0:
                grad = grad + sums[0, :, half]
                down_part = down_part + sums[1, :, half]
            elif has_prior:
                grad = grad + prior_grad[:, half]
                down_part = down_part + prior_down[:, half]
            if t < quarters - 1:
                sums[0, :, half] = grad
                sums[1, :, half] = down_part
            else:
                grad_ref[:, half] = grad.astype(grad_ref.dtype)
                down_part_ref[:, half] = down_part.astype(down_part_ref.dtype)


def feed_part(second, cot, gathers, quarter, prior, kind):
    top = gathers[0].top
    quarters = len(gathers)
    rows, depth = second.shape
    pieces, places, sizes = [], [], []
    for gather in gathers:
        operands, where = gather.refs()
        pieces += operands
        places.append(where)
        sizes.append(len(operands))
    width = pieces[0].shape[1]
    vmem = pl.BlockSpec(memory_space=pltpu.VMEM)
    out = jax.ShapeDtypeStruct((rows, depth), kind)
    hidden = [
        jax.ShapeDtypeStruct((rows, quarter), low),
        jax.ShapeDtypeStruct((rows, 2 * quarter), low),
    ]
    return pl.pallas_call(
        functools.partial(feed_kernel, top, quarter, places, sizes, bool(prior)),
        in_specs=[vmem] * 2
        + [pl.BlockSpec(memory_space=pl.ANY)] * len(pieces)
        + [vmem] * len(prior),
        out_specs=[vmem] * (2 * quarters + 2),
        out_shape=hidden * quarters + [out, out],
        scratch_shapes=[
            pltpu.VMEM((quarters, depth, width), low),
            pltpu.VMEM((quarters, depth, width), low),
            pltpu.VMEM((rows, quarter), wide),
            pltpu.VMEM((rows, quarter), wide),
            pltpu.VMEM((rows, quarter), wide),
            pltpu.VMEM((2, rows, depth), wide),
            pltpu.SemaphoreType.DMA((4 * top * quarters,)),
        ],
        compiler_params=pltpu.CompilerParams(vmem_limit_bytes=(22 + 12 * quarters) * 2**20),
        cost_estimate=brief,
    )(second, cot, *pieces, *prior)


def outer_kernel(count, added, rows, bits, *refs):
    lefts, rights, refs = refs[:count], refs[count : 2 * count], refs[2 * count :]
    got = refs[0] if added else None
    outs, flipped = refs[added:-1], refs[-1]
    turn = pl.program_id(0)
    starts = [sum(ref.shape[0] for ref in lefts[:i]) for i in range(count)]

    @pl.when(turn == 0)
    def _():
        for begin, ref in zip(starts, lefts):
            flipped[:, pl.ds(begin, ref.shape[0])] = ref[...].T

    total = 0.0
    for begin, ref in zip(starts, rights):
        total = total + dot(flipped[:, pl.ds(begin, ref.shape[0])], ref[...])
    if added:
        total = total + got[...].astype(wide)
    if bits is None:
        outs[0][...] = total.astype(low)
    else:
        for k in range(2):

            @pl.when(turn // (pl.num_programs(0) // 2) == k)
            def _(k=k):
                taken = [0, 0]
                for i, side in enumerate(bits[k]):
                    place = pl.ds(taken[side] * rows, rows)
                    outs[2 * k + side][place, :] = total[i * rows : (i + 1) * rows].astype(low)
                    taken[side] += 1


def outer_half(lefts, rights, part, got=None, rows=None, bits=None, places=None):
    depth = lefts[0].shape[1] // 2
    columns = rights[0].shape[1]
    block = 512 if columns % 1024 == 0 else 256
    blocks = columns // block
    whole = pl.BlockSpec((depth, block), lambda j, p: (0, j))
    extra = [] if got is None else [got]
    if bits is None:
        out_specs, out_shape = [whole], [jax.ShapeDtypeStruct((depth, columns), low)]
    else:
        early = pl.BlockSpec((depth // 2, block), lambda j, p: (0, jnp.minimum(j, blocks // 2 - 1)))
        late = pl.BlockSpec((depth // 2, block), lambda j, p: (0, jnp.maximum(j - blocks // 2, 0)))
        out_specs = [early, early, late, late]
        out_shape = [jax.ShapeDtypeStruct((depth // 2, columns // 2), low)] * 4
    if places is None:
        places = jnp.zeros(len(lefts), jnp.int32)
    kernel = functools.partial(outer_kernel, len(lefts), len(extra), rows, bits)
    result = pl.pallas_call(
        lambda place_ref, *refs: kernel(*refs),
        grid_spec=pltpu.PrefetchScalarGridSpec(
            num_scalar_prefetch=1,
            grid=(blocks,),
            in_specs=[pl.BlockSpec((v.shape[0], depth), lambda j, p: (0, part)) for v in lefts]
            + [
                pl.BlockSpec((v.shape[0], block), lambda j, p, i=i: (p[i], j))
                for i, v in enumerate(lefts)
            ]
            + [whole] * len(extra),
            out_specs=out_specs,
            scratch_shapes=[pltpu.VMEM((depth, sum(v.shape[0] for v in lefts)), low)],
        ),
        out_shape=out_shape,
        compiler_params=pltpu.CompilerParams(vmem_limit_bytes=20 * 2**20),
        cost_estimate=brief,
    )(places, *lefts, *rights, *extra)
    return result[0] if bits is None else list(result)


def rows_kernel(parts, sides, sums, size, begin_ref, *refs):
    lefts = [refs[p * sides : (p + 1) * sides] for p in range(parts)]
    refs = refs[parts * sides :]
    xhats, weights, out_ref = refs[: parts * sums], refs[parts * sums :][:sides], refs[parts * sums + sides]
    for p in range(parts):
        part = dot(lefts[p][0][...], weights[0][...], 1, 1)
        for k in range(1, sides):
            part = part + dot(lefts[p][k][...], weights[k][...], 1, 1)
        out_ref[pl.ds(p * size, size), :] = part.astype(out_ref.dtype)
        if sums:
            sums_ref = refs[-1]
            gain = jnp.sum(part * xhats[p][...].astype(wide), axis=0, keepdims=True)
            shift = jnp.sum(part, axis=0, keepdims=True)
            sums_ref[0:1, :] = gain if p == 0 else sums_ref[0:1, :] + gain
            sums_ref[1:2, :] = shift if p == 0 else sums_ref[1:2, :] + shift


def rows_back(lefts, weights, begins, size, xhat=None):
    depth = weights[0][0].shape[0]
    block = 512
    parts, sides = len(begins), len(lefts)
    in_specs, operands = [], []
    for p in range(parts):
        for (left, column), (_, _, columns) in zip(lefts, weights):
            in_specs.append(pl.BlockSpec((size, columns), lambda j, b, p=p, column=column: (b[p], column)))
            operands.append(left)
    if xhat is not None:
        for p in range(parts):
            in_specs.append(pl.BlockSpec((size, block), lambda j, b, p=p: (b[p], j)))
            operands.append(xhat)
    for weight, column, columns in weights:
        in_specs.append(pl.BlockSpec((block, columns), lambda j, b, column=column: (j, column)))
        operands.append(weight)
    out_specs = [pl.BlockSpec((parts * size, block), lambda j, b: (0, j))]
    out_shape = [jax.ShapeDtypeStruct((parts * size, depth), low)]
    if xhat is not None:
        out_specs.append(pl.BlockSpec((2, block), lambda j, b: (0, j)))
        out_shape.append(jax.ShapeDtypeStruct((2, depth), wide))
    return pl.pallas_call(
        functools.partial(rows_kernel, parts, sides, int(xhat is not None), size),
        grid_spec=pltpu.PrefetchScalarGridSpec(
            num_scalar_prefetch=1, grid=(depth // block,), in_specs=in_specs, out_specs=out_specs
        ),
        out_shape=out_shape,
        compiler_params=pltpu.CompilerParams(vmem_limit_bytes=56 * 2**20),
        cost_estimate=brief,
    )(jnp.stack(begins) // size, *operands)


def parts_of(heads):
    values = [pl.ds(h * VD, VD) for h in range(heads)]
    keys = [pl.ds(heads * VD + h * KD, KD) for h in range(heads)]
    return values, keys


def state_halves(state, heads, refs):
    if heads == 2:
        for h in range(2):
            refs[h][...] = state[h].astype(low)
    else:
        for k in range(2):
            refs[k][...] = state[0, pl.ds(k * KD // 2, KD // 2), :].astype(low)


def state_kernel(heads, chunks, rate_ref, kv_ref, one_ref, two_ref, state):
    values, keys = parts_of(heads)
    turn = pl.program_id(0)

    @pl.when(turn == 0)
    def _():
        state[...] = jnp.zeros_like(state)

    for h in range(heads):
        rate = rate_ref[h]
        scaled = (kv_ref[:, keys[h]].astype(wide) * tail_of(rate)).astype(low)
        kept = state[h] * jnp.exp(jnp.full((1, 1), rate * CHUNK, wide))
        state[h] = kept + dot(scaled, kv_ref[:, values[h]], 0, 0)

    @pl.when(turn == chunks - 1)
    def _():
        state_halves(state, heads, [one_ref, two_ref])


def final_state(kv, log_rate, heads):
    length, columns = kv.shape
    chunks = length // CHUNK
    half = jax.ShapeDtypeStruct((heads * KD // 2, VD), low)
    return call(
        functools.partial(state_kernel, heads, chunks),
        (chunks,),
        in_specs=[smem, pl.BlockSpec((CHUNK, columns), lambda c: (c, 0))],
        out_specs=[pl.BlockSpec(half.shape, lambda c: (0, 0))] * 2,
        out_shape=[half, half],
        scratch_shapes=[pltpu.VMEM((heads, KD, VD), wide)],
    )(log_rate, kv)


def retain_kernel(
    heads, rate_ref, kv_ref, qs_ref, first_ref, gated_ref, grouped_ref, factor_ref, states_ref, held, table
):
    values, keys = parts_of(heads)

    @pl.when(pl.program_id(0) == 0)
    def _():
        held[...] = first_ref[...]
        for h in range(heads):
            table[h] = decay_of(rate_ref[h])

    for h in range(heads):
        rate = rate_ref[h]
        query, key = qs_ref[:, keys[h]], kv_ref[:, keys[h]]
        value = kv_ref[:, values[h]]
        state = held[h]
        state_low = state.astype(low)
        states_ref[0, h] = state_low
        mixing = (dot(query, key, 1, 1) * table[h]).astype(low)
        retained = dot(mixing, value) + reach_of(rate) * dot(query, state_low)
        scaled = (key.astype(wide) * tail_of(rate)).astype(low)
        held[h] = state * jnp.exp(jnp.full((1, 1), rate * CHUNK, wide)) + dot(scaled, value, 0, 0)
        factor = lax.rsqrt(jnp.mean(retained * retained, axis=1, keepdims=True) + eps_group)
        grouped = (retained * factor).astype(low)
        factor_ref[h] = factor
        grouped_ref[:, values[h]] = grouped
        pre = qs_ref[:, values[h]].astype(wide)
        gated_ref[:, values[h]] = (grouped.astype(wide) * (pre * jax.nn.sigmoid(pre))).astype(low)


def retain(kv, qs, first, log_rate, heads):
    length, columns = kv.shape
    chunks = length // CHUNK
    rows = pl.BlockSpec((CHUNK, columns), lambda c: (c, 0))
    out = pl.BlockSpec((CHUNK, heads * VD), lambda c: (c, 0))
    return call(
        functools.partial(retain_kernel, heads),
        (chunks,),
        56,
        in_specs=[smem, rows, rows, pl.BlockSpec((heads, KD, VD), lambda c: (0, 0, 0))],
        out_specs=[
            out,
            out,
            pl.BlockSpec((heads, CHUNK, 1), lambda c: (0, c, 0)),
            pl.BlockSpec((1, heads, KD, VD), lambda c: (c, 0, 0, 0)),
        ],
        out_shape=[
            jax.ShapeDtypeStruct((length, heads * VD), low),
            jax.ShapeDtypeStruct((length, heads * VD), low),
            jax.ShapeDtypeStruct((heads, length, 1), wide),
            jax.ShapeDtypeStruct((chunks, heads, KD, VD), low),
        ],
        scratch_shapes=[pltpu.VMEM((heads, KD, VD), wide), pltpu.VMEM((heads, CHUNK, CHUNK), wide)],
    )(log_rate, kv, qs, first)


def gate_back_kernel(
    heads, first, last, place_ref, rate_ref, branch_ref, left_ref, right_ref, grouped_ref, factor_ref, qs_ref, *refs
):
    values, keys = parts_of(heads)
    if not first:
        _, _, prior_ref, *refs = refs
    swish_ref, retained_ref, *halves, crossed_ref = refs
    start = (place_ref[0] * CHUNK).astype(wide)
    sides = [dot(branch_ref[...], ref[...]) for ref in (left_ref, right_ref)]
    gated = sides if heads == 2 else [jnp.concatenate(sides, axis=1)]
    for h in range(heads):
        rate = rate_ref[h]
        gated_grad = gated[h]
        grouped = grouped_ref[:, values[h]].astype(wide)
        pre = qs_ref[:, values[h]].astype(wide)
        sigma = jax.nn.sigmoid(pre)
        swish_ref[:, values[h]] = (
            gated_grad * grouped * (sigma * (1.0 + pre * (1.0 - sigma)))
        ).astype(low)
        grouped_grad = (gated_grad * (pre * sigma)).astype(low).astype(wide)
        factor = factor_ref[h]
        mean = jnp.mean(grouped_grad * grouped, axis=1, keepdims=True)
        retained_grad = (factor * (grouped_grad - grouped * mean)).astype(low)
        retained_ref[:, values[h]] = retained_grad
        scale = reach_of(rate) * jnp.exp(jnp.full((1, 1), rate * start, wide))
        scaled = (qs_ref[:, keys[h]].astype(wide) * scale).astype(low)
        crossed = dot(scaled, retained_grad, 0, 0)
        crossed_ref[h] = crossed if first else prior_ref[h] + crossed
    if last:
        state_halves(crossed_ref, heads, halves)


def gate_back(branch, left, right, column, grouped, factor, qs, log_rate, heads, place, prior, last):
    length, columns = qs.shape
    depth = branch.shape[1]
    part = pl.BlockSpec((CHUNK, heads * VD), lambda i, p: (p[0], 0))
    total = pl.BlockSpec((heads, KD, VD), lambda i, p: (0, 0, 0))
    whole = pl.BlockSpec(memory_space=pl.ANY)
    half = pl.BlockSpec((heads * KD // 2, VD), lambda i, p: (0, 0))
    grid_spec = pltpu.PrefetchScalarGridSpec(
        num_scalar_prefetch=1,
        grid=(1,),
        in_specs=[
            smem,
            pl.BlockSpec((CHUNK, depth), lambda i, p: (0, 0)),
            pl.BlockSpec((depth, heads * VD // 2), lambda i, p: (0, column)),
            pl.BlockSpec((depth, heads * VD // 2), lambda i, p: (0, column)),
            part,
            pl.BlockSpec((heads, CHUNK, 1), lambda i, p: (0, p[0], 0)),
            pl.BlockSpec((CHUNK, columns), lambda i, p: (p[0], 0)),
        ]
        + [whole, whole, total][: len(prior)],
        out_specs=[part, part] + ([half] * 2 if last else [total]),
        scratch_shapes=[pltpu.VMEM((heads, KD, VD), wide)] if last else [],
    )
    return pl.pallas_call(
        functools.partial(gate_back_kernel, heads, not prior, last),
        grid_spec=grid_spec,
        out_shape=[
            jax.ShapeDtypeStruct((length, heads * VD), low),
            jax.ShapeDtypeStruct((length, heads * VD), low),
        ]
        + (
            [jax.ShapeDtypeStruct((heads * KD // 2, VD), low)] * 2
            if last
            else [jax.ShapeDtypeStruct((heads, KD, VD), wide)]
        ),
        input_output_aliases={8: 0, 9: 1} if prior else {},
        compiler_params=pltpu.CompilerParams(vmem_limit_bytes=56 * 2**20),
        cost_estimate=brief,
    )(place.reshape(1), log_rate, branch, left, right, grouped, factor, qs, *prior)


def retain_back_kernel(
    heads, rate_ref, kv_ref, qs_ref, grad_ref, states_ref, last_ref, back_ref, held, table
):
    values, keys = parts_of(heads)
    queries = [pl.ds(heads * (VD + KD) + h * KD, KD) for h in range(heads)]

    @pl.when(pl.program_id(0) == 0)
    def _():
        held[...] = last_ref[...]
        for h in range(heads):
            table[h] = decay_of(rate_ref[h])

    for h in range(heads):
        rate = rate_ref[h]
        query, key = qs_ref[:, keys[h]], kv_ref[:, keys[h]]
        value, grad = kv_ref[:, values[h]], grad_ref[:, values[h]]
        decay = table[h]
        reach, tail = reach_of(rate), tail_of(rate)
        later = held[h]
        later_low = later.astype(low)
        mixing = (dot(query, key, 1, 1) * decay).astype(low)
        scores_grad = (dot(grad, value, 1, 1) * decay).astype(low)
        back_ref[:, queries[h]] = (
            dot(scores_grad, key) + reach * dot(grad, states_ref[0, h], 1, 1)
        ).astype(low)
        back_ref[:, keys[h]] = (
            dot(scores_grad, query, 0, 0) + tail * dot(value, later_low, 1, 1)
        ).astype(low)
        back_ref[:, values[h]] = (
            dot(mixing, grad, 0, 0) + tail * dot(key, later_low)
        ).astype(low)
        scaled = (query.astype(wide) * reach).astype(low)
        held[h] = later * jnp.exp(jnp.full((1, 1), rate * CHUNK, wide)) + dot(scaled, grad, 0, 0)


def retain_back(kv, qs, retained_grad, states, last, log_rate, heads):
    length, columns = kv.shape
    chunks = length // CHUNK
    rows = pl.BlockSpec((CHUNK, columns), lambda c: (chunks - 1 - c, 0))
    part = pl.BlockSpec((CHUNK, heads * VD), lambda c: (chunks - 1 - c, 0))
    return call(
        functools.partial(retain_back_kernel, heads),
        (chunks,),
        56,
        in_specs=[
            smem,
            rows,
            rows,
            part,
            pl.BlockSpec((1, heads, KD, VD), lambda c: (chunks - 1 - c, 0, 0, 0)),
            pl.BlockSpec((heads, KD, VD), lambda c: (0, 0, 0)),
        ],
        out_specs=pl.BlockSpec((CHUNK, columns + heads * KD), lambda c: (chunks - 1 - c, 0)),
        out_shape=jax.ShapeDtypeStruct((length, columns + heads * KD), low),
        scratch_shapes=[pltpu.VMEM((heads, KD, VD), wide), pltpu.VMEM((heads, CHUNK, CHUNK), wide)],
    )(log_rate, kv, qs, retained_grad, states, last)


def shards(
    layer_in,
    norm1_gain,
    norm1_bias,
    w_query,
    w_key,
    w_value,
    w_swish,
    w_out,
    norm2_gain,
    norm2_bias,
    w_gate,
    w_up,
    w_down,
    cotangent,
):
    count_sq = lax.axis_size("sq")
    count_head = lax.axis_size("head")
    sq_index = lax.axis_index("sq")
    head_index = lax.axis_index("head")
    own_rows = layer_in.shape[0]
    length = own_rows * count_head
    key_scale = KD ** (-0.5)
    value_width = w_value.shape[1]
    depth = layer_in.shape[1]
    heads = value_width // VD
    log_rate = log_decay(head_index * heads, heads)
    order = jnp.stack([sq_index ^ mask_of(s, count_sq) for s in range(count_sq)]).astype(jnp.int32)
    start = [lax.rem(head_index - t + count_head, count_head) * own_rows for t in range(count_head)]
    kin_steps = []
    while 2 << len(kin_steps) < count_head:
        kin_steps.append(2 << len(kin_steps))

    key_width = w_key.shape[1]
    pair_width = value_width + key_width

    norm = Small(jnp.stack([norm1_gain, norm1_bias, norm2_gain, norm2_bias]))
    out_shard = w_out.T
    out_half = out_shard.shape[1] // 2
    first = Gather(
        jnp.concatenate(
            [w_value, (w_key.astype(wide) * key_scale).astype(low), out_shard[:, :out_half]], axis=1
        ),
        jnp.concatenate([w_swish, w_query, out_shard[:, out_half:]], axis=1),
    )
    quarter_width = w_gate.shape[1]
    middle = quarter_width // 2
    down_shard = w_down.T
    feed_first = Box(jnp.concatenate([w_gate, down_shard[:, :middle]], axis=1))
    feed_later = Box(jnp.concatenate([w_up, down_shard[:, middle:]], axis=1))
    kin_parts = [
        Box(w_gate),
        Box(w_up),
        Box(down_shard),
    ]
    cot_own = Box(own_order(cotangent))
    x_own = Box(own_order(layer_in))
    slots = [Box(layer_in)]
    settle(slots[0], first, norm)
    for turn in range(1, count_head):
        slots.append(Box(ring_step(slots[-1].value)))
        first.core()
        first.send()
        norm.send()
        settle(slots[-1], first, norm, feed_first, feed_later, cot_own, x_own, *kin_parts)
    norm.rest()
    first.rest()
    first.core()

    def kin(value):
        held = [value]
        for step in kin_steps:
            held += [swap_head(v, step) for v in held]
        return held

    x_own = x_own.value
    packs = [Many(*kin(kin_parts[0].value)[1:])]
    cot_far = Box(swap_head(cot_own.value, 1))
    feeds = [Gather(feed_first.value, feed_later.value)]
    feeds[0].stage()
    feeds[0].send()
    norms = jnp.concatenate([norm.pieces[s] for s in range(count_sq)], axis=1).astype(wide)
    gain_one, shift_one, gain_two, shift_two = norms[0], norms[1], norms[2], norms[3]
    normed, xhat, kv, first_full = norm_project(
        [b.value for b in slots],
        norms,
        first,
        pair_width,
        order,
        jnp.stack(start).astype(jnp.int32),
    )
    passed = Gather(*final_state(kv, log_rate, heads))
    settle(passed, *packs, cot_far, feeds[0], cot_own, *kin_parts[1:])

    passed.send()
    packs.append(Many(*kin(kin_parts[1].value)[1:]))
    settle(passed)
    passed.rest()
    qs, later_full = project_pieces(normed, first, pair_width)
    qs = Box(qs)
    settle(passed, packs[1], cot_far, feeds[0], cot_own, kin_parts[2], qs)
    qs, cot_own = qs.value, cot_own.value
    passed.core()
    packs.append(Many(*kin(kin_parts[2].value)[1:]))
    feeds[0].core()
    feeds[0].send()
    incoming = combine(passed, log_rate, length, False)
    gated_low, grouped, factor, states = retain(kv, qs, incoming, log_rate, heads)

    out_column = pair_width // out_half

    def out_part(turns):
        (parts,) = rows_back(
            [(gated_low, 0), (gated_low, 1)],
            [(first_full, out_column, out_half), (later_full, out_column, out_half)],
            [start[turn % count_head] for turn in turns],
            own_rows,
        )
        return parts

    total = Box(out_part([1]))
    gated = Box(gated_low)
    settle(packs[2], total, feeds[0], gated)
    gated_low = gated.value
    quarters = 1 + len(packs[0].value)
    parts = Box(out_part(range(2, count_head + 1)))
    for turn in range(2, count_head + 1):
        got = ring_step(total.value)
        if turn == 2:
            feeds[0].stage()
            feeds[0].send()
            for gate, up, down in zip(*[p.value for p in packs]):
                feeds.append(
                    Gather(
                        jnp.concatenate([gate, down[:, :middle]], axis=1),
                        jnp.concatenate([up, down[:, middle:]], axis=1),
                    )
                )
                feeds[-1].stage()
        else:
            feeds[0].core()
            if turn == 3:
                feeds[0].stage()
            for thing in feeds[1:]:
                if turn == 3:
                    thing.core()
                thing.send()
        total = Box(add_rows(parts.value, turn - 2, got, low if turn < count_head else wide))
        settle(total, *feeds, parts)
    hidden = x_own.astype(wide) + total.value
    second_own = Box(layer_norm(hidden, gain_two, shift_two).astype(low))

    settle(second_own, *feeds)
    second_own = second_own.value
    second_far = Box(swap_head(second_own, 1))
    for thing in feeds[1:]:
        thing.core()
        thing.rest()
    feeds[0].finish()
    fed = feed_part(second_own, cot_own, feeds[:1], quarter_width, [], wide)
    inner_own, grads_own, fed_sums = [fed[0]], [fed[1]], Many(*fed[2:])
    settle(second_far, *feeds[1:], cot_far, fed_sums)
    second_far, cot_far = second_far.value, cot_far.value
    for thing in feeds[1:]:
        thing.finish()
    fed = feed_part(second_far, cot_far, feeds, quarter_width, [], low)
    inner_far, grads_far = fed[: 2 * quarters : 2], fed[1 : 2 * quarters : 2]
    grad_far, down_far, near = Box(fed[-2]), Box(fed[-1]), Box(second_own)
    settle(grad_far, near, down_far)

    grad_far = Box(swap_head(grad_far.value, 1))
    fed = feed_part(near.value, cot_own, feeds[1:], quarter_width, fed_sums.value, wide)
    inner_own += fed[: 2 * quarters - 2 : 2]
    grads_own += fed[1 : 2 * quarters - 2 : 2]
    second = Many(near.value, second_far)
    cot = Many(cot_own, cot_far)
    inner = Many(beside(inner_own), beside(inner_far))
    grads = [Many(a, b) for a, b in zip(grads_own, grads_far)]
    late_sums = [Scatter(second.value, g.value) for g in grads[1:]]
    down_sum = Scatter(cot.value, inner.value)
    settle(grad_far, *late_sums, down_sum, second, grads[0], down_far)
    second_grad = fed[-2] + grad_far.value.astype(wide)
    _, second_back = jax.vjp(layer_norm, hidden, gain_two, shift_two)
    hidden_part, gain_two_part, shift_two_part = second_back(second_grad)
    grad_hidden = cot_own.astype(wide) + hidden_part

    slots = [Box(grad_hidden.astype(low))]
    settle(slots[0], *late_sums, down_sum, second, grads[0], down_far)
    waits = [*late_sums, down_sum, down_far]
    passing = []
    for turn in range(count_head):
        rows = slots[-1]
        if turn < count_head - 1:
            slots.append(Box(ring_step(rows.value)))
        if turn == 0:
            for thing in [*late_sums, down_sum]:
                thing.core()
                thing.near()
            early_sum = Scatter(second.value, grads[0].value)
            waits.append(early_sum)
        elif turn == 1:
            for thing in late_sums:
                thing.send()
            early_sum.core()
        elif turn == 2:
            send_together(down_sum, late_sums[0])
            for thing in late_sums:
                thing.rest()
            early_sum.near()
            down_far = Box(swap_head(down_far.value, 1))
            waits.append(down_far)
        for done in {0: (), 1: (0,), 2: (1, 2)}.get(turn, (turn,)):
            passing = gate_back(
                slots[done].value,
                first_full,
                later_full,
                out_column,
                grouped,
                factor,
                qs,
                log_rate,
                heads,
                start[done] // own_rows,
                passing,
                done == count_head - 1,
            )
        if turn < count_head - 1:
            passing = Many(*passing)
            settle(slots[-1], *waits, passing)
            passing = passing.value
    swish_grad, retained_grad, *crossed = passing

    def kin_sum(held):
        parts = []
        held = [None] + list(held)
        for step in kin_steps[::-1]:
            size = len(held) // 2
            got = [swap_head(h, step) for h in held[size:]]
            parts.append(got[0])
            held = [None] + [
                (h.astype(wide) + g.astype(wide)).astype(low) for h, g in zip(held[1:size], got[1:])
            ]
        return parts

    branch, gated = Many(*[rows.value for rows in slots]), Box(gated_low)
    places = (jnp.stack(start) // own_rows).astype(jnp.int32)
    cut = 3 * quarter_width // 4
    gates = [thing.rest()[0].astype(low) for thing in late_sums]
    ups = [thing.rest()[1].astype(low) for thing in late_sums]
    early = [Many(*kin_sum([gate[:, :cut] for gate in gates]))]
    kin_next = Many(
        *[beside([gate[:, cut:], up[:, :cut]]) for gate, up in zip(gates, ups)]
    )
    ups = Many(*[up[:, cut:] for up in ups])
    passed = Gather(*crossed)
    swish = Box(swish_grad)
    settle(passed, early_sum, down_sum, ups, kin_next, branch, gated, swish)
    passed.send()
    settle(passed, early[0], down_sum, ups, kin_next, swish, branch, gated)
    early.append(Many(*kin_sum(kin_next.value)))
    passed.rest_grouped()
    down_sum.send(True)
    swish_sum = Scatter([normed], [swish.value])
    out_sum = Scatter(branch.value, [gated.value] * count_head, places)
    settle(passed, early[1], early_sum, down_sum, ups, swish_sum, out_sum)
    passed.core()
    down_parts = jnp.split(jnp.concatenate(down_sum.rest(), axis=1), quarters, axis=1)
    early.append(
        Many(
            *kin_sum(
                [
                    beside([up, part.astype(low)])
                    for up, part in zip(ups.value, down_parts[1:])
                ]
            )
        )
    )
    early_sum.send(True)
    swish_sum.core()
    returned = combine(passed, log_rate, length, True)
    backs = retain_back(kv, qs, retained_grad, states, returned, log_rate, heads)

    def normed_part(turns, backs):
        query = 2 + value_width // key_width - 1
        return rows_back(
            [(backs, 0), (swish_grad, 0), (backs, query)],
            [
                (first_full, 0, pair_width),
                (later_full, 0, value_width),
                (later_full, query - 1, key_width),
            ],
            [start[turn % count_head] for turn in turns],
            own_rows,
            xhat,
        )

    total, norm_sums = normed_part([1], backs)
    total, backs, norm_sums = Box(total), Box(backs), Box(norm_sums)
    settle(total, early_sum, swish_sum, out_sum, backs, norm_sums, early[2])
    parts, more_sums = normed_part([2], backs.value)
    parts = [Box(parts)]
    norm_sums = Many(norm_sums.value, more_sums)
    for turn in range(2, count_head + 1):
        got = ring_step(total.value)
        if turn == 2:
            early_sum.rest()
            out_sum.core()
            back_sum = Scatter([normed], [backs.value])
            back_sum.core()
            back_sum.near()
            settle(back_sum, parts[0])
            waits = [early_sum, swish_sum, back_sum, out_sum]
        elif turn == 3:
            back_sum.send()
            swish_sum.near()
            swish_sum.send(True)
            out_sum.near()
            later_parts, more_sums = normed_part(range(3, count_head + 1), backs.value)
            parts.append(Box(later_parts))
            norm_sums = Many(*norm_sums.value, more_sums)
            waits = [swish_sum, back_sum, out_sum]
        elif turn == 4:
            back_sum.rest()
            out_sum.send(True)
            norm_sums = true_order(
                jnp.concatenate(
                    [sum(norm_sums.value), jnp.stack([gain_two_part, shift_two_part])]
                )
            )
            norm_sums = Many(sum_others(norm_sums, "sq", [1]))
            waits = [back_sum, swish_sum, out_sum]
        part = (parts[0], 0) if turn == 2 else (parts[1], turn - 3)
        total = Box(
            add_rows(part[0].value, part[1], got, low if turn < count_head else wide)
        )
        settle(total, *waits, *parts, norm_sums, backs)
    _, first_back = jax.vjp(lambda v: layer_norm(v, gain_one, shift_one), x_own.astype(wide))
    grad_in = grad_hidden + first_back(total.value)[0]
    norm_sums = sum_others(norm_sums.value[0], "sq", range(2, count_sq, 2))
    norm_sums = sum_others(norm_sums, "head", range(1, count_head))
    first_sum, later_sum = early_sum.rest()
    early = [sum(p.astype(wide) for p in e.value) for e in early]
    early = jnp.concatenate(early, axis=1)
    grad_gate = first_sum + early[:, :quarter_width]
    grad_up = later_sum + early[:, quarter_width : 2 * quarter_width]
    grad_down = (down_parts[0] + early[:, 2 * quarter_width :]).T
    grad_value, grad_key_query = back_sum.rest()
    grad_swish = jnp.concatenate(swish_sum.rest(), axis=1)
    grad_out = jnp.concatenate(out_sum.rest(), axis=1).T
    result = (hidden + fed[-1] + down_far.value.astype(wide)).astype(low)

    piece = depth // (count_sq * count_head)
    first_norm = lax.dynamic_slice_in_dim(
        norm_sums[:2], (head_index * count_sq + sq_index) * piece, piece, 1
    )
    piece = depth // count_sq
    second_norm = lax.dynamic_slice_in_dim(norm_sums[2:], sq_index * piece, piece, 1)
    return (
        true_order(result),
        true_order(grad_in),
        first_norm[0],
        first_norm[1],
        grad_key_query[:, key_width:],
        grad_key_query[:, :key_width] * key_scale,
        grad_value,
        grad_swish,
        grad_out,
        second_norm[0],
        second_norm[1],
        grad_gate,
        grad_up,
        grad_down,
    )


def solution(mesh):
    return jax.shard_map(
        shards,
        mesh=mesh,
        in_specs=(
            P(("sq", "head"), None),
            P("sq"),
            P("sq"),
            P("sq", "head"),
            P("sq", "head"),
            P("sq", "head"),
            P("sq", "head"),
            P("head", "sq"),
            P("sq"),
            P("sq"),
            P("sq", "head"),
            P("sq", "head"),
            P("head", "sq"),
            P(("sq", "head"), None),
        ),
        out_specs=(
            P(("sq", "head"), None),
            P(("sq", "head"), None),
            P(("head", "sq")),
            P(("head", "sq")),
            P("sq", "head"),
            P("sq", "head"),
            P("sq", "head"),
            P("sq", "head"),
            P("head", "sq"),
            P("sq"),
            P("sq"),
            P("sq", "head"),
            P("sq", "head"),
            P("head", "sq"),
        ),
        check_vma=False,
    )
```

```python
import functools

import jax
import jax.numpy as jnp
from jax import lax
from jax.experimental import pallas as pl
from jax.experimental.pallas import tpu as pltpu
from jax.sharding import PartitionSpec as P

KD = 256
VD = 512
CHUNK = 256


eps_layer = 1e-05
eps_group = 1e-06
low = jnp.bfloat16
wide = jnp.float32


def mask_of(slot, count):
    bits = count.bit_length() - 1
    return ((slot << 1) & (count - 1)) | (slot >> (bits - 1))


def slot_of(mask, count):
    bits = count.bit_length() - 1
    return (mask >> 1) | ((mask & 1) << (bits - 1))


def flip(value, mask):
    count = lax.axis_size("sq")
    return lax.ppermute(value, "sq", [(i, i ^ mask) for i in range(count)])


def route(swapped):
    count = lax.axis_size("sq")
    lower = list(range(count.bit_length() - 2))
    return lower[::-1] if swapped else lower


def own_order(values):
    count = lax.axis_size("sq")
    width = values.shape[-1] // count
    place = lax.axis_index("sq")
    return jnp.concatenate(
        [
            lax.dynamic_slice_in_dim(values, (place ^ mask_of(s, count)) * width, width, -1)
            for s in range(count)
        ],
        axis=-1,
    )


def true_order(values):
    count = lax.axis_size("sq")
    width = values.shape[-1] // count
    place = lax.axis_index("sq")
    return jnp.concatenate(
        [
            lax.dynamic_slice_in_dim(values, slot_of(place ^ b, count) * width, width, -1)
            for b in range(count)
        ],
        axis=-1,
    )


class Box:
    def __init__(self, value):
        self.value = value

    def get(self):
        return [self.value]

    def put(self, values):
        (self.value,) = values


class Many:
    def __init__(self, *values):
        self.value = list(values)

    def get(self):
        return self.value

    def put(self, values):
        self.value = list(values)


class Gather:
    def __init__(self, *shards):
        self.count = lax.axis_size("sq")
        self.top = self.count // 2
        self.pieces = [{0: shard} for shard in shards]
        self.far = []
        self.staged = None
        self.todo = []
        for swapped in (False, True):
            slots, units = [0], []
            for bit in route(swapped):
                units += [(s, bit) for s in slots]
                slots += [s | 1 << bit for s in slots]
            self.todo.append(units)

    def send(self, times=1):
        for k, held in enumerate(self.pieces):
            for slot, bit in self.todo[k][:times]:
                held[slot | 1 << bit] = flip(held[slot], mask_of(1 << bit, self.count))
            self.todo[k] = self.todo[k][times:]

    def rest(self):
        self.send(len(self.todo[0]))

    def rest_grouped(self):
        for k, held in enumerate(self.pieces):
            while self.todo[k]:
                bit = self.todo[k][0][1]
                slots = [s for s, b in self.todo[k] if b == bit]
                self.todo[k] = self.todo[k][len(slots) :]
                got = flip(stack([held[s] for s in slots]), mask_of(1 << bit, self.count))
                for i, slot in enumerate(slots):
                    held[slot | 1 << bit] = got[i]

    def stage(self):
        sent = [s for slots, _ in self.far for s in slots]
        ready = [s for s in range(self.top) if s not in sent and all(s in h for h in self.pieces)]
        if ready:
            self.staged = ready, stack([held[s] for s in ready for held in self.pieces])

    def core(self):
        if self.staged is None:
            self.stage()
        if self.staged is not None:
            slots, both = self.staged
            self.far.append((slots, flip(both, mask_of(self.top, self.count))))
            self.staged = None

    def finish(self):
        self.rest()
        self.core()
        self.core()

    def refs(self):
        operands = [held[s] for held in self.pieces for s in range(self.top)]
        places = [[(k * self.top + s, None) for s in range(self.top)] for k in range(2)]
        for k in range(2):
            for s in range(self.top):
                for g, (slots, _) in enumerate(self.far):
                    if s in slots:
                        places[k].append((2 * self.top + g, 2 * slots.index(s) + k))
        return operands + [array for _, array in self.far], places

    def get(self):
        near = [held[s] for held in self.pieces for s in sorted(held)]
        staged = [] if self.staged is None else [self.staged[1]]
        return near + [array for _, array in self.far] + staged

    def put(self, values):
        values = iter(values)
        self.pieces = [{s: next(values) for s in sorted(held)} for held in self.pieces]
        self.far = [(slots, next(values)) for slots, _ in self.far]
        if self.staged is not None:
            self.staged = self.staged[0], next(values)


class Small:
    def __init__(self, shard):
        self.count = lax.axis_size("sq")
        self.pieces = {0: shard}
        bits = self.count.bit_length() - 1
        self.todo = [bits - 1, *range(bits - 1)]

    def send(self):
        if self.todo:
            bit, self.todo = self.todo[0], self.todo[1:]
            slots = sorted(self.pieces)
            far = flip(jnp.stack([self.pieces[s] for s in slots]), mask_of(1 << bit, self.count))
            for k, s in enumerate(slots):
                self.pieces[s | 1 << bit] = far[k]

    def rest(self):
        while self.todo:
            self.send()

    def get(self):
        return [self.pieces[s] for s in sorted(self.pieces)]

    def put(self, values):
        self.pieces = dict(zip(sorted(self.pieces), values))


class Scatter:
    def __init__(self, lefts, rights, places=None):
        self.count = lax.axis_size("sq")
        top = self.count // 2
        self.rows = lefts[0].shape[1] // self.count
        self.todo = [route(k == 1)[::-1] for k in range(2)]
        self.slots = [list(range(top)) for _ in range(2)]
        self.arrived = False
        self.sources = lefts, rights
        self.places = places
        self.held = [outer_half(lefts, rights, 1, places=places)]

    def core(self):
        self.held = [flip(self.held[0], mask_of(self.count // 2, self.count))]

    def near(self):
        self.held = outer_half(
            *self.sources, 0, self.held[0], self.rows, self.part(), self.places
        )

    def part(self):
        return [[s >> self.todo[k][0] & 1 for s in self.slots[k]] for k in range(2)]

    def send(self, lazy=False):
        self.merge()
        if not self.todo[0]:
            return
        for k in range(2):
            bit, self.todo[k] = self.todo[k][0], self.todo[k][1:]
            self.held[2 * k + 1] = flip(self.held[2 * k + 1], mask_of(1 << bit, self.count))
            self.slots[k] = [s for s in self.slots[k] if not s >> bit & 1]
        self.arrived = True
        if not lazy:
            self.merge()

    def merge(self):
        if self.arrived:
            bits = self.part() if self.todo[0] else None
            self.held = list(split(self.held[::2], self.held[1::2], self.rows, bits))
            self.arrived = False

    def rest(self):
        self.merge()
        while self.todo[0]:
            self.send()
        return self.held

    def get(self):
        return list(self.held)

    def put(self, values):
        self.held = list(values)


def send_together(*sums):
    wanted = {}
    for thing in sums:
        thing.merge()
    sums = [thing for thing in sums if thing.todo[0]]
    for thing in sums:
        for k in range(2):
            wanted.setdefault(thing.todo[k][0], []).append((thing, k))
    for bit, group in wanted.items():
        parts = [thing.held[2 * k + 1] for thing, k in group]
        got = flip(above(parts) if len(parts) > 1 else parts[0], mask_of(1 << bit, sums[0].count))
        begin = 0
        for (thing, k), part in zip(group, parts):
            thing.held[2 * k + 1] = got[begin : begin + part.shape[0]]
            begin += part.shape[0]
            thing.todo[k] = thing.todo[k][1:]
            thing.slots[k] = [s for s in thing.slots[k] if not s >> bit & 1]
    for thing in sums:
        thing.arrived = True
        thing.merge()


def settle(*things):
    values = lax.optimization_barrier(tuple(v for t in things for v in t.get()))
    values = list(values)
    for thing in things:
        size = len(thing.get())
        thing.put(values[:size])
        values = values[size:]


def ring_step(value):
    count = lax.axis_size("head")
    return lax.ppermute(value, "head", [(i, (i + 1) % count) for i in range(count)])


def sum_others(values, axis, masks):
    count = lax.axis_size(axis)
    held = [values]
    held += [lax.ppermute(values, axis, [(i, i ^ m) for i in range(count)]) for m in masks]
    while len(held) > 1:
        held = [a + b for a, b in zip(held[::2], held[1::2])]
    return held[0]


def layer_norm(values, weight_gain, weight_shift):
    centered = values - jnp.mean(values, axis=-1, keepdims=True)
    spread = lax.rsqrt(jnp.mean(centered * centered, axis=-1, keepdims=True) + eps_layer)
    return centered * spread * weight_gain + weight_shift


def gelu_gate(pre_gate, pre_up):
    return jax.nn.gelu(pre_gate) * pre_up


def log_decay(first_head, head_count):
    head_ids = (first_head + jnp.arange(head_count)).astype(jnp.float32)
    return jnp.log(1.0 - jnp.exp2(-5.0 - head_ids))


def project(left_side, right_side):
    return jnp.dot(left_side, right_side, preferred_element_type=jnp.float32)


def outer_sum(left_side, right_side):
    return lax.dot_general(
        left_side, right_side, (((0,), (0,)), ((), ())), preferred_element_type=jnp.float32
    )


def back_project(gradient, weight):
    return lax.dot_general(
        gradient, weight, (((1,), (1,)), ((), ())), preferred_element_type=jnp.float32
    )


def swap_head(value, mask):
    count = lax.axis_size("head")
    return lax.ppermute(value, "head", [(i, i ^ mask) for i in range(count)])


def stack_kernel(*refs):
    for k, ref in enumerate(refs[:-1]):
        refs[-1][k] = ref[...]


def stack(pieces):
    vmem = pl.BlockSpec(memory_space=pltpu.VMEM)
    return pl.pallas_call(
        stack_kernel,
        in_specs=[vmem] * len(pieces),
        out_specs=vmem,
        out_shape=jax.ShapeDtypeStruct((len(pieces),) + pieces[0].shape, pieces[0].dtype),
        compiler_params=pltpu.CompilerParams(vmem_limit_bytes=16 * 2**20),
        cost_estimate=brief,
    )(*pieces)


def beside_kernel(*refs):
    begin = 0
    for ref in refs[:-1]:
        refs[-1][:, pl.ds(begin, ref.shape[1])] = ref[...]
        begin += ref.shape[1]


def beside(pieces):
    vmem = pl.BlockSpec(memory_space=pltpu.VMEM)
    columns = sum(p.shape[1] for p in pieces)
    return pl.pallas_call(
        beside_kernel,
        in_specs=[vmem] * len(pieces),
        out_specs=vmem,
        out_shape=jax.ShapeDtypeStruct((pieces[0].shape[0], columns), pieces[0].dtype),
        compiler_params=pltpu.CompilerParams(vmem_limit_bytes=16 * 2**20),
        cost_estimate=brief,
    )(*pieces)


def above_kernel(*refs):
    begin = 0
    for ref in refs[:-1]:
        refs[-1][pl.ds(begin, ref.shape[0]), :] = ref[...]
        begin += ref.shape[0]


def above(pieces):
    vmem = pl.BlockSpec(memory_space=pltpu.VMEM)
    rows = sum(p.shape[0] for p in pieces)
    return pl.pallas_call(
        above_kernel,
        in_specs=[vmem] * len(pieces),
        out_specs=vmem,
        out_shape=jax.ShapeDtypeStruct((rows, pieces[0].shape[1]), pieces[0].dtype),
        compiler_params=pltpu.CompilerParams(vmem_limit_bytes=16 * 2**20),
        cost_estimate=brief,
    )(*pieces)


def add_rows_kernel(whole_ref, got_ref, out_ref):
    total = whole_ref[...].astype(wide) + got_ref[...].astype(wide)
    out_ref[...] = total.astype(out_ref.dtype)


def add_rows(whole, place, got, kind):
    rows, columns = got.shape
    block = min(columns, 1024)
    part = pl.BlockSpec((rows, block), lambda j: (0, j))
    return call(
        add_rows_kernel,
        (columns // block,),
        in_specs=[pl.BlockSpec((rows, block), lambda j: (place, j)), part],
        out_specs=part,
        out_shape=jax.ShapeDtypeStruct(got.shape, kind),
    )(whole, got)


def split_kernel(rows, bits, *refs):
    ins, outs = refs[:4], refs[4:]
    for k in range(2):
        kept, got = ins[2 * k : 2 * k + 2]
        total = kept[...].astype(wide) + got[...].astype(wide)
        if bits is None:
            outs[k][...] = total
        else:
            taken = [0, 0]
            for i, side in enumerate(bits[k]):
                place = pl.ds(taken[side] * rows, rows)
                outs[2 * k + side][place, :] = total[i * rows : (i + 1) * rows].astype(low)
                taken[side] += 1


def split(kept, got, rows, bits):
    size, columns = kept[0].shape
    block = 512 if columns % 512 == 0 else 256
    part = pl.BlockSpec((size, block), lambda j: (0, j))
    half = pl.BlockSpec((size // 2, block), lambda j: (0, j))
    if bits is None:
        out_specs = [part] * 2
        out_shape = [jax.ShapeDtypeStruct((size, columns), wide)] * 2
    else:
        out_specs = [half] * 4
        out_shape = [jax.ShapeDtypeStruct((size // 2, columns), low)] * 4
    return call(
        functools.partial(split_kernel, rows, bits),
        (columns // block,),
        in_specs=[part] * 4,
        out_specs=out_specs,
        out_shape=out_shape,
    )(kept[0], got[0], kept[1], got[1])


def combine_kernel(heads, places, factor_ref, *refs):
    *piece_refs, total_ref = refs
    size = heads * KD // 2
    for part in range(2):
        for begin in range(0, size, KD // 2):
            h, row = divmod(part * size + begin, KD)
            rows = pl.ds(begin, KD // 2)
            total = jnp.zeros((KD // 2, VD), wide)
            for k, (operand, index) in enumerate(places[part][1:]):
                ref = piece_refs[operand]
                piece = ref[rows, :] if index is None else ref[index, rows, :]
                total = total + factor_ref[k * heads + h] * piece.astype(wide)
            total_ref[h, pl.ds(row, KD // 2), :] = total


def combine(gather, log_rate, length, backward):
    count = lax.axis_size("sq")
    place = lax.axis_index("sq")
    heads = log_rate.shape[0]
    factors = []
    for slot in range(1, count):
        other = place ^ mask_of(slot, count)
        ahead = (other - place) if backward else (place - other)
        between = jnp.maximum(ahead - 1, 0).astype(wide) * length
        factors.append(jnp.where(ahead > 0, jnp.exp(log_rate * between), 0.0))
    operands, places = gather.refs()
    vmem = pl.BlockSpec(memory_space=pltpu.VMEM)
    return pl.pallas_call(
        functools.partial(combine_kernel, heads, places),
        in_specs=[smem] + [vmem] * len(operands),
        out_specs=vmem,
        out_shape=jax.ShapeDtypeStruct((heads, KD, VD), wide),
        compiler_params=pltpu.CompilerParams(vmem_limit_bytes=56 * 2**20),
        cost_estimate=brief,
    )(jnp.concatenate(factors), *operands)


def call(kernel, grid, grant=20, **options):
    return pl.pallas_call(
        kernel,
        grid=grid,
        cost_estimate=brief,
        compiler_params=pltpu.CompilerParams(
            dimension_semantics=("arbitrary",) * len(grid), vmem_limit_bytes=grant * 2**20
        ),
        **options,
    )


def dot(left_side, right_side, left_dim=1, right_dim=0):
    return lax.dot_general(
        left_side,
        right_side,
        (((left_dim,), (right_dim,)), ((), ())),
        preferred_element_type=wide,
    )


smem = pl.BlockSpec(memory_space=pltpu.SMEM)


def reach_of(rate):
    place = lax.broadcasted_iota(jnp.int32, (CHUNK, 1), 0).astype(wide)
    return jnp.exp(rate * (place + 1.0))


def tail_of(rate):
    place = lax.broadcasted_iota(jnp.int32, (CHUNK, 1), 0).astype(wide)
    return jnp.exp(rate * (CHUNK - 1.0 - place))


def decay_of(rate):
    row = lax.broadcasted_iota(jnp.int32, (CHUNK, CHUNK), 0)
    column = lax.broadcasted_iota(jnp.int32, (CHUNK, CHUNK), 1)
    spacing = (row - column).astype(wide)
    return jnp.where(spacing >= 0, jnp.exp(rate * jnp.maximum(spacing, 0.0)), 0.0)


brief = pl.CostEstimate(flops=1, bytes_accessed=1, transcendentals=0)


def bring(copies):
    for copy in copies:
        copy.start()
    return copies


def bring_pieces(refs, places, whole, sems, first):
    rows = whole.shape[0] // len(places)
    return bring(
        [
            pltpu.make_async_copy(
                refs[operand] if index is None else refs[operand].at[index],
                whole.at[pl.ds(k * rows, rows), :],
                sems.at[first + k],
            )
            for k, (operand, index) in enumerate(places)
        ]
    )


def wait_all(copies):
    for copy in copies:
        copy.wait()


def project_blocks(left, weight, product_ref):
    block = 256

    def one(j, carry):
        columns = pl.ds(pl.multiple_of(j * block, block), block)
        product_ref[:, columns] = dot(left[...], weight[:, columns]).astype(low)
        return carry

    lax.fori_loop(0, product_ref.shape[1] // block, one, 0)


def norm_project_kernel(count, slots, places, order, start, *refs):
    row_refs = refs[:slots]
    norm_ref = refs[slots]
    piece_refs = refs[slots + 1 : -8]
    normed_ref, xhat_ref, product_ref, full_ref, weight, normed, xhat, sems = refs[-8:]
    width = normed.shape[1] // count
    size = row_refs[0].shape[0]
    tile = 64
    copies = bring_pieces(piece_refs, places, weight, sems, 0)
    for turn, ref in enumerate(row_refs):

        def tile_of(t, carry, ref=ref, turn=turn):
            rows = pl.ds(pl.multiple_of(t * tile, tile), tile)
            values = [
                ref[rows, pl.ds(pl.multiple_of(order[s] * width, width), width)].astype(wide)
                for s in range(count)
            ]
            total = values[0]
            for v in values[1:]:
                total = total + v
            mean = jnp.sum(total, axis=1, keepdims=True) / (count * width)
            values = [v - mean for v in values]
            square = values[0] * values[0]
            for v in values[1:]:
                square = square + v * v
            square = jnp.sum(square, axis=1, keepdims=True)
            spread = lax.rsqrt(square / (count * width) + eps_layer)
            target = pl.ds(pl.multiple_of(start[turn] + t * tile, tile), tile)
            for s in range(count):
                columns = pl.ds(s * width, width)
                scaled = values[s] * spread
                xhat[target, columns] = scaled.astype(low)
                normed[target, columns] = (
                    scaled * norm_ref[0:1, columns] + norm_ref[1:2, columns]
                ).astype(low)
            return carry

        lax.fori_loop(0, size // tile, tile_of, 0)

    away = bring(
        [
            pltpu.make_async_copy(normed, normed_ref, sems.at[count]),
            pltpu.make_async_copy(xhat, xhat_ref, sems.at[count + 1]),
        ]
    )
    wait_all(copies)
    away += bring([pltpu.make_async_copy(weight, full_ref, sems.at[count + 2])])
    project_blocks(normed, weight, product_ref)
    wait_all(away)


def norm_project(slots, norms, gather, columns, order, start):
    count = gather.count
    pieces, places = gather.refs()
    size, depth = slots[0].shape
    length = size * len(slots)
    width = pieces[0].shape[1]
    vmem = pl.BlockSpec(memory_space=pltpu.VMEM)
    whole = pl.BlockSpec(memory_space=pl.ANY)
    return pl.pallas_call(
        functools.partial(norm_project_kernel, count, len(slots), places[0]),
        in_specs=[smem, smem] + [vmem] * (len(slots) + 1) + [whole] * len(pieces),
        out_specs=[whole, whole, vmem, whole],
        out_shape=[
            jax.ShapeDtypeStruct((length, depth), low),
            jax.ShapeDtypeStruct((length, depth), low),
            jax.ShapeDtypeStruct((length, columns), low),
            jax.ShapeDtypeStruct((depth, width), low),
        ],
        scratch_shapes=[
            pltpu.VMEM((depth, width), low),
            pltpu.VMEM((length, depth), low),
            pltpu.VMEM((length, depth), low),
            pltpu.SemaphoreType.DMA((count + 3,)),
        ],
        compiler_params=pltpu.CompilerParams(vmem_limit_bytes=36 * 2**20),
        cost_estimate=brief,
    )(order, start, *slots, norms, *pieces)


def project_kernel(count, places, left_ref, *refs):
    product_ref, full_ref, weight, sems = refs[-4:]
    wait_all(bring_pieces(refs[:-4], places, weight, sems, 0))
    away = bring([pltpu.make_async_copy(weight, full_ref, sems.at[count])])
    project_blocks(left_ref, weight, product_ref)
    wait_all(away)


def project_pieces(left_side, gather, columns):
    length, depth = left_side.shape
    count = gather.count
    pieces, places = gather.refs()
    width = pieces[0].shape[1]
    vmem = pl.BlockSpec(memory_space=pltpu.VMEM)
    whole = pl.BlockSpec(memory_space=pl.ANY)
    return pl.pallas_call(
        functools.partial(project_kernel, count, places[1]),
        in_specs=[vmem] + [whole] * len(pieces),
        out_specs=[vmem, whole],
        out_shape=[
            jax.ShapeDtypeStruct((length, columns), low),
            jax.ShapeDtypeStruct((depth, width), low),
        ],
        scratch_shapes=[pltpu.VMEM((depth, width), low), pltpu.SemaphoreType.DMA((count + 1,))],
        compiler_params=pltpu.CompilerParams(vmem_limit_bytes=20 * 2**20),
        cost_estimate=brief,
    )(left_side, *pieces)


def feed_kernel(top, quarter, places, sizes, has_prior, second_ref, cot_ref, *refs):
    quarters = len(places)
    piece_refs = []
    for size in sizes:
        piece_refs.append(refs[:size])
        refs = refs[size:]
    if has_prior:
        prior_grad, prior_down, *refs = refs
    hidden_refs = [refs[2 * t : 2 * t + 2] for t in range(quarters)]
    grad_ref, down_part_ref = refs[2 * quarters : 2 * quarters + 2]
    first, later, gate_pre, up_pre, grad_inner, sums, sems = refs[2 * quarters + 2 :]
    rows, depth = second_ref.shape
    middle = quarter // 2
    hidden = pl.ds(0, quarter)
    hidden_up = pl.ds(quarter, quarter)
    down = pl.ds(quarter, middle)
    sides = [pl.ds(0, middle), pl.ds(middle, middle)]
    halves = [pl.ds(0, depth // 2), pl.ds(depth // 2, depth // 2)]
    copies = []
    for t in range(quarters):
        for k, whole in enumerate((first, later)):
            index = (t * 2 + k) * 2 * top
            some = bring_pieces(piece_refs[t], places[t][k], whole.at[t], sems, index)
            copies += [some[:top], some[top:]]
    tile = 16
    scale = 0.7978845608028654
    for t in range(quarters):
        inner_ref, grads_ref = hidden_refs[t]
        for k, (whole, target) in enumerate(((first, gate_pre), (later, up_pre))):
            for h in range(2):
                wait_all(copies[(t * 2 + k) * 2 + h])
                part = dot(second_ref[:, halves[h]], whole[t, halves[h], hidden])
                side = dot(cot_ref[:, halves[h]], whole[t, halves[h], down])
                target[...] = part if h == 0 else target[...] + part
                grad_inner[:, sides[k]] = side if h == 0 else grad_inner[:, sides[k]] + side

        def activate(i, carry, inner_ref=inner_ref, grads_ref=grads_ref):
            at = pl.ds(pl.multiple_of(i * tile, tile), tile)
            v, u, g = gate_pre[at, :], up_pre[at, :], grad_inner[at, :]
            square = v * v
            bent = jnp.tanh(scale * v * (1.0 + 0.044715 * square))
            shared = 0.5 * (1.0 + bent)
            gelu = v * shared
            slope = shared + (0.5 * scale) * v * (1.0 - bent * bent) * (1.0 + 0.134145 * square)
            inner_ref[at, :] = (gelu * u).astype(low)
            grads_ref[at, hidden] = (g * u * slope).astype(low)
            grads_ref[at, hidden_up] = (g * gelu).astype(low)
            return carry

        lax.fori_loop(0, rows // tile, activate, 0)
        for half in halves:
            grad = dot(grads_ref[:, hidden], first[t, half, hidden], 1, 1)
            grad = grad + dot(grads_ref[:, hidden_up], later[t, half, hidden], 1, 1)
            down_part = dot(inner_ref[:, sides[0]], first[t, half, down], 1, 1)
            down_part = down_part + dot(inner_ref[:, sides[1]], later[t, half, down], 1, 1)
            if t > 0:
                grad = grad + sums[0, :, half]
                down_part = down_part + sums[1, :, half]
            elif has_prior:
                grad = grad + prior_grad[:, half]
                down_part = down_part + prior_down[:, half]
            if t < quarters - 1:
                sums[0, :, half] = grad
                sums[1, :, half] = down_part
            else:
                grad_ref[:, half] = grad.astype(grad_ref.dtype)
                down_part_ref[:, half] = down_part.astype(down_part_ref.dtype)


def feed_part(second, cot, gathers, quarter, prior, kind):
    top = gathers[0].top
    quarters = len(gathers)
    rows, depth = second.shape
    pieces, places, sizes = [], [], []
    for gather in gathers:
        operands, where = gather.refs()
        pieces += operands
        places.append(where)
        sizes.append(len(operands))
    width = pieces[0].shape[1]
    vmem = pl.BlockSpec(memory_space=pltpu.VMEM)
    out = jax.ShapeDtypeStruct((rows, depth), kind)
    hidden = [
        jax.ShapeDtypeStruct((rows, quarter), low),
        jax.ShapeDtypeStruct((rows, 2 * quarter), low),
    ]
    return pl.pallas_call(
        functools.partial(feed_kernel, top, quarter, places, sizes, bool(prior)),
        in_specs=[vmem] * 2
        + [pl.BlockSpec(memory_space=pl.ANY)] * len(pieces)
        + [vmem] * len(prior),
        out_specs=[vmem] * (2 * quarters + 2),
        out_shape=hidden * quarters + [out, out],
        scratch_shapes=[
            pltpu.VMEM((quarters, depth, width), low),
            pltpu.VMEM((quarters, depth, width), low),
            pltpu.VMEM((rows, quarter), wide),
            pltpu.VMEM((rows, quarter), wide),
            pltpu.VMEM((rows, quarter), wide),
            pltpu.VMEM((2, rows, depth), wide),
            pltpu.SemaphoreType.DMA((4 * top * quarters,)),
        ],
        compiler_params=pltpu.CompilerParams(vmem_limit_bytes=(22 + 12 * quarters) * 2**20),
        cost_estimate=brief,
    )(second, cot, *pieces, *prior)


def outer_kernel(count, added, rows, bits, *refs):
    lefts, rights, refs = refs[:count], refs[count : 2 * count], refs[2 * count :]
    got = refs[0] if added else None
    outs, flipped = refs[added:-1], refs[-1]
    turn = pl.program_id(0)
    starts = [sum(ref.shape[0] for ref in lefts[:i]) for i in range(count)]

    @pl.when(turn == 0)
    def _():
        for begin, ref in zip(starts, lefts):
            flipped[:, pl.ds(begin, ref.shape[0])] = ref[...].T

    total = 0.0
    for begin, ref in zip(starts, rights):
        total = total + dot(flipped[:, pl.ds(begin, ref.shape[0])], ref[...])
    if added:
        total = total + got[...].astype(wide)
    if bits is None:
        outs[0][...] = total.astype(low)
    else:
        for k in range(2):

            @pl.when(turn // (pl.num_programs(0) // 2) == k)
            def _(k=k):
                taken = [0, 0]
                for i, side in enumerate(bits[k]):
                    place = pl.ds(taken[side] * rows, rows)
                    outs[2 * k + side][place, :] = total[i * rows : (i + 1) * rows].astype(low)
                    taken[side] += 1


def outer_half(lefts, rights, part, got=None, rows=None, bits=None, places=None):
    depth = lefts[0].shape[1] // 2
    columns = rights[0].shape[1]
    block = 512 if columns % 1024 == 0 else 256
    blocks = columns // block
    whole = pl.BlockSpec((depth, block), lambda j, p: (0, j))
    extra = [] if got is None else [got]
    if bits is None:
        out_specs, out_shape = [whole], [jax.ShapeDtypeStruct((depth, columns), low)]
    else:
        early = pl.BlockSpec((depth // 2, block), lambda j, p: (0, jnp.minimum(j, blocks // 2 - 1)))
        late = pl.BlockSpec((depth // 2, block), lambda j, p: (0, jnp.maximum(j - blocks // 2, 0)))
        out_specs = [early, early, late, late]
        out_shape = [jax.ShapeDtypeStruct((depth // 2, columns // 2), low)] * 4
    if places is None:
        places = jnp.zeros(len(lefts), jnp.int32)
    kernel = functools.partial(outer_kernel, len(lefts), len(extra), rows, bits)
    result = pl.pallas_call(
        lambda place_ref, *refs: kernel(*refs),
        grid_spec=pltpu.PrefetchScalarGridSpec(
            num_scalar_prefetch=1,
            grid=(blocks,),
            in_specs=[pl.BlockSpec((v.shape[0], depth), lambda j, p: (0, part)) for v in lefts]
            + [
                pl.BlockSpec((v.shape[0], block), lambda j, p, i=i: (p[i], j))
                for i, v in enumerate(lefts)
            ]
            + [whole] * len(extra),
            out_specs=out_specs,
            scratch_shapes=[pltpu.VMEM((depth, sum(v.shape[0] for v in lefts)), low)],
        ),
        out_shape=out_shape,
        compiler_params=pltpu.CompilerParams(vmem_limit_bytes=20 * 2**20),
        cost_estimate=brief,
    )(places, *lefts, *rights, *extra)
    return result[0] if bits is None else list(result)


def rows_kernel(parts, sides, sums, size, begin_ref, *refs):
    lefts = [refs[p * sides : (p + 1) * sides] for p in range(parts)]
    refs = refs[parts * sides :]
    xhats, weights, out_ref = refs[: parts * sums], refs[parts * sums :][:sides], refs[parts * sums + sides]
    for p in range(parts):
        part = dot(lefts[p][0][...], weights[0][...], 1, 1)
        for k in range(1, sides):
            part = part + dot(lefts[p][k][...], weights[k][...], 1, 1)
        out_ref[pl.ds(p * size, size), :] = part.astype(out_ref.dtype)
        if sums:
            sums_ref = refs[-1]
            gain = jnp.sum(part * xhats[p][...].astype(wide), axis=0, keepdims=True)
            shift = jnp.sum(part, axis=0, keepdims=True)
            sums_ref[0:1, :] = gain if p == 0 else sums_ref[0:1, :] + gain
            sums_ref[1:2, :] = shift if p == 0 else sums_ref[1:2, :] + shift


def rows_back(lefts, weights, begins, size, xhat=None):
    depth = weights[0][0].shape[0]
    block = 512
    parts, sides = len(begins), len(lefts)
    in_specs, operands = [], []
    for p in range(parts):
        for (left, column), (_, _, columns) in zip(lefts, weights):
            in_specs.append(pl.BlockSpec((size, columns), lambda j, b, p=p, column=column: (b[p], column)))
            operands.append(left)
    if xhat is not None:
        for p in range(parts):
            in_specs.append(pl.BlockSpec((size, block), lambda j, b, p=p: (b[p], j)))
            operands.append(xhat)
    for weight, column, columns in weights:
        in_specs.append(pl.BlockSpec((block, columns), lambda j, b, column=column: (j, column)))
        operands.append(weight)
    out_specs = [pl.BlockSpec((parts * size, block), lambda j, b: (0, j))]
    out_shape = [jax.ShapeDtypeStruct((parts * size, depth), low)]
    if xhat is not None:
        out_specs.append(pl.BlockSpec((2, block), lambda j, b: (0, j)))
        out_shape.append(jax.ShapeDtypeStruct((2, depth), wide))
    return pl.pallas_call(
        functools.partial(rows_kernel, parts, sides, int(xhat is not None), size),
        grid_spec=pltpu.PrefetchScalarGridSpec(
            num_scalar_prefetch=1, grid=(depth // block,), in_specs=in_specs, out_specs=out_specs
        ),
        out_shape=out_shape,
        compiler_params=pltpu.CompilerParams(vmem_limit_bytes=56 * 2**20),
        cost_estimate=brief,
    )(jnp.stack(begins) // size, *operands)


def parts_of(heads):
    values = [pl.ds(h * VD, VD) for h in range(heads)]
    keys = [pl.ds(heads * VD + h * KD, KD) for h in range(heads)]
    return values, keys


def state_halves(state, heads, refs):
    if heads == 2:
        for h in range(2):
            refs[h][...] = state[h].astype(low)
    else:
        for k in range(2):
            refs[k][...] = state[0, pl.ds(k * KD // 2, KD // 2), :].astype(low)


def state_kernel(heads, chunks, rate_ref, kv_ref, one_ref, two_ref, state):
    values, keys = parts_of(heads)
    turn = pl.program_id(0)

    @pl.when(turn == 0)
    def _():
        state[...] = jnp.zeros_like(state)

    for h in range(heads):
        rate = rate_ref[h]
        scaled = (kv_ref[:, keys[h]].astype(wide) * tail_of(rate)).astype(low)
        kept = state[h] * jnp.exp(jnp.full((1, 1), rate * CHUNK, wide))
        state[h] = kept + dot(scaled, kv_ref[:, values[h]], 0, 0)

    @pl.when(turn == chunks - 1)
    def _():
        state_halves(state, heads, [one_ref, two_ref])


def final_state(kv, log_rate, heads):
    length, columns = kv.shape
    chunks = length // CHUNK
    half = jax.ShapeDtypeStruct((heads * KD // 2, VD), low)
    return call(
        functools.partial(state_kernel, heads, chunks),
        (chunks,),
        in_specs=[smem, pl.BlockSpec((CHUNK, columns), lambda c: (c, 0))],
        out_specs=[pl.BlockSpec(half.shape, lambda c: (0, 0))] * 2,
        out_shape=[half, half],
        scratch_shapes=[pltpu.VMEM((heads, KD, VD), wide)],
    )(log_rate, kv)


def retain_kernel(
    heads, rate_ref, kv_ref, qs_ref, first_ref, gated_ref, grouped_ref, factor_ref, states_ref, held, table
):
    values, keys = parts_of(heads)

    @pl.when(pl.program_id(0) == 0)
    def _():
        held[...] = first_ref[...]
        for h in range(heads):
            table[h] = decay_of(rate_ref[h])

    for h in range(heads):
        rate = rate_ref[h]
        query, key = qs_ref[:, keys[h]], kv_ref[:, keys[h]]
        value = kv_ref[:, values[h]]
        state = held[h]
        state_low = state.astype(low)
        states_ref[0, h] = state_low
        mixing = (dot(query, key, 1, 1) * table[h]).astype(low)
        retained = dot(mixing, value) + reach_of(rate) * dot(query, state_low)
        scaled = (key.astype(wide) * tail_of(rate)).astype(low)
        held[h] = state * jnp.exp(jnp.full((1, 1), rate * CHUNK, wide)) + dot(scaled, value, 0, 0)
        factor = lax.rsqrt(jnp.mean(retained * retained, axis=1, keepdims=True) + eps_group)
        grouped = (retained * factor).astype(low)
        factor_ref[h] = factor
        grouped_ref[:, values[h]] = grouped
        pre = qs_ref[:, values[h]].astype(wide)
        gated_ref[:, values[h]] = (grouped.astype(wide) * (pre * jax.nn.sigmoid(pre))).astype(low)


def retain(kv, qs, first, log_rate, heads):
    length, columns = kv.shape
    chunks = length // CHUNK
    rows = pl.BlockSpec((CHUNK, columns), lambda c: (c, 0))
    out = pl.BlockSpec((CHUNK, heads * VD), lambda c: (c, 0))
    return call(
        functools.partial(retain_kernel, heads),
        (chunks,),
        56,
        in_specs=[smem, rows, rows, pl.BlockSpec((heads, KD, VD), lambda c: (0, 0, 0))],
        out_specs=[
            out,
            out,
            pl.BlockSpec((heads, CHUNK, 1), lambda c: (0, c, 0)),
            pl.BlockSpec((1, heads, KD, VD), lambda c: (c, 0, 0, 0)),
        ],
        out_shape=[
            jax.ShapeDtypeStruct((length, heads * VD), low),
            jax.ShapeDtypeStruct((length, heads * VD), low),
            jax.ShapeDtypeStruct((heads, length, 1), wide),
            jax.ShapeDtypeStruct((chunks, heads, KD, VD), low),
        ],
        scratch_shapes=[pltpu.VMEM((heads, KD, VD), wide), pltpu.VMEM((heads, CHUNK, CHUNK), wide)],
    )(log_rate, kv, qs, first)


def gate_back_kernel(
    heads, first, last, place_ref, rate_ref, branch_ref, left_ref, right_ref, grouped_ref, factor_ref, qs_ref, *refs
):
    values, keys = parts_of(heads)
    if not first:
        _, _, prior_ref, *refs = refs
    swish_ref, retained_ref, *halves, crossed_ref = refs
    start = (place_ref[0] * CHUNK).astype(wide)
    sides = [dot(branch_ref[...], ref[...]) for ref in (left_ref, right_ref)]
    gated = sides if heads == 2 else [jnp.concatenate(sides, axis=1)]
    for h in range(heads):
        rate = rate_ref[h]
        gated_grad = gated[h]
        grouped = grouped_ref[:, values[h]].astype(wide)
        pre = qs_ref[:, values[h]].astype(wide)
        sigma = jax.nn.sigmoid(pre)
        swish_ref[:, values[h]] = (
            gated_grad * grouped * (sigma * (1.0 + pre * (1.0 - sigma)))
        ).astype(low)
        grouped_grad = (gated_grad * (pre * sigma)).astype(low).astype(wide)
        factor = factor_ref[h]
        mean = jnp.mean(grouped_grad * grouped, axis=1, keepdims=True)
        retained_grad = (factor * (grouped_grad - grouped * mean)).astype(low)
        retained_ref[:, values[h]] = retained_grad
        scale = reach_of(rate) * jnp.exp(jnp.full((1, 1), rate * start, wide))
        scaled = (qs_ref[:, keys[h]].astype(wide) * scale).astype(low)
        crossed = dot(scaled, retained_grad, 0, 0)
        crossed_ref[h] = crossed if first else prior_ref[h] + crossed
    if last:
        state_halves(crossed_ref, heads, halves)


def gate_back(branch, left, right, column, grouped, factor, qs, log_rate, heads, place, prior, last):
    length, columns = qs.shape
    depth = branch.shape[1]
    part = pl.BlockSpec((CHUNK, heads * VD), lambda i, p: (p[0], 0))
    total = pl.BlockSpec((heads, KD, VD), lambda i, p: (0, 0, 0))
    whole = pl.BlockSpec(memory_space=pl.ANY)
    half = pl.BlockSpec((heads * KD // 2, VD), lambda i, p: (0, 0))
    grid_spec = pltpu.PrefetchScalarGridSpec(
        num_scalar_prefetch=1,
        grid=(1,),
        in_specs=[
            smem,
            pl.BlockSpec((CHUNK, depth), lambda i, p: (0, 0)),
            pl.BlockSpec((depth, heads * VD // 2), lambda i, p: (0, column)),
            pl.BlockSpec((depth, heads * VD // 2), lambda i, p: (0, column)),
            part,
            pl.BlockSpec((heads, CHUNK, 1), lambda i, p: (0, p[0], 0)),
            pl.BlockSpec((CHUNK, columns), lambda i, p: (p[0], 0)),
        ]
        + [whole, whole, total][: len(prior)],
        out_specs=[part, part] + ([half] * 2 if last else [total]),
        scratch_shapes=[pltpu.VMEM((heads, KD, VD), wide)] if last else [],
    )
    return pl.pallas_call(
        functools.partial(gate_back_kernel, heads, not prior, last),
        grid_spec=grid_spec,
        out_shape=[
            jax.ShapeDtypeStruct((length, heads * VD), low),
            jax.ShapeDtypeStruct((length, heads * VD), low),
        ]
        + (
            [jax.ShapeDtypeStruct((heads * KD // 2, VD), low)] * 2
            if last
            else [jax.ShapeDtypeStruct((heads, KD, VD), wide)]
        ),
        input_output_aliases={8: 0, 9: 1} if prior else {},
        compiler_params=pltpu.CompilerParams(vmem_limit_bytes=56 * 2**20),
        cost_estimate=brief,
    )(place.reshape(1), log_rate, branch, left, right, grouped, factor, qs, *prior)


def retain_back_kernel(
    heads, rate_ref, kv_ref, qs_ref, grad_ref, states_ref, last_ref, back_ref, held, table
):
    values, keys = parts_of(heads)
    queries = [pl.ds(heads * (VD + KD) + h * KD, KD) for h in range(heads)]

    @pl.when(pl.program_id(0) == 0)
    def _():
        held[...] = last_ref[...]
        for h in range(heads):
            table[h] = decay_of(rate_ref[h])

    for h in range(heads):
        rate = rate_ref[h]
        query, key = qs_ref[:, keys[h]], kv_ref[:, keys[h]]
        value, grad = kv_ref[:, values[h]], grad_ref[:, values[h]]
        decay = table[h]
        reach, tail = reach_of(rate), tail_of(rate)
        later = held[h]
        later_low = later.astype(low)
        mixing = (dot(query, key, 1, 1) * decay).astype(low)
        scores_grad = (dot(grad, value, 1, 1) * decay).astype(low)
        back_ref[:, queries[h]] = (
            dot(scores_grad, key) + reach * dot(grad, states_ref[0, h], 1, 1)
        ).astype(low)
        back_ref[:, keys[h]] = (
            dot(scores_grad, query, 0, 0) + tail * dot(value, later_low, 1, 1)
        ).astype(low)
        back_ref[:, values[h]] = (
            dot(mixing, grad, 0, 0) + tail * dot(key, later_low)
        ).astype(low)
        scaled = (query.astype(wide) * reach).astype(low)
        held[h] = later * jnp.exp(jnp.full((1, 1), rate * CHUNK, wide)) + dot(scaled, grad, 0, 0)


def retain_back(kv, qs, retained_grad, states, last, log_rate, heads):
    length, columns = kv.shape
    chunks = length // CHUNK
    rows = pl.BlockSpec((CHUNK, columns), lambda c: (chunks - 1 - c, 0))
    part = pl.BlockSpec((CHUNK, heads * VD), lambda c: (chunks - 1 - c, 0))
    return call(
        functools.partial(retain_back_kernel, heads),
        (chunks,),
        56,
        in_specs=[
            smem,
            rows,
            rows,
            part,
            pl.BlockSpec((1, heads, KD, VD), lambda c: (chunks - 1 - c, 0, 0, 0)),
            pl.BlockSpec((heads, KD, VD), lambda c: (0, 0, 0)),
        ],
        out_specs=pl.BlockSpec((CHUNK, columns + heads * KD), lambda c: (chunks - 1 - c, 0)),
        out_shape=jax.ShapeDtypeStruct((length, columns + heads * KD), low),
        scratch_shapes=[pltpu.VMEM((heads, KD, VD), wide), pltpu.VMEM((heads, CHUNK, CHUNK), wide)],
    )(log_rate, kv, qs, retained_grad, states, last)


def shards(
    layer_in,
    norm1_gain,
    norm1_bias,
    w_query,
    w_key,
    w_value,
    w_swish,
    w_out,
    norm2_gain,
    norm2_bias,
    w_gate,
    w_up,
    w_down,
    cotangent,
):
    count_sq = lax.axis_size("sq")
    count_head = lax.axis_size("head")
    sq_index = lax.axis_index("sq")
    head_index = lax.axis_index("head")
    own_rows = layer_in.shape[0]
    length = own_rows * count_head
    key_scale = KD ** (-0.5)
    value_width = w_value.shape[1]
    depth = layer_in.shape[1]
    heads = value_width // VD
    log_rate = log_decay(head_index * heads, heads)
    order = jnp.stack([sq_index ^ mask_of(s, count_sq) for s in range(count_sq)]).astype(jnp.int32)
    start = [lax.rem(head_index - t + count_head, count_head) * own_rows for t in range(count_head)]
    kin_steps = []
    while 2 << len(kin_steps) < count_head:
        kin_steps.append(2 << len(kin_steps))

    key_width = w_key.shape[1]
    pair_width = value_width + key_width

    norm = Small(jnp.stack([norm1_gain, norm1_bias, norm2_gain, norm2_bias]))
    out_shard = w_out.T
    out_half = out_shard.shape[1] // 2
    first = Gather(
        jnp.concatenate(
            [w_value, (w_key.astype(wide) * key_scale).astype(low), out_shard[:, :out_half]], axis=1
        ),
        jnp.concatenate([w_swish, w_query, out_shard[:, out_half:]], axis=1),
    )
    quarter_width = w_gate.shape[1]
    middle = quarter_width // 2
    down_shard = w_down.T
    feed_first = Box(jnp.concatenate([w_gate, down_shard[:, :middle]], axis=1))
    feed_later = Box(jnp.concatenate([w_up, down_shard[:, middle:]], axis=1))
    kin_parts = [
        Box(w_gate),
        Box(w_up),
        Box(down_shard),
    ]
    cot_own = Box(own_order(cotangent))
    x_own = Box(own_order(layer_in))
    slots = [Box(layer_in)]
    settle(slots[0], first, norm)
    for turn in range(1, count_head):
        slots.append(Box(ring_step(slots[-1].value)))
        first.core()
        first.send()
        norm.send()
        settle(slots[-1], first, norm, feed_first, feed_later, cot_own, x_own, *kin_parts)
    norm.rest()
    first.rest()
    first.core()

    def kin(value):
        held = [value]
        for step in kin_steps:
            held += [swap_head(v, step) for v in held]
        return held

    x_own = x_own.value
    packs = [Many(*kin(kin_parts[0].value)[1:])]
    cot_far = Box(swap_head(cot_own.value, 1))
    feeds = [Gather(feed_first.value, feed_later.value)]
    feeds[0].stage()
    feeds[0].send()
    norms = jnp.concatenate([norm.pieces[s] for s in range(count_sq)], axis=1).astype(wide)
    gain_one, shift_one, gain_two, shift_two = norms[0], norms[1], norms[2], norms[3]
    normed, xhat, kv, first_full = norm_project(
        [b.value for b in slots],
        norms,
        first,
        pair_width,
        order,
        jnp.stack(start).astype(jnp.int32),
    )
    passed = Gather(*final_state(kv, log_rate, heads))
    settle(passed, *packs, cot_far, feeds[0], cot_own, *kin_parts[1:])

    passed.send()
    packs.append(Many(*kin(kin_parts[1].value)[1:]))
    settle(passed)
    passed.rest()
    qs, later_full = project_pieces(normed, first, pair_width)
    qs = Box(qs)
    settle(passed, packs[1], cot_far, feeds[0], cot_own, kin_parts[2], qs)
    qs, cot_own = qs.value, cot_own.value
    passed.core()
    packs.append(Many(*kin(kin_parts[2].value)[1:]))
    feeds[0].core()
    feeds[0].send()
    incoming = combine(passed, log_rate, length, False)
    gated_low, grouped, factor, states = retain(kv, qs, incoming, log_rate, heads)

    out_column = pair_width // out_half

    def out_part(turns):
        (parts,) = rows_back(
            [(gated_low, 0), (gated_low, 1)],
            [(first_full, out_column, out_half), (later_full, out_column, out_half)],
            [start[turn % count_head] for turn in turns],
            own_rows,
        )
        return parts

    total = Box(out_part([1]))
    gated = Box(gated_low)
    settle(packs[2], total, feeds[0], gated)
    gated_low = gated.value
    quarters = 1 + len(packs[0].value)
    parts = Box(out_part(range(2, count_head + 1)))
    for turn in range(2, count_head + 1):
        got = ring_step(total.value)
        if turn == 2:
            feeds[0].stage()
            feeds[0].send()
            for gate, up, down in zip(*[p.value for p in packs]):
                feeds.append(
                    Gather(
                        jnp.concatenate([gate, down[:, :middle]], axis=1),
                        jnp.concatenate([up, down[:, middle:]], axis=1),
                    )
                )
                feeds[-1].stage()
        else:
            feeds[0].core()
            if turn == 3:
                feeds[0].stage()
            for thing in feeds[1:]:
                if turn == 3:
                    thing.core()
                thing.send()
        total = Box(add_rows(parts.value, turn - 2, got, low if turn < count_head else wide))
        settle(total, *feeds, parts)
    hidden = x_own.astype(wide) + total.value
    second_own = Box(layer_norm(hidden, gain_two, shift_two).astype(low))

    settle(second_own, *feeds)
    second_own = second_own.value
    second_far = Box(swap_head(second_own, 1))
    for thing in feeds[1:]:
        thing.core()
        thing.rest()
    feeds[0].finish()
    fed = feed_part(second_own, cot_own, feeds[:1], quarter_width, [], wide)
    inner_own, grads_own, fed_sums = [fed[0]], [fed[1]], Many(*fed[2:])
    settle(second_far, *feeds[1:], cot_far, fed_sums)
    second_far, cot_far = second_far.value, cot_far.value
    for thing in feeds[1:]:
        thing.finish()
    fed = feed_part(second_far, cot_far, feeds, quarter_width, [], low)
    inner_far, grads_far = fed[: 2 * quarters : 2], fed[1 : 2 * quarters : 2]
    grad_far, down_far, near = Box(fed[-2]), Box(fed[-1]), Box(second_own)
    settle(grad_far, near, down_far)

    grad_far = Box(swap_head(grad_far.value, 1))
    fed = feed_part(near.value, cot_own, feeds[1:], quarter_width, fed_sums.value, wide)
    inner_own += fed[: 2 * quarters - 2 : 2]
    grads_own += fed[1 : 2 * quarters - 2 : 2]
    second = Many(near.value, second_far)
    cot = Many(cot_own, cot_far)
    inner = Many(beside(inner_own), beside(inner_far))
    grads = [Many(a, b) for a, b in zip(grads_own, grads_far)]
    late_sums = [Scatter(second.value, g.value) for g in grads[1:]]
    down_sum = Scatter(cot.value, inner.value)
    settle(grad_far, *late_sums, down_sum, second, grads[0], down_far)
    second_grad = fed[-2] + grad_far.value.astype(wide)
    _, second_back = jax.vjp(layer_norm, hidden, gain_two, shift_two)
    hidden_part, gain_two_part, shift_two_part = second_back(second_grad)
    grad_hidden = cot_own.astype(wide) + hidden_part

    slots = [Box(grad_hidden.astype(low))]
    settle(slots[0], *late_sums, down_sum, second, grads[0], down_far)
    waits = [*late_sums, down_sum, down_far]
    passing = []
    for turn in range(count_head):
        rows = slots[-1]
        if turn < count_head - 1:
            slots.append(Box(ring_step(rows.value)))
        if turn == 0:
            for thing in [*late_sums, down_sum]:
                thing.core()
                thing.near()
            early_sum = Scatter(second.value, grads[0].value)
            waits.append(early_sum)
        elif turn == 1:
            for thing in late_sums:
                thing.send()
            early_sum.core()
        elif turn == 2:
            send_together(down_sum, late_sums[0])
            for thing in late_sums:
                thing.rest()
            early_sum.near()
            down_far = Box(swap_head(down_far.value, 1))
            waits.append(down_far)
        for done in {0: (), 1: (0,), 2: (1, 2)}.get(turn, (turn,)):
            passing = gate_back(
                slots[done].value,
                first_full,
                later_full,
                out_column,
                grouped,
                factor,
                qs,
                log_rate,
                heads,
                start[done] // own_rows,
                passing,
                done == count_head - 1,
            )
        if turn < count_head - 1:
            passing = Many(*passing)
            settle(slots[-1], *waits, passing)
            passing = passing.value
    swish_grad, retained_grad, *crossed = passing

    def kin_sum(held):
        parts = []
        held = [None] + list(held)
        for step in kin_steps[::-1]:
            size = len(held) // 2
            got = [swap_head(h, step) for h in held[size:]]
            parts.append(got[0])
            held = [None] + [
                (h.astype(wide) + g.astype(wide)).astype(low) for h, g in zip(held[1:size], got[1:])
            ]
        return parts

    branch, gated = Many(*[rows.value for rows in slots]), Box(gated_low)
    places = (jnp.stack(start) // own_rows).astype(jnp.int32)
    cut = 3 * quarter_width // 4
    gates = [thing.rest()[0].astype(low) for thing in late_sums]
    ups = [thing.rest()[1].astype(low) for thing in late_sums]
    early = [Many(*kin_sum([gate[:, :cut] for gate in gates]))]
    kin_next = Many(
        *[beside([gate[:, cut:], up[:, :cut]]) for gate, up in zip(gates, ups)]
    )
    ups = Many(*[up[:, cut:] for up in ups])
    passed = Gather(*crossed)
    swish = Box(swish_grad)
    settle(passed, early_sum, down_sum, ups, kin_next, branch, gated, swish)
    passed.send()
    settle(passed, early[0], down_sum, ups, kin_next, swish, branch, gated)
    early.append(Many(*kin_sum(kin_next.value)))
    passed.rest_grouped()
    down_sum.send(True)
    swish_sum = Scatter([normed], [swish.value])
    out_sum = Scatter(branch.value, [gated.value] * count_head, places)
    settle(passed, early[1], early_sum, down_sum, ups, swish_sum, out_sum)
    passed.core()
    down_parts = jnp.split(jnp.concatenate(down_sum.rest(), axis=1), quarters, axis=1)
    early.append(
        Many(
            *kin_sum(
                [
                    beside([up, part.astype(low)])
                    for up, part in zip(ups.value, down_parts[1:])
                ]
            )
        )
    )
    early_sum.send(True)
    swish_sum.core()
    returned = combine(passed, log_rate, length, True)
    backs = retain_back(kv, qs, retained_grad, states, returned, log_rate, heads)

    def normed_part(turns, backs):
        query = 2 + value_width // key_width - 1
        return rows_back(
            [(backs, 0), (swish_grad, 0), (backs, query)],
            [
                (first_full, 0, pair_width),
                (later_full, 0, value_width),
                (later_full, query - 1, key_width),
            ],
            [start[turn % count_head] for turn in turns],
            own_rows,
            xhat,
        )

    total, norm_sums = normed_part([1], backs)
    total, backs, norm_sums = Box(total), Box(backs), Box(norm_sums)
    settle(total, early_sum, swish_sum, out_sum, backs, norm_sums, early[2])
    parts, more_sums = normed_part([2], backs.value)
    parts = [Box(parts)]
    norm_sums = Many(norm_sums.value, more_sums)
    for turn in range(2, count_head + 1):
        got = ring_step(total.value)
        if turn == 2:
            early_sum.rest()
            out_sum.core()
            swish_sum.near()
            back_sum = Scatter([normed], [backs.value])
            back_sum.core()
            back_sum.near()
            settle(back_sum, parts[0])
            waits = [early_sum, swish_sum, back_sum, out_sum]
        elif turn == 3:
            back_sum.send()
            swish_sum.send(True)
            out_sum.near()
            later_parts, more_sums = normed_part(range(3, count_head + 1), backs.value)
            parts.append(Box(later_parts))
            norm_sums = Many(*norm_sums.value, more_sums)
            waits = [swish_sum, back_sum, out_sum]
        elif turn == 4:
            back_sum.rest()
            out_sum.send(True)
            norm_sums = true_order(
                jnp.concatenate(
                    [sum(norm_sums.value), jnp.stack([gain_two_part, shift_two_part])]
                )
            )
            norm_sums = Many(sum_others(norm_sums, "sq", [1]))
            waits = [back_sum, swish_sum, out_sum]
        part = (parts[0], 0) if turn == 2 else (parts[1], turn - 3)
        total = Box(
            add_rows(part[0].value, part[1], got, low if turn < count_head else wide)
        )
        settle(total, *waits, *parts, norm_sums, backs)
    _, first_back = jax.vjp(lambda v: layer_norm(v, gain_one, shift_one), x_own.astype(wide))
    grad_in = grad_hidden + first_back(total.value)[0]
    norm_sums = sum_others(norm_sums.value[0], "sq", range(2, count_sq, 2))
    norm_sums = sum_others(norm_sums, "head", range(1, count_head))
    first_sum, later_sum = early_sum.rest()
    early = [sum(p.astype(wide) for p in e.value) for e in early]
    early = jnp.concatenate(early, axis=1)
    grad_gate = first_sum + early[:, :quarter_width]
    grad_up = later_sum + early[:, quarter_width : 2 * quarter_width]
    grad_down = (down_parts[0] + early[:, 2 * quarter_width :]).T
    grad_value, grad_key_query = back_sum.rest()
    grad_swish = jnp.concatenate(swish_sum.rest(), axis=1)
    grad_out = jnp.concatenate(out_sum.rest(), axis=1).T
    result = (hidden + fed[-1] + down_far.value.astype(wide)).astype(low)

    piece = depth // (count_sq * count_head)
    first_norm = lax.dynamic_slice_in_dim(
        norm_sums[:2], (head_index * count_sq + sq_index) * piece, piece, 1
    )
    piece = depth // count_sq
    second_norm = lax.dynamic_slice_in_dim(norm_sums[2:], sq_index * piece, piece, 1)
    return (
        true_order(result),
        true_order(grad_in),
        first_norm[0],
        first_norm[1],
        grad_key_query[:, key_width:],
        grad_key_query[:, :key_width] * key_scale,
        grad_value,
        grad_swish,
        grad_out,
        second_norm[0],
        second_norm[1],
        grad_gate,
        grad_up,
        grad_down,
    )


def solution(mesh):
    return jax.shard_map(
        shards,
        mesh=mesh,
        in_specs=(
            P(("sq", "head"), None),
            P("sq"),
            P("sq"),
            P("sq", "head"),
            P("sq", "head"),
            P("sq", "head"),
            P("sq", "head"),
            P("head", "sq"),
            P("sq"),
            P("sq"),
            P("sq", "head"),
            P("sq", "head"),
            P("head", "sq"),
            P(("sq", "head"), None),
        ),
        out_specs=(
            P(("sq", "head"), None),
            P(("sq", "head"), None),
            P(("head", "sq")),
            P(("head", "sq")),
            P("sq", "head"),
            P("sq", "head"),
            P("sq", "head"),
            P("sq", "head"),
            P("head", "sq"),
            P("sq"),
            P("sq"),
            P("sq", "head"),
            P("sq", "head"),
            P("head", "sq"),
        ),
        check_vma=False,
    )
```
